256 devices in a mesh: frame: 64 (over z, x, y_hi), strip: 4 (over y_lo, core).
Axes of the slice: x: 4, y: 4 (y_hi: 2, y_lo: 2; y = y_hi * 2 + y_lo), z: 8, core: 2. Of those that a mesh axis runs over, the one named last changes fastest.
Arguments:
- features: bfloat16 [64, 120, 32, 256], P('frame', None, 'strip'), may hold values from -6 to 6
- w_mutual: bfloat16 [2, 120, 360], replicated, may hold values from -4 to 4
- w_self: bfloat16 [2, 120, 360], replicated, may hold values from -4 to 4
- w_proj: bfloat16 [2, 240, 120], replicated, may hold values from -0.375 to 0.375
- w_gate: bfloat16 [2, 120, 240], replicated, may hold values from -0.5 to 0.5
- w_up: bfloat16 [2, 120, 240], replicated, may hold values from -0.5 to 0.5
- w_down: bfloat16 [2, 240, 120], replicated, may hold values from -0.375 to 0.375
Outputs:
- refined: bfloat16 [64, 120, 32, 256], P('frame', None, 'strip')
The draws below stay inside these ranges and needn't reach their ends.
All inputs are finite; a program needn't handle non-finite values.
Results may differ from the reference program's by a relative error of at most 0.012.
The reference program's roundings to bfloat16 on the way count: a program that leaves them out, or rounds other values in their place, can miss the bound.
Values may be sent and summed in bfloat16 or wider, within the bound.
No kernel may reach another device: no remote copies, remote signals or barrier semaphores. Data moves between devices by JAX's collectives and lax.ppermute only.
A program may use at most 64 MiB of HBM per device.

```python
import jax
import jax.numpy as jnp
from jax import lax

C = 120
HEADS = 6
HEAD = 20
FFN = 240
WIN = 8
LAYERS = 2
COLS = 256
FRAMES = 64
NR = 32


def draw_features(key, part):
    key = jax.random.fold_in(key, 11)
    full_shape = (FRAMES, C, NR, COLS)
    values = jax.random.normal(key, full_shape, jnp.float32)
    return jnp.clip(values, -6.0, 6.0).astype(jnp.bfloat16)


def attention_weights(key, gain_lo, gain_hi):
    base_draw = jnp.clip(jax.random.normal(jax.random.fold_in(key, 1), (LAYERS, C, 3 * C), jnp.float32), -4.0, 4.0) * C ** (-0.5)
    head_gains = jnp.exp(jax.random.uniform(jax.random.fold_in(key, 2), (LAYERS, 1, HEADS), jnp.float32, jnp.log(gain_lo), jnp.log(gain_hi)))
    head_gains = jnp.repeat(head_gains, HEAD, axis=2)
    queries = base_draw[:, :, :C] * head_gains
    keys_part = base_draw[:, :, C:2 * C] * head_gains
    joined = jnp.concatenate([queries, keys_part, base_draw[:, :, 2 * C:]], axis=2)
    return jnp.clip(joined, -4.0, 4.0).astype(jnp.bfloat16)


def draw_w_mutual(key, part):
    key = jax.random.fold_in(key, 21)
    return attention_weights(key, 1.0, 1.0)


def draw_w_self(key, part):
    key = jax.random.fold_in(key, 31)
    return attention_weights(key, 1.0, 1.0)


def bell_draw(own_key, shape, width, most, held_as=jnp.bfloat16):
    values = width * jax.random.normal(own_key, shape, jnp.float32)
    return jnp.clip(values, min=-most, max=most).astype(held_as)


def setup_inputs(seed: int = 0) -> dict:
    splits = jax.random.split(jax.random.key(seed), 8)
    features = draw_features(jax.random.fold_in(splits[7], 71), 0)
    w_mutual = draw_w_mutual(jax.random.fold_in(splits[7], 71), 0)
    w_self = draw_w_self(jax.random.fold_in(splits[7], 71), 0)
    w_proj = bell_draw(splits[3], (LAYERS, 2 * C, C), (2 * C) ** -0.5, 0.375)
    w_gate = bell_draw(splits[4], (LAYERS, C, FFN), C ** -0.5, 0.5)
    w_up = bell_draw(splits[5], (LAYERS, C, FFN), C ** -0.5, 0.5)
    w_down = bell_draw(splits[6], (LAYERS, FFN, C), FFN ** -0.5, 0.375)
    return {"features": features, "w_mutual": w_mutual, "w_self": w_self, "w_proj": w_proj, "w_gate": w_gate, "w_up": w_up, "w_down": w_down}


epsilon = 1e-05
block_cols = 64

def normed(values):
    centre_mean = lax.optimization_barrier(jnp.mean(values, axis=0, keepdims=True))
    centred = values - centre_mean
    spread = lax.optimization_barrier(jnp.mean(centred * centred, axis=0, keepdims=True))
    return (centred * lax.rsqrt(spread + epsilon)).astype(jnp.bfloat16)

def project(weight, values):
    return jnp.einsum('ck,crw->krw', weight.astype(jnp.float32), values.astype(jnp.float32))

def to_windows(strip_data):
    win_count = strip_data.shape[2] // WIN
    shaped = strip_data.reshape(HEADS, HEAD, WIN, win_count, WIN)
    return shaped.transpose(3, 0, 2, 4, 1).reshape(win_count, HEADS, WIN * WIN, HEAD)

def from_windows(mixed_out):
    win_count = mixed_out.shape[0]
    shaped = mixed_out.reshape(win_count, HEADS, WIN, WIN, HEAD)
    return shaped.transpose(1, 4, 2, 0, 3).reshape(HEADS * HEAD, WIN, win_count * WIN)

def window_mix(queries, key_rows, values):
    scores = jnp.einsum('nhqd,nhkd->nhqk', queries.astype(jnp.float32), key_rows.astype(jnp.float32)) * HEAD ** (-0.5)
    row_max = lax.optimization_barrier(jnp.max(scores, axis=-1, keepdims=True))
    weights = jnp.exp(scores - row_max)
    weights = (weights / lax.optimization_barrier(jnp.sum(weights, axis=-1, keepdims=True))).astype(jnp.bfloat16)
    return jnp.einsum('nhqk,nhkd->nhqd', weights.astype(jnp.float32), values.astype(jnp.float32)).astype(jnp.bfloat16)

def attend(own_mut, own_self, other_kv):
    block_count = own_mut.shape[2] // block_cols

    def column_block(position):
        col_start = position * block_cols

        def take_cols(array):
            return lax.dynamic_slice_in_dim(array, col_start, block_cols, 2)
        mutual = window_mix(to_windows(take_cols(own_mut[:C])), to_windows(take_cols(other_kv[:C])), to_windows(take_cols(other_kv[C:2 * C])))
        key_rows = jnp.concatenate([to_windows(take_cols(own_self[C:2 * C])), to_windows(take_cols(other_kv[2 * C:3 * C]))], axis=2)
        value_rows = jnp.concatenate([to_windows(take_cols(own_self[2 * C:])), to_windows(take_cols(other_kv[3 * C:]))], axis=2)
        selfish = window_mix(to_windows(take_cols(own_self[:C])), key_rows, value_rows)
        return jnp.concatenate([from_windows(mutual), from_windows(selfish)], axis=0)
    blocks = lax.map(column_block, jnp.arange(block_count, dtype=jnp.int32))
    return blocks.transpose(1, 2, 0, 3).reshape(2 * C, WIN, block_count * block_cols)

def project_all(current, w_mut, w_slf):
    normal_rows = normed(current.astype(jnp.float32))
    return (normal_rows, project(w_mut, normal_rows).astype(jnp.bfloat16), project(w_slf, normal_rows).astype(jnp.bfloat16))

def finish(current, own_mut, own_self, other_kv, w_prj, w_gte, w_upp, w_dwn):
    joined = attend(own_mut, own_self, other_kv)
    middle = current.astype(jnp.float32) + project(w_prj, joined)
    second_norm = normed(middle)
    hidden = (jax.nn.gelu(project(w_gte, second_norm), approximate=False) * project(w_upp, second_norm)).astype(jnp.bfloat16)
    return (middle + project(w_dwn, hidden)).astype(jnp.bfloat16)

def pair_layer(frames, w_mut, w_slf, w_prj, w_gte, w_upp, w_dwn):
    frame_count, channels, band_rows, columns = frames.shape
    grouped = frames.reshape(frame_count // 2, 2, channels, band_rows // WIN, WIN, columns)
    grouped = grouped.transpose(0, 3, 1, 2, 4, 5).reshape(-1, 2, channels, WIN, columns)

    def pair_block(pair_frames):
        first_norm, first_mut, first_self = project_all(pair_frames[0], w_mut, w_slf)
        second_norm, second_mut, second_self = project_all(pair_frames[1], w_mut, w_slf)
        first_kv = jnp.concatenate([first_mut[C:], first_self[C:]], axis=0)
        second_kv = jnp.concatenate([second_mut[C:], second_self[C:]], axis=0)
        first_out = finish(pair_frames[0], first_mut, first_self, second_kv, w_prj, w_gte, w_upp, w_dwn)
        second_out = finish(pair_frames[1], second_mut, second_self, first_kv, w_prj, w_gte, w_upp, w_dwn)
        return jnp.stack([first_out, second_out])
    results = lax.map(pair_block, grouped)
    results = results.reshape(frame_count // 2, band_rows // WIN, 2, channels, WIN, columns)
    return results.transpose(0, 2, 3, 1, 4, 5).reshape(frame_count, channels, band_rows, columns)

def reference(features, w_mutual, w_self, w_proj, w_gate, w_up, w_down):
    half_win = WIN // 2
    layer_one = pair_layer(features, w_mutual[0], w_self[0], w_proj[0], w_gate[0], w_up[0], w_down[0])
    shifted = jnp.roll(layer_one, (-1, -half_win, -half_win), axis=(0, 2, 3))
    layer_two = pair_layer(shifted, w_mutual[1], w_self[1], w_proj[1], w_gate[1], w_up[1], w_down[1])
    return jnp.roll(layer_two, (1, half_win, half_win), axis=(0, 2, 3))
```

```python
import jax
import jax.numpy as jnp
import numpy as np
from jax import lax
from jax.experimental import pallas as pl
from jax.experimental.pallas import tpu as pltpu
from jax.sharding import PartitionSpec as P

C = 120
HEADS = 6
HEAD = 20
FFN = 240
WIN = 8
LANES = 128
VHEAD = 24
HALF = 16
TOK = WIN * WIN
EPS = 1e-05
EXP2_SCALE = float(np.log2(np.e) * HEAD**-0.5)
VMEM_LIMIT = 56 * 1024 * 1024


def matmul(a, b):
    return lax.dot_general(a, b, (((1,), (0,)), ((), ())), preferred_element_type=jnp.float32)


def matmul_nt(a, b):
    return lax.dot_general(a, b, (((1,), (1,)), ((), ())), preferred_element_type=jnp.float32)


def matmul_tn(a, b):
    return lax.dot_general(a, b, (((0,), (0,)), ((), ())), preferred_element_type=jnp.float32)


def normed(x):
    lane = lax.broadcasted_iota(jnp.int32, x.shape, 1)
    mean = jnp.sum(x, axis=1, keepdims=True) * (1.0 / C)
    centred = jnp.where(lane < C, x - mean, 0.0)
    spread = jnp.sum(centred * centred, axis=1, keepdims=True) * (1.0 / C)
    return (centred * lax.rsqrt(spread + EPS)).astype(jnp.bfloat16)


def head_only(q_t, head):
    low = head * HEAD // 16 * 16
    high = -(-(head * HEAD + HEAD) // 16) * 16
    part = q_t[low:high].astype(jnp.float32)
    row = lax.broadcasted_iota(jnp.int32, part.shape, 0) + low
    keep = (row >= head * HEAD) & (row < head * HEAD + HEAD)
    part = jnp.where(keep, part, 0.0).astype(jnp.bfloat16)
    pieces = [part]
    if low:
        pieces.insert(0, jnp.zeros((low, q_t.shape[1]), jnp.bfloat16))
    if high < LANES:
        pieces.append(jnp.zeros((LANES - high, q_t.shape[1]), jnp.bfloat16))
    return jnp.concatenate(pieces, axis=0)


def softmax_rows(scores):
    top = jnp.max(scores, axis=0, keepdims=True)
    weights = jnp.exp2((scores - top) * EXP2_SCALE)
    total = jnp.sum(weights, axis=0, keepdims=True)
    return weights * (1.0 / total)


def attend(keys, q_t, v_t):
    outs = []
    lane = lax.broadcasted_iota(jnp.int32, (TOK, 2 * LANES), 1)
    of_first = (lane % LANES) < TOK
    for kind in range(2):
        kind_keys = keys[:, kind * LANES : (kind + 1) * LANES]
        kind_q = q_t[kind * LANES : (kind + 1) * LANES]
        for pair in range(HEADS // 2):
            queries = jnp.concatenate(
                [head_only(kind_q, 2 * pair), head_only(kind_q, 2 * pair + 1)], axis=1
            )
            scores = matmul(kind_keys, queries)
            if kind == 0:
                probs = softmax_rows(jnp.where(of_first, scores[TOK:], scores[:TOK]))
                probs = jnp.concatenate(
                    [jnp.where(of_first, 0.0, probs), jnp.where(of_first, probs, 0.0)], axis=0
                )
            else:
                probs = softmax_rows(scores)
            base = kind * HEADS * VHEAD + pair * 2 * VHEAD
            mixed = matmul(v_t[base : base + 2 * VHEAD], probs.astype(jnp.bfloat16))
            outs += [mixed[:VHEAD, :LANES], mixed[VHEAD:, LANES:]]
    return jnp.concatenate(outs, axis=0).astype(jnp.bfloat16)


def layer_tokens(x, w_k, w_qv, w_prj, w_gu, w_dwn):
    count = x.shape[0] // LANES
    normal = normed(x)
    keys = matmul(normal, w_k).astype(jnp.bfloat16)
    qv_t = matmul_nt(w_qv, normal).astype(jnp.bfloat16)
    middles = []
    for i in range(count):
        span = slice(i * LANES, (i + 1) * LANES)
        joined = attend(keys[span], qv_t[: 2 * LANES, span], qv_t[2 * LANES :, span])
        middles.append(x[span] + matmul_tn(joined, w_prj))
    middle = jnp.concatenate(middles, axis=0)
    both = matmul(normed(middle), w_gu)
    gate, up = both[:, : 2 * LANES], both[:, 2 * LANES :]
    gelu = 0.5 * gate * (1.0 + lax.erf(gate * float(np.sqrt(0.5))))
    hidden = (gelu * up).astype(jnp.bfloat16)
    return middle + matmul(hidden, w_dwn)


def to_tokens_kernel(h_ref, x_ref, send_ref, own_ref, wide, tiles):
    h = h_ref[0]
    wide[...] = x_ref[...].astype(jnp.float32)
    pad = jnp.zeros((LANES - C, LANES), jnp.float32)
    for k in range(2):
        half = 1 - h if k == 0 else h
        col = pl.multiple_of(half * LANES, LANES)
        for r in range(WIN):
            block = wide[:, r, pl.ds(col, LANES)]
            block = jnp.concatenate([block, pad], axis=0).T
            tiles[k, :HALF, r] = block.reshape(HALF, WIN, LANES)
    for k, ref in enumerate((send_ref, own_ref)):
        main = tiles[k, :HALF].reshape(HALF * TOK, LANES)
        ref[: HALF * TOK] = main.astype(jnp.bfloat16)
        ref[HALF * TOK :] = tiles[1 - k, 0].reshape(TOK, LANES).astype(jnp.bfloat16)


def layer_one_kernel(own_ref, oth_ref, w_k, w_qv, w_prj, w_gu, w_dwn, *rest):
    outs, (flat, tiles) = rest[:4], rest[4:]
    weights = (w_k, w_qv, w_prj, w_gu, w_dwn)

    def work(first, count):
        parts = []
        for i in range(count):
            start = pl.multiple_of((first + i) * TOK, TOK)
            parts += [own_ref[pl.ds(start, TOK)], oth_ref[pl.ds(start, TOK)]]
        x = jnp.concatenate(parts, axis=0).astype(jnp.float32)
        y = layer_tokens(x, *[w[...] for w in weights])
        y = y.reshape(count, 2, WIN, WIN, LANES)
        for i in range(count):
            col = pl.multiple_of((first + i) * WIN, WIN)
            for f in range(2):
                flat[f, :, pl.ds(col, WIN), :] = y[i, f]

    def body(step, carry):
        work(step * 2, 2)
        return carry

    lax.fori_loop(0, HALF // 2, body, 0)
    work(HALF, 1)
    for f in range(2):
        for r in range(WIN):
            block = flat[f, r, WIN // 2 : WIN // 2 + LANES, :]
            tiles[f, r // 4, :, r % 4] = block.reshape(HALF, WIN, LANES)
        for k in range(2):
            piece = tiles[f, k].reshape(HALF * TOK // 2, LANES)
            outs[2 * f + k][...] = piece.astype(jnp.bfloat16)


def layer_two_kernel(own_lo, own_up, oth_lo, oth_up, w_k, w_qv, w_prj, w_gu, w_dwn, *outs):
    weights = (w_k, w_qv, w_prj, w_gu, w_dwn)
    ins = (own_lo, own_up, oth_lo, oth_up)
    half_tok = TOK // 2

    def body(step, carry):
        parts = []
        starts = []
        for i in range(2):
            start = pl.multiple_of((step * 2 + i) * half_tok, half_tok)
            starts.append(start)
            parts += [ref[pl.ds(start, half_tok)] for ref in ins]
        x = jnp.concatenate(parts, axis=0).astype(jnp.float32)
        y = layer_tokens(x, *[w[...] for w in weights]).astype(jnp.bfloat16)
        for i in range(2):
            for j in range(4):
                low = i * LANES + j * half_tok
                outs[j][pl.ds(starts[i], half_tok)] = y[low : low + half_tok]
        return carry

    lax.fori_loop(0, HALF // 2, body, 0)


def from_tokens_kernel(h_ref, own_lo, own_up, oth_lo, oth_up, out_ref, tiles, wide):
    h = h_ref[0]
    for j, ref in enumerate((own_lo, own_up, oth_lo, oth_up)):
        half = h if j < 2 else 1 - h
        tiles[half, j % 2] = ref[...].astype(jnp.float32).reshape(HALF, 4, WIN, LANES)
    for r in range(WIN):
        lo = 0 if r >= 4 else 1
        row = [tiles[half, lo, :, r % 4].reshape(LANES, LANES).T for half in range(2)]
        row = pltpu.roll(jnp.concatenate(row, axis=1), WIN // 2, 1)
        wide[:, r, :] = row[:C]
    out_ref[...] = wide[...].astype(jnp.bfloat16)


VMEM = pl.BlockSpec(memory_space=pltpu.VMEM)
SMEM = pl.BlockSpec(memory_space=pltpu.SMEM)
PARAMS = pltpu.CompilerParams(vmem_limit_bytes=VMEM_LIMIT)


def tokens_shape(rows):
    return jax.ShapeDtypeStruct((rows, LANES), jnp.bfloat16)


def to_tokens(h, x):
    rows = (HALF + 1) * TOK
    return pl.pallas_call(
        to_tokens_kernel,
        out_shape=[tokens_shape(rows)] * 2,
        in_specs=[SMEM, VMEM],
        out_specs=[VMEM] * 2,
        scratch_shapes=[
            pltpu.VMEM((C, WIN, 2 * LANES), jnp.float32),
            pltpu.VMEM((2, HALF, WIN, WIN, LANES), jnp.float32),
        ],
        compiler_params=PARAMS,
        name="to_tokens",
    )(h, x)


def layer_one(own, oth, weights):
    return pl.pallas_call(
        layer_one_kernel,
        out_shape=[tokens_shape(HALF * TOK // 2)] * 4,
        in_specs=[VMEM] * 7,
        out_specs=[VMEM] * 4,
        scratch_shapes=[
            pltpu.VMEM((2, WIN, (HALF + 1) * WIN, LANES), jnp.float32),
            pltpu.VMEM((2, 2, HALF, 4, WIN, LANES), jnp.float32),
        ],
        compiler_params=PARAMS,
        name="layer_one",
    )(own, oth, *weights)


def layer_two(pieces, weights):
    return pl.pallas_call(
        layer_two_kernel,
        out_shape=[tokens_shape(HALF * TOK // 2)] * 4,
        in_specs=[VMEM] * 9,
        out_specs=[VMEM] * 4,
        compiler_params=PARAMS,
        name="layer_two",
    )(*pieces, *weights)


def from_tokens(h, pieces):
    return pl.pallas_call(
        from_tokens_kernel,
        out_shape=jax.ShapeDtypeStruct((C, WIN, 2 * LANES), jnp.bfloat16),
        in_specs=[SMEM] + [VMEM] * 4,
        out_specs=VMEM,
        scratch_shapes=[
            pltpu.VMEM((2, 2, HALF, 4, WIN, LANES), jnp.float32),
            pltpu.VMEM((C, WIN, 2 * LANES), jnp.float32),
        ],
        compiler_params=PARAMS,
        name="from_tokens",
    )(h, *pieces)


def pad_to(array, rows, cols):
    return jnp.pad(array, ((0, rows - array.shape[0]), (0, cols - array.shape[1])))


def by_head(array):
    spread = array.reshape(HEADS, HEAD, array.shape[1])
    spread = jnp.pad(spread, ((0, 0), (0, VHEAD - HEAD), (0, 0)))
    return spread.reshape(HEADS * VHEAD, array.shape[1])


def prepared(w_mut, w_slf, w_prj, w_gte, w_upp, w_dwn):
    w_k = [pad_to(w[:, C : 2 * C], LANES, LANES) for w in (w_mut, w_slf)]
    w_q = [pad_to(w[:, :C].T, LANES, LANES) for w in (w_mut, w_slf)]
    w_v = [pad_to(by_head(w[:, 2 * C :].T), HEADS * VHEAD, LANES) for w in (w_mut, w_slf)]
    w_p = [pad_to(by_head(w), HEADS * VHEAD, LANES) for w in (w_prj[:C], w_prj[C:])]
    return (
        jnp.concatenate(w_k, axis=1),
        jnp.concatenate(w_q + w_v, axis=0),
        jnp.concatenate(w_p, axis=0),
        jnp.concatenate([pad_to(w, LANES, 2 * LANES) for w in (w_gte, w_upp)], axis=1),
        pad_to(w_dwn, 2 * LANES, LANES),
    )


def on_device(features, *weights):
    frames, strips = lax.axis_size("frame"), lax.axis_size("strip")

    def route(frame_step, strip_step):
        pairs = []
        for f in range(frames):
            for s in range(strips):
                to = (f + frame_step * (1 - 2 * (f % 2))) % frames
                pairs.append((f * strips + s, to * strips + (s + strip_step) % strips))
        return pairs

    def send(value, frame_step, strip_step):
        return lax.ppermute(value, ("frame", "strip"), route(frame_step, strip_step))

    h = (lax.axis_index("frame") % 2).astype(jnp.int32).reshape(1)
    w_one = prepared(*[w[0] for w in weights])
    w_two = prepared(*[w[1] for w in weights])
    to_send, own = to_tokens(h, features[0])
    oth = send(to_send, 1, 0)
    own_up, own_lo, oth_up, oth_lo = layer_one(own, oth, w_one)
    oth_lo = send(oth_lo, 2, 0)
    oth_up = send(oth_up, 2, -1)
    own_up = send(own_up, 0, -1)
    own_lo, own_up, oth_lo, oth_up = layer_two((own_lo, own_up, oth_lo, oth_up), w_two)
    oth_lo = send(oth_lo, -1, 0)
    oth_up = send(oth_up, -1, 1)
    own_up = send(own_up, 0, 1)
    return from_tokens(h, (own_lo, own_up, oth_lo, oth_up))[None]


def solution(mesh):
    in_specs = (P("frame", None, "strip", None), P(), P(), P(), P(), P(), P())
    out_specs = P("frame", None, "strip", None)
    return jax.shard_map(
        on_device, mesh=mesh, in_specs=in_specs, out_specs=out_specs, check_vma=False
    )
```

```python
import jax
import jax.numpy as jnp
import numpy as np
from jax import lax
from jax.experimental import pallas as pl
from jax.experimental.pallas import tpu as pltpu
from jax.sharding import PartitionSpec as P

C = 120
HEADS = 6
HEAD = 20
FFN = 240
WIN = 8
LANES = 128
VHEAD = 24
GROUP = 8
HALF = 16
TOK = WIN * WIN
EPS = 1e-05
EXP2_SCALE = float(np.log2(np.e) * HEAD**-0.5)
VMEM_LIMIT = 56 * 1024 * 1024


def matmul(a, b):
    return lax.dot_general(a, b, (((1,), (0,)), ((), ())), preferred_element_type=jnp.float32)


def matmul_nt(a, b):
    return lax.dot_general(a, b, (((1,), (1,)), ((), ())), preferred_element_type=jnp.float32)


def matmul_tn(a, b):
    return lax.dot_general(a, b, (((0,), (0,)), ((), ())), preferred_element_type=jnp.float32)


def normed(x):
    lane = lax.broadcasted_iota(jnp.int32, x.shape, 1)
    mean = jnp.sum(x, axis=1, keepdims=True) * (1.0 / C)
    centred = jnp.where(lane < C, x - mean, 0.0)
    spread = jnp.sum(centred * centred, axis=1, keepdims=True) * (1.0 / C)
    return (centred * lax.rsqrt(spread + EPS)).astype(jnp.bfloat16)


def head_only(q_t, head):
    low = head * HEAD // 16 * 16
    high = -(-(head * HEAD + HEAD) // 16) * 16
    part = q_t[low:high].astype(jnp.float32)
    row = lax.broadcasted_iota(jnp.int32, part.shape, 0) + low
    keep = (row >= head * HEAD) & (row < head * HEAD + HEAD)
    part = jnp.where(keep, part, 0.0).astype(jnp.bfloat16)
    pieces = [part]
    if low:
        pieces.insert(0, jnp.zeros((low, q_t.shape[1]), jnp.bfloat16))
    if high < LANES:
        pieces.append(jnp.zeros((LANES - high, q_t.shape[1]), jnp.bfloat16))
    return jnp.concatenate(pieces, axis=0)


def softmax_rows(scores):
    top = jnp.max(scores, axis=0, keepdims=True)
    weights = jnp.exp2((scores - top) * EXP2_SCALE)
    total = jnp.sum(weights, axis=0, keepdims=True)
    return weights * (1.0 / total)


def project_windows(x, w_k, w_qv, keys, qv_t, first):
    normal = normed(x)
    new_keys = matmul(normal, w_k[...]).astype(jnp.bfloat16)
    new_qv = matmul_nt(w_qv[...], normal).astype(jnp.bfloat16)
    for i in range(x.shape[0] // LANES):
        span = slice(i * LANES, (i + 1) * LANES)
        keys[first + i] = new_keys[span]
        qv_t[first + i] = new_qv[:, span]


def score_block(kind, pair, keys, qv_t, window, of_first):
    kind_q = qv_t[window, kind * LANES : (kind + 1) * LANES]
    queries = jnp.concatenate(
        [head_only(kind_q, 2 * pair), head_only(kind_q, 2 * pair + 1)], axis=1
    )
    scores = matmul(keys[window, :, kind * LANES : (kind + 1) * LANES], queries)
    if kind == 0:
        scores = jnp.where(of_first, scores[TOK:], scores[:TOK])
    return scores


def mix_block(kind, pair, scores, qv_t, window, of_first):
    probs = [softmax_rows(scores[:, i * LANES : (i + 1) * LANES]) for i in range(2)]
    probs = jnp.concatenate(probs, axis=1)
    if kind == 0:
        probs = jnp.concatenate(
            [jnp.where(of_first, 0.0, probs), jnp.where(of_first, probs, 0.0)], axis=0
        )
    base = 2 * LANES + (kind * HEADS + 2 * pair) * VHEAD
    mixed = matmul(qv_t[window, base : base + 2 * VHEAD], probs.astype(jnp.bfloat16))
    return [mixed[:VHEAD, :LANES], mixed[VHEAD:, LANES:]]


def attend(count, keys, qv_t, mutual_scores, self_scores, joined):
    scores = (mutual_scores, self_scores)

    def body(step, carry):
        lane = lax.broadcasted_iota(jnp.int32, (TOK, 2 * LANES), 1)
        of_first = (lane % LANES) < TOK
        now = jnp.minimum(step, count - 1)
        old = jnp.maximum(step - 1, 0)
        outs = []
        for kind in range(2):
            for pair in range(HEADS // 2):
                ref = scores[kind]
                outs += mix_block(kind, pair, ref[pair], qv_t, old, of_first)
                ref[pair] = score_block(kind, pair, keys, qv_t, now, of_first)
        joined[old] = jnp.concatenate(outs, axis=0).astype(jnp.bfloat16)
        return carry

    lax.fori_loop(0, count + 1, body, 0)


def finished(x, joined, w_prj, w_gu, w_dwn):
    mixed = [matmul_tn(block, w_prj[...]) for block in joined]
    middle = x + jnp.concatenate(mixed, axis=0)
    both = matmul(normed(middle), w_gu[...])
    gate, up = both[:, : 2 * LANES], both[:, 2 * LANES :]
    gelu = 0.5 * gate * (1.0 + lax.erf(gate * float(np.sqrt(0.5))))
    hidden = (gelu * up).astype(jnp.bfloat16)
    return middle + matmul(hidden, w_dwn[...])


def to_tokens_kernel(h_ref, x_ref, send_ref, own_ref, wide, tiles):
    h = h_ref[0]
    wide[...] = x_ref[...].astype(jnp.float32)
    pad = jnp.zeros((LANES - C, LANES), jnp.float32)
    for k in range(2):
        half = 1 - h if k == 0 else h
        col = pl.multiple_of(half * LANES, LANES)
        for r in range(WIN):
            block = wide[:, r, pl.ds(col, LANES)]
            block = jnp.concatenate([block, pad], axis=0).T
            tiles[k, :HALF, r] = block.reshape(HALF, WIN, LANES)
    for k, ref in enumerate((send_ref, own_ref)):
        main = tiles[k, :HALF].reshape(HALF * TOK, LANES)
        ref[: HALF * TOK] = main.astype(jnp.bfloat16)
        ref[HALF * TOK :] = tiles[1 - k, 0].reshape(TOK, LANES).astype(jnp.bfloat16)


def layer_one_kernel(own_ref, oth_ref, w_k, w_qv, w_prj, w_gu, w_dwn, *rest):
    outs, (flat, tiles), scratch = rest[:4], rest[4:6], rest[6:]
    keys, qv_t, joined = scratch[0], scratch[1], scratch[-1]

    def tokens(first, count):
        parts = []
        for i in range(count):
            start = pl.multiple_of((first + i) * TOK, TOK)
            parts += [own_ref[pl.ds(start, TOK)], oth_ref[pl.ds(start, TOK)]]
        return jnp.concatenate(parts, axis=0).astype(jnp.float32)

    def front(first, count):
        project_windows(tokens(first, count), w_k, w_qv, keys, qv_t, first)

    def back(first, count):
        blocks = [joined[first + i] for i in range(count)]
        y = finished(tokens(first, count), blocks, w_prj, w_gu, w_dwn)
        y = y.reshape(count, 2, WIN, WIN, LANES)
        for i in range(count):
            col = pl.multiple_of((first + i) * WIN, WIN)
            for f in range(2):
                flat[f, :, pl.ds(col, WIN), :] = y[i, f]

    def pairs(work):
        def body(step, carry):
            work(step * GROUP, GROUP)
            return carry

        lax.fori_loop(0, HALF // GROUP, body, 0)
        work(HALF, 1)

    pairs(front)
    attend(HALF + 1, *scratch)
    pairs(back)
    for f in range(2):
        for r in range(WIN):
            block = flat[f, r, WIN // 2 : WIN // 2 + LANES, :]
            tiles[f, r // 4, :, r % 4] = block.reshape(HALF, WIN, LANES)
        for k in range(2):
            piece = tiles[f, k].reshape(HALF * TOK // 2, LANES)
            outs[2 * f + k][...] = piece.astype(jnp.bfloat16)


def layer_two_kernel(own_lo, own_up, oth_lo, oth_up, w_k, w_qv, w_prj, w_gu, w_dwn, *rest):
    outs, scratch = rest[:4], rest[4:]
    keys, qv_t, joined = scratch[0], scratch[1], scratch[-1]
    ins = (own_lo, own_up, oth_lo, oth_up)
    half_tok = TOK // 2

    def starts(step):
        return [pl.multiple_of((step * GROUP + i) * half_tok, half_tok) for i in range(GROUP)]

    def tokens(step):
        parts = [ref[pl.ds(start, half_tok)] for start in starts(step) for ref in ins]
        return jnp.concatenate(parts, axis=0).astype(jnp.float32)

    def front(step, carry):
        project_windows(tokens(step), w_k, w_qv, keys, qv_t, step * GROUP)
        return carry

    def back(step, carry):
        blocks = [joined[step * GROUP + i] for i in range(GROUP)]
        y = finished(tokens(step), blocks, w_prj, w_gu, w_dwn).astype(jnp.bfloat16)
        for i, start in enumerate(starts(step)):
            for j in range(4):
                low = i * LANES + j * half_tok
                outs[j][pl.ds(start, half_tok)] = y[low : low + half_tok]
        return carry

    lax.fori_loop(0, HALF // GROUP, front, 0)
    attend(HALF, *scratch)
    lax.fori_loop(0, HALF // GROUP, back, 0)


def from_tokens_kernel(h_ref, own_lo, own_up, oth_lo, oth_up, out_ref, tiles, wide):
    h = h_ref[0]
    for j, ref in enumerate((own_lo, own_up, oth_lo, oth_up)):
        half = h if j < 2 else 1 - h
        tiles[half, j % 2] = ref[...].astype(jnp.float32).reshape(HALF, 4, WIN, LANES)
    for r in range(WIN):
        lo = 0 if r >= 4 else 1
        row = [tiles[half, lo, :, r % 4].reshape(LANES, LANES).T for half in range(2)]
        row = pltpu.roll(jnp.concatenate(row, axis=1), WIN // 2, 1)
        wide[:, r, :] = row[:C]
    out_ref[...] = wide[...].astype(jnp.bfloat16)


VMEM = pl.BlockSpec(memory_space=pltpu.VMEM)
SMEM = pl.BlockSpec(memory_space=pltpu.SMEM)
PARAMS = pltpu.CompilerParams(vmem_limit_bytes=VMEM_LIMIT)


def attention_scratch(count):
    return [
        pltpu.VMEM((count, LANES, 2 * LANES), jnp.bfloat16),
        pltpu.VMEM((count, 2 * LANES + 2 * HEADS * VHEAD, LANES), jnp.bfloat16),
        pltpu.VMEM((HEADS // 2, TOK, 2 * LANES), jnp.float32),
        pltpu.VMEM((HEADS // 2, 2 * TOK, 2 * LANES), jnp.float32),
        pltpu.VMEM((count, 2 * HEADS * VHEAD, LANES), jnp.bfloat16),
    ]


def tokens_shape(rows):
    return jax.ShapeDtypeStruct((rows, LANES), jnp.bfloat16)


def to_tokens(h, x):
    rows = (HALF + 1) * TOK
    return pl.pallas_call(
        to_tokens_kernel,
        out_shape=[tokens_shape(rows)] * 2,
        in_specs=[SMEM, VMEM],
        out_specs=[VMEM] * 2,
        scratch_shapes=[
            pltpu.VMEM((C, WIN, 2 * LANES), jnp.float32),
            pltpu.VMEM((2, HALF, WIN, WIN, LANES), jnp.float32),
        ],
        compiler_params=PARAMS,
        name="to_tokens",
    )(h, x)


def layer_one(own, oth, weights):
    return pl.pallas_call(
        layer_one_kernel,
        out_shape=[tokens_shape(HALF * TOK // 2)] * 4,
        in_specs=[VMEM] * 7,
        out_specs=[VMEM] * 4,
        scratch_shapes=[
            pltpu.VMEM((2, WIN, (HALF + 1) * WIN, LANES), jnp.float32),
            pltpu.VMEM((2, 2, HALF, 4, WIN, LANES), jnp.float32),
            *attention_scratch(HALF + 1),
        ],
        compiler_params=PARAMS,
        name="layer_one",
    )(own, oth, *weights)


def layer_two(pieces, weights):
    return pl.pallas_call(
        layer_two_kernel,
        out_shape=[tokens_shape(HALF * TOK // 2)] * 4,
        in_specs=[VMEM] * 9,
        out_specs=[VMEM] * 4,
        scratch_shapes=attention_scratch(HALF),
        compiler_params=PARAMS,
        name="layer_two",
    )(*pieces, *weights)


def from_tokens(h, pieces):
    return pl.pallas_call(
        from_tokens_kernel,
        out_shape=jax.ShapeDtypeStruct((C, WIN, 2 * LANES), jnp.bfloat16),
        in_specs=[SMEM] + [VMEM] * 4,
        out_specs=VMEM,
        scratch_shapes=[
            pltpu.VMEM((2, 2, HALF, 4, WIN, LANES), jnp.float32),
            pltpu.VMEM((C, WIN, 2 * LANES), jnp.float32),
        ],
        compiler_params=PARAMS,
        name="from_tokens",
    )(h, *pieces)


def pad_to(array, rows, cols):
    return jnp.pad(array, ((0, rows - array.shape[0]), (0, cols - array.shape[1])))


def by_head(array):
    spread = array.reshape(HEADS, HEAD, array.shape[1])
    spread = jnp.pad(spread, ((0, 0), (0, VHEAD - HEAD), (0, 0)))
    return spread.reshape(HEADS * VHEAD, array.shape[1])


def prepared(w_mut, w_slf, w_prj, w_gte, w_upp, w_dwn):
    w_k = [pad_to(w[:, C : 2 * C], LANES, LANES) for w in (w_mut, w_slf)]
    w_q = [pad_to(w[:, :C].T, LANES, LANES) for w in (w_mut, w_slf)]
    w_v = [pad_to(by_head(w[:, 2 * C :].T), HEADS * VHEAD, LANES) for w in (w_mut, w_slf)]
    w_p = [pad_to(by_head(w), HEADS * VHEAD, LANES) for w in (w_prj[:C], w_prj[C:])]
    return (
        jnp.concatenate(w_k, axis=1),
        jnp.concatenate(w_q + w_v, axis=0),
        jnp.concatenate(w_p, axis=0),
        jnp.concatenate([pad_to(w, LANES, 2 * LANES) for w in (w_gte, w_upp)], axis=1),
        pad_to(w_dwn, 2 * LANES, LANES),
    )


def on_device(features, *weights):
    frames, strips = lax.axis_size("frame"), lax.axis_size("strip")

    def route(frame_step, strip_step):
        pairs = []
        for f in range(frames):
            for s in range(strips):
                to = (f + frame_step * (1 - 2 * (f % 2))) % frames
                pairs.append((f * strips + s, to * strips + (s + strip_step) % strips))
        return pairs

    def send(value, frame_step, strip_step):
        return lax.ppermute(value, ("frame", "strip"), route(frame_step, strip_step))

    h = (lax.axis_index("frame") % 2).astype(jnp.int32).reshape(1)
    w_one = prepared(*[w[0] for w in weights])
    w_two = prepared(*[w[1] for w in weights])
    to_send, own = to_tokens(h, features[0])
    oth = send(to_send, 1, 0)
    own_up, own_lo, oth_up, oth_lo = layer_one(own, oth, w_one)
    oth_lo = send(oth_lo, 2, 0)
    oth_up = send(oth_up, 2, -1)
    own_up = send(own_up, 0, -1)
    own_lo, own_up, oth_lo, oth_up = layer_two((own_lo, own_up, oth_lo, oth_up), w_two)
    oth_lo = send(oth_lo, -1, 0)
    oth_up = send(oth_up, -1, 1)
    own_up = send(own_up, 0, 1)
    return from_tokens(h, (own_lo, own_up, oth_lo, oth_up))[None]


def solution(mesh):
    in_specs = (P("frame", None, "strip", None), P(), P(), P(), P(), P(), P())
    out_specs = P("frame", None, "strip", None)
    return jax.shard_map(
        on_device, mesh=mesh, in_specs=in_specs, out_specs=out_specs, check_vma=False
    )
```

```python
import functools

import jax
import jax.numpy as jnp
import numpy as np
from jax import lax
from jax.experimental import pallas as pl
from jax.experimental.pallas import tpu as pltpu
from jax.sharding import PartitionSpec as P

C = 120
HEADS = 6
HEAD = 20
FFN = 240
WIN = 8
LANES = 128
VHEAD = 24
HALF = 16
TOK = WIN * WIN
EPS = 1e-05
SHIFTED = ((0, 8), (8, 16))
WINDOWS = ((0, 9), (9, 17))
EXP2_SCALE = float(np.log2(np.e) * HEAD**-0.5)
VMEM_LIMIT = 56 * 1024 * 1024


def matmul(a, b):
    return lax.dot_general(a, b, (((1,), (0,)), ((), ())), preferred_element_type=jnp.float32)


def matmul_nt(a, b):
    return lax.dot_general(a, b, (((1,), (1,)), ((), ())), preferred_element_type=jnp.float32)


def matmul_tn(a, b):
    return lax.dot_general(a, b, (((0,), (0,)), ((), ())), preferred_element_type=jnp.float32)


def normed(x):
    lane = lax.broadcasted_iota(jnp.int32, x.shape, 1)
    mean = jnp.sum(x, axis=1, keepdims=True) * (1.0 / C)
    centred = jnp.where(lane < C, x - mean, 0.0)
    spread = jnp.sum(centred * centred, axis=1, keepdims=True) * (1.0 / C)
    return (centred * lax.rsqrt(spread + EPS)).astype(jnp.bfloat16)


def head_only(q_t, head):
    low = head * HEAD // 16 * 16
    high = -(-(head * HEAD + HEAD) // 16) * 16
    part = q_t[low:high].astype(jnp.float32)
    row = lax.broadcasted_iota(jnp.int32, part.shape, 0) + low
    keep = (row >= head * HEAD) & (row < head * HEAD + HEAD)
    part = jnp.where(keep, part, 0.0).astype(jnp.bfloat16)
    pieces = [part]
    if low:
        pieces.insert(0, jnp.zeros((low, q_t.shape[1]), jnp.bfloat16))
    if high < LANES:
        pieces.append(jnp.zeros((LANES - high, q_t.shape[1]), jnp.bfloat16))
    return jnp.concatenate(pieces, axis=0)


def softmax_rows(scores):
    top = jnp.max(scores, axis=0, keepdims=True)
    weights = jnp.exp2((scores - top) * EXP2_SCALE)
    total = jnp.sum(weights, axis=0, keepdims=True)
    return weights * (1.0 / total)


def project_windows(x, w_k, w_qv, keys, qv_t, first):
    normal = normed(x)
    new_keys = matmul(normal, w_k[...]).astype(jnp.bfloat16)
    new_qv = matmul_nt(w_qv[...], normal).astype(jnp.bfloat16)
    for i in range(x.shape[0] // LANES):
        span = slice(i * LANES, (i + 1) * LANES)
        keys[first + i] = new_keys[span]
        qv_t[first + i] = new_qv[:, span]


def score_block(kind, pair, keys, qv_t, window, of_first):
    kind_q = qv_t[window, kind * LANES : (kind + 1) * LANES]
    queries = jnp.concatenate(
        [head_only(kind_q, 2 * pair), head_only(kind_q, 2 * pair + 1)], axis=1
    )
    scores = matmul(keys[window, :, kind * LANES : (kind + 1) * LANES], queries)
    if kind == 0:
        scores = jnp.where(of_first, scores[TOK:], scores[:TOK])
    return scores


def mix_block(kind, pair, scores, qv_t, window, of_first):
    probs = [softmax_rows(scores[:, i * LANES : (i + 1) * LANES]) for i in range(2)]
    probs = jnp.concatenate(probs, axis=1)
    if kind == 0:
        probs = jnp.concatenate(
            [jnp.where(of_first, 0.0, probs), jnp.where(of_first, probs, 0.0)], axis=0
        )
    base = 2 * LANES + (kind * HEADS + 2 * pair) * VHEAD
    mixed = matmul(qv_t[window, base : base + 2 * VHEAD], probs.astype(jnp.bfloat16))
    return [mixed[:VHEAD, :LANES], mixed[VHEAD:, LANES:]]


def attend(count, keys, qv_t, mutual_scores, self_scores, joined):
    scores = (mutual_scores, self_scores)

    def body(step, carry):
        lane = lax.broadcasted_iota(jnp.int32, (TOK, 2 * LANES), 1)
        of_first = (lane % LANES) < TOK
        now = jnp.minimum(step, count - 1)
        old = jnp.maximum(step - 1, 0)
        outs = []
        for kind in range(2):
            for pair in range(HEADS // 2):
                ref = scores[kind]
                outs += mix_block(kind, pair, ref[pair], qv_t, old, of_first)
                ref[pair] = score_block(kind, pair, keys, qv_t, now, of_first)
        joined[old] = jnp.concatenate(outs, axis=0).astype(jnp.bfloat16)
        return carry

    lax.fori_loop(0, count + 1, body, 0)


def finished(x, joined, w_prj, w_gu, w_dwn):
    mixed = [matmul_tn(block, w_prj[...]) for block in joined]
    middle = x + jnp.concatenate(mixed, axis=0)
    both = matmul(normed(middle), w_gu[...])
    gate, up = both[:, : 2 * LANES], both[:, 2 * LANES :]
    gelu = 0.5 * gate * (1.0 + lax.erf(gate * float(np.sqrt(0.5))))
    hidden = (gelu * up).astype(jnp.bfloat16)
    return middle + matmul(hidden, w_dwn[...])


def to_tokens_kernel(h_ref, x_ref, *rest):
    outs, (wide, tiles) = rest[:-2], rest[-2:]
    h = h_ref[0]
    for half in range(2):
        part = x_ref[:, :, half * LANES : (half + 1) * LANES].astype(jnp.float32)
        wide[half] = part.reshape(C * WIN, LANES)
    pad = jnp.zeros((LANES - C, LANES), jnp.float32)
    for k in range(2):
        half = 1 - h if k == 0 else h
        for r in range(WIN):
            block = wide.at[half][pl.ds(r, C, stride=WIN), :]
            block = jnp.concatenate([block, pad], axis=0).T
            tiles[k, :HALF, r] = block.reshape(HALF, WIN, LANES)
    for k in range(2):
        tiles[k, HALF] = tiles[1 - k, 0]
    for k in range(2):
        for j, (low, high) in enumerate(WINDOWS):
            part = tiles[k, low:high].reshape((high - low) * TOK, LANES)
            outs[k * len(WINDOWS) + j][...] = part.astype(jnp.bfloat16)


def layer_one_kernel(count, first, last, own_ref, oth_ref, *rest):
    if not first:
        before, rest = rest[0], rest[1:]
    w_k, w_qv, w_prj, w_gu, w_dwn = rest[:5]
    outs, rest = rest[5:9], rest[9:]
    if not last:
        after, rest = rest[0], rest[1:]
    flat, tiles, *scratch = rest
    keys, qv_t, joined = scratch[0], scratch[1], scratch[-1]
    shift = 0 if first else WIN

    def tokens():
        parts = []
        for i in range(count):
            span = slice(i * TOK, (i + 1) * TOK)
            parts += [own_ref[span], oth_ref[span]]
        return jnp.concatenate(parts, axis=0).astype(jnp.float32)

    project_windows(tokens(), w_k, w_qv, keys, qv_t, 0)
    attend(count, *scratch)
    y = finished(tokens(), [joined[i] for i in range(count)], w_prj, w_gu, w_dwn)
    y = y.reshape(count, 2, WIN, WIN, LANES)
    if not first:
        flat[:, :, :WIN, :] = before[...]
    for i in range(count):
        for f in range(2):
            flat[f, :, shift + i * WIN : shift + (i + 1) * WIN, :] = y[i, f]
    width = shift + (count - 1) * WIN
    if not last:
        after[...] = flat[:, :, width : width + WIN, :]
    for f in range(2):
        for r in range(WIN):
            block = flat[f, r, WIN // 2 : WIN // 2 + width, :]
            tiles[f, r // 4, :, r % 4] = block.reshape(width // WIN, WIN, LANES)
        for k in range(2):
            piece = tiles[f, k].reshape(width * 4, LANES)
            outs[2 * f + k][...] = piece.astype(jnp.bfloat16)


def layer_two_kernel(count, *rest):
    ins, rest = rest[:4], rest[4:]
    w_k, w_qv, w_prj, w_gu, w_dwn = rest[:5]
    outs, scratch = rest[5:9], rest[9:]
    keys, qv_t, joined = scratch[0], scratch[1], scratch[-1]
    half_tok = TOK // 2
    spans = [slice(i * half_tok, (i + 1) * half_tok) for i in range(count)]

    def tokens():
        return jnp.concatenate([ref[s] for s in spans for ref in ins], axis=0).astype(jnp.float32)

    project_windows(tokens(), w_k, w_qv, keys, qv_t, 0)
    attend(count, *scratch)
    y = finished(tokens(), [joined[i] for i in range(count)], w_prj, w_gu, w_dwn)
    y = y.astype(jnp.bfloat16)
    for i in range(count):
        for j in range(4):
            low = i * LANES + j * half_tok
            outs[j][spans[i]] = y[low : low + half_tok]


def from_tokens_kernel(h_ref, *rest):
    ins, (out_ref, tiles, wide) = rest[:-3], rest[-3:]
    h = h_ref[0]
    for k, (low, high) in enumerate(SHIFTED):
        for j in range(4):
            half = h if j < 2 else 1 - h
            part = ins[4 * k + j][...].astype(jnp.float32)
            tiles[half, j % 2, low:high] = part.reshape(high - low, 4, WIN, LANES)
    for r in range(WIN):
        lo = 0 if r >= 4 else 1
        row = [tiles[half, lo, :, r % 4].reshape(LANES, LANES).T for half in range(2)]
        row = pltpu.roll(jnp.concatenate(row, axis=1), WIN // 2, 1)
        for half in range(2):
            part = row[:C, half * LANES : (half + 1) * LANES]
            wide.at[half][pl.ds(r, C, stride=WIN), :] = part
    for half in range(2):
        part = wide[half].reshape(C, WIN, LANES).astype(jnp.bfloat16)
        out_ref[:, :, half * LANES : (half + 1) * LANES] = part


VMEM = pl.BlockSpec(memory_space=pltpu.VMEM)
SMEM = pl.BlockSpec(memory_space=pltpu.SMEM)
PARAMS = pltpu.CompilerParams(vmem_limit_bytes=VMEM_LIMIT)


def attention_scratch(count):
    return [
        pltpu.VMEM((count, LANES, 2 * LANES), jnp.bfloat16),
        pltpu.VMEM((count, 2 * LANES + 2 * HEADS * VHEAD, LANES), jnp.bfloat16),
        pltpu.VMEM((HEADS // 2, TOK, 2 * LANES), jnp.float32),
        pltpu.VMEM((HEADS // 2, 2 * TOK, 2 * LANES), jnp.float32),
        pltpu.VMEM((count, 2 * HEADS * VHEAD, LANES), jnp.bfloat16),
    ]


def tokens_shape(rows):
    return jax.ShapeDtypeStruct((rows, LANES), jnp.bfloat16)


def to_tokens(h, x):
    shapes = [tokens_shape((high - low) * TOK) for low, high in WINDOWS]
    return pl.pallas_call(
        to_tokens_kernel,
        out_shape=shapes * 2,
        in_specs=[SMEM, VMEM],
        out_specs=[VMEM] * (2 * len(shapes)),
        scratch_shapes=[
            pltpu.VMEM((2, C * WIN, LANES), jnp.float32),
            pltpu.VMEM((2, HALF + 1, WIN, WIN, LANES), jnp.float32),
        ],
        compiler_params=PARAMS,
        name="to_tokens",
    )(h, x)


def layer_one(chunk, own, oth, before, weights):
    first, last = chunk == 0, chunk == len(WINDOWS) - 1
    count = WINDOWS[chunk][1] - WINDOWS[chunk][0]
    width = SHIFTED[chunk][1] - SHIFTED[chunk][0]
    edge = [] if last else [jax.ShapeDtypeStruct((2, WIN, WIN, LANES), jnp.float32)]
    shapes = [tokens_shape(width * TOK // 2)] * 4 + edge
    args = (own, oth, *before, *weights)
    return pl.pallas_call(
        functools.partial(layer_one_kernel, count, first, last),
        out_shape=shapes,
        in_specs=[VMEM] * len(args),
        out_specs=[VMEM] * len(shapes),
        scratch_shapes=[
            pltpu.VMEM((2, WIN, (width + 1) * WIN, LANES), jnp.float32),
            pltpu.VMEM((2, 2, width, 4, WIN, LANES), jnp.float32),
            *attention_scratch(count),
        ],
        compiler_params=PARAMS,
        name="layer_one",
    )(*args)


def layer_two(chunk, pieces, weights):
    count = SHIFTED[chunk][1] - SHIFTED[chunk][0]
    return pl.pallas_call(
        functools.partial(layer_two_kernel, count),
        out_shape=[tokens_shape(count * TOK // 2)] * 4,
        in_specs=[VMEM] * 9,
        out_specs=[VMEM] * 4,
        scratch_shapes=attention_scratch(count),
        compiler_params=PARAMS,
        name="layer_two",
    )(*pieces, *weights)


def from_tokens(h, pieces):
    return pl.pallas_call(
        from_tokens_kernel,
        out_shape=jax.ShapeDtypeStruct((C, WIN, 2 * LANES), jnp.bfloat16),
        in_specs=[SMEM] + [VMEM] * len(pieces),
        out_specs=VMEM,
        scratch_shapes=[
            pltpu.VMEM((2, 2, HALF, 4, WIN, LANES), jnp.float32),
            pltpu.VMEM((2, C * WIN, LANES), jnp.float32),
        ],
        compiler_params=PARAMS,
        name="from_tokens",
    )(h, *pieces)


def pad_to(array, rows, cols):
    return jnp.pad(array, ((0, rows - array.shape[0]), (0, cols - array.shape[1])))


def by_head(array):
    spread = array.reshape(HEADS, HEAD, array.shape[1])
    spread = jnp.pad(spread, ((0, 0), (0, VHEAD - HEAD), (0, 0)))
    return spread.reshape(HEADS * VHEAD, array.shape[1])


def prepared(w_mut, w_slf, w_prj, w_gte, w_upp, w_dwn):
    w_k = [pad_to(w[:, C : 2 * C], LANES, LANES) for w in (w_mut, w_slf)]
    w_q = [pad_to(w[:, :C].T, LANES, LANES) for w in (w_mut, w_slf)]
    w_v = [pad_to(by_head(w[:, 2 * C :].T), HEADS * VHEAD, LANES) for w in (w_mut, w_slf)]
    w_p = [pad_to(by_head(w), HEADS * VHEAD, LANES) for w in (w_prj[:C], w_prj[C:])]
    return (
        jnp.concatenate(w_k, axis=1),
        jnp.concatenate(w_q + w_v, axis=0),
        jnp.concatenate(w_p, axis=0),
        jnp.concatenate([pad_to(w, LANES, 2 * LANES) for w in (w_gte, w_upp)], axis=1),
        pad_to(w_dwn, 2 * LANES, LANES),
    )


def on_device(features, *weights):
    frames, strips = lax.axis_size("frame"), lax.axis_size("strip")

    def route(frame_step, strip_step):
        pairs = []
        for f in range(frames):
            for s in range(strips):
                to = (f + frame_step * (1 - 2 * (f % 2))) % frames
                pairs.append((f * strips + s, to * strips + (s + strip_step) % strips))
        return pairs

    def send(value, frame_step, strip_step):
        return lax.ppermute(value, ("frame", "strip"), route(frame_step, strip_step))

    h = (lax.axis_index("frame") % 2).astype(jnp.int32).reshape(1)
    w_one = prepared(*[w[0] for w in weights])
    w_two = prepared(*[w[1] for w in weights])
    parts = to_tokens(h, features[0])
    chunks = range(len(WINDOWS))
    others = [send(parts[k], 1, 0) for k in chunks]
    edge = ()
    pieces = []
    for k in chunks:
        own_up, own_lo, oth_up, oth_lo, *edge = layer_one(
            k, parts[len(WINDOWS) + k], others[k], edge, w_one
        )
        oth_lo = send(oth_lo, 2, 0)
        oth_up = send(oth_up, 2, -1)
        own_up = send(own_up, 0, -1)
        pieces.append((own_lo, own_up, oth_lo, oth_up))
    home = []
    for k in chunks:
        own_lo, own_up, oth_lo, oth_up = layer_two(k, pieces[k], w_two)
        oth_lo = send(oth_lo, -1, 0)
        oth_up = send(oth_up, -1, 1)
        own_up = send(own_up, 0, 1)
        home += [own_lo, own_up, oth_lo, oth_up]
    return from_tokens(h, home)[None]


def solution(mesh):
    in_specs = (P("frame", None, "strip", None), P(), P(), P(), P(), P(), P())
    out_specs = P("frame", None, "strip", None)
    return jax.shard_map(
        on_device, mesh=mesh, in_specs=in_specs, out_specs=out_specs, check_vma=False
    )
```

```python
import functools

import jax
import jax.numpy as jnp
import numpy as np
from jax import lax
from jax.experimental import pallas as pl
from jax.experimental.pallas import tpu as pltpu
from jax.sharding import PartitionSpec as P

C = 120
HEADS = 6
HEAD = 20
FFN = 240
WIN = 8
LANES = 128
VHEAD = 24
HALF = 16
TOK = WIN * WIN
EPS = 1e-05
SHIFTED = ((0, 8), (8, 16))
WINDOWS = ((0, 9), (9, 17))
EXP2_SCALE = float(np.log2(np.e) * HEAD**-0.5)
VMEM_LIMIT = 56 * 1024 * 1024


def matmul(a, b):
    return lax.dot_general(a, b, (((1,), (0,)), ((), ())), preferred_element_type=jnp.float32)


def matmul_nt(a, b):
    return lax.dot_general(a, b, (((1,), (1,)), ((), ())), preferred_element_type=jnp.float32)


def matmul_tn(a, b):
    return lax.dot_general(a, b, (((0,), (0,)), ((), ())), preferred_element_type=jnp.float32)


def normed(x):
    lane = lax.broadcasted_iota(jnp.int32, x.shape, 1)
    mean = jnp.sum(x, axis=1, keepdims=True) * (1.0 / C)
    centred = jnp.where(lane < C, x - mean, 0.0)
    spread = jnp.sum(centred * centred, axis=1, keepdims=True) * (1.0 / C)
    return (centred * lax.rsqrt(spread + EPS)).astype(jnp.bfloat16)


def head_only(q_t, head):
    low = head * HEAD // 16 * 16
    high = -(-(head * HEAD + HEAD) // 16) * 16
    part = q_t[low:high].astype(jnp.float32)
    row = lax.broadcasted_iota(jnp.int32, part.shape, 0) + low
    keep = (row >= head * HEAD) & (row < head * HEAD + HEAD)
    part = jnp.where(keep, part, 0.0).astype(jnp.bfloat16)
    pieces = [part]
    if low:
        pieces.insert(0, jnp.zeros((low, q_t.shape[1]), jnp.bfloat16))
    if high < LANES:
        pieces.append(jnp.zeros((LANES - high, q_t.shape[1]), jnp.bfloat16))
    return jnp.concatenate(pieces, axis=0)


def softmax_rows(scores):
    top = jnp.max(scores, axis=0, keepdims=True)
    weights = jnp.exp2((scores - top) * EXP2_SCALE)
    total = jnp.sum(weights, axis=0, keepdims=True)
    return weights * (1.0 / total)


def project_windows(x, w_k, w_qv, keys, qv_t, first):
    normal = normed(x)
    new_keys = matmul(normal, w_k[...]).astype(jnp.bfloat16)
    new_qv = matmul_nt(w_qv[...], normal).astype(jnp.bfloat16)
    for i in range(x.shape[0] // LANES):
        span = slice(i * LANES, (i + 1) * LANES)
        keys[first + i] = new_keys[span]
        qv_t[first + i] = new_qv[:, span]


def score_block(kind, pair, keys, qv_t, window, of_first):
    kind_q = qv_t[window, kind * LANES : (kind + 1) * LANES]
    queries = jnp.concatenate(
        [head_only(kind_q, 2 * pair), head_only(kind_q, 2 * pair + 1)], axis=1
    )
    scores = matmul(keys[window, :, kind * LANES : (kind + 1) * LANES], queries)
    if kind == 0:
        scores = jnp.where(of_first, scores[TOK:], scores[:TOK])
    return scores


def mix_block(kind, pair, scores, qv_t, window, of_first):
    probs = [softmax_rows(scores[:, i * LANES : (i + 1) * LANES]) for i in range(2)]
    probs = jnp.concatenate(probs, axis=1)
    if kind == 0:
        probs = jnp.concatenate(
            [jnp.where(of_first, 0.0, probs), jnp.where(of_first, probs, 0.0)], axis=0
        )
    base = 2 * LANES + (kind * HEADS + 2 * pair) * VHEAD
    mixed = matmul(qv_t[window, base : base + 2 * VHEAD], probs.astype(jnp.bfloat16))
    return [mixed[:VHEAD, :LANES], mixed[VHEAD:, LANES:]]


def attend(count, keys, qv_t, mutual_scores, self_scores, joined):
    scores = (mutual_scores, self_scores)
    lane = lax.broadcasted_iota(jnp.int32, (TOK, 2 * LANES), 1)
    of_first = (lane % LANES) < TOK
    blocks = [(kind, pair) for kind in range(2) for pair in range(HEADS // 2)]
    for kind, pair in blocks:
        scores[kind][0, pair] = score_block(kind, pair, keys, qv_t, 0, of_first)
    for i in range(count):
        outs = []
        for kind, pair in blocks:
            ref = scores[kind]
            if i + 1 < count:
                ref[(i + 1) % 2, pair] = score_block(kind, pair, keys, qv_t, i + 1, of_first)
            outs += mix_block(kind, pair, ref[i % 2, pair], qv_t, i, of_first)
        joined[i] = jnp.concatenate(outs, axis=0).astype(jnp.bfloat16)


def finished(x, joined, w_prj, w_gu, w_dwn):
    mixed = [matmul_tn(block, w_prj[...]) for block in joined]
    middle = x + jnp.concatenate(mixed, axis=0)
    both = matmul(normed(middle), w_gu[...])
    gate, up = both[:, : 2 * LANES], both[:, 2 * LANES :]
    gelu = 0.5 * gate * (1.0 + lax.erf(gate * float(np.sqrt(0.5))))
    hidden = (gelu * up).astype(jnp.bfloat16)
    return middle + matmul(hidden, w_dwn[...])


def to_tokens_kernel(h_ref, x_ref, *rest):
    outs, (wide, tiles) = rest[:-2], rest[-2:]
    h = h_ref[0]
    for half in range(2):
        part = x_ref[:, :, half * LANES : (half + 1) * LANES].astype(jnp.float32)
        wide[half] = part.reshape(C * WIN, LANES)
    pad = jnp.zeros((LANES - C, LANES), jnp.float32)
    for k in range(2):
        half = 1 - h if k == 0 else h
        for r in range(WIN):
            block = wide.at[half][pl.ds(r, C, stride=WIN), :]
            block = jnp.concatenate([block, pad], axis=0).T
            tiles[k, :HALF, r] = block.reshape(HALF, WIN, LANES)
    for k in range(2):
        tiles[k, HALF] = tiles[1 - k, 0]
    for k in range(2):
        for j, (low, high) in enumerate(WINDOWS):
            part = tiles[k, low:high].reshape((high - low) * TOK, LANES)
            outs[k * len(WINDOWS) + j][...] = part.astype(jnp.bfloat16)


def layer_one_kernel(count, first, last, own_ref, oth_ref, *rest):
    if not first:
        before, rest = rest[0], rest[1:]
    w_k, w_qv, w_prj, w_gu, w_dwn = rest[:5]
    outs, rest = rest[5:9], rest[9:]
    if not last:
        after, rest = rest[0], rest[1:]
    flat, tiles, *scratch = rest
    keys, qv_t, joined = scratch[0], scratch[1], scratch[-1]
    shift = 0 if first else WIN

    def tokens():
        parts = []
        for i in range(count):
            span = slice(i * TOK, (i + 1) * TOK)
            parts += [own_ref[span], oth_ref[span]]
        return jnp.concatenate(parts, axis=0).astype(jnp.float32)

    project_windows(tokens(), w_k, w_qv, keys, qv_t, 0)
    attend(count, *scratch)
    y = finished(tokens(), [joined[i] for i in range(count)], w_prj, w_gu, w_dwn)
    y = y.reshape(count, 2, WIN, WIN, LANES)
    if not first:
        flat[:, :, :WIN, :] = before[...]
    for i in range(count):
        for f in range(2):
            flat[f, :, shift + i * WIN : shift + (i + 1) * WIN, :] = y[i, f]
    width = shift + (count - 1) * WIN
    if not last:
        after[...] = flat[:, :, width : width + WIN, :]
    for f in range(2):
        for r in range(WIN):
            block = flat[f, r, WIN // 2 : WIN // 2 + width, :]
            tiles[f, r // 4, :, r % 4] = block.reshape(width // WIN, WIN, LANES)
        for k in range(2):
            piece = tiles[f, k].reshape(width * 4, LANES)
            outs[2 * f + k][...] = piece.astype(jnp.bfloat16)


def layer_two_kernel(count, *rest):
    ins, rest = rest[:4], rest[4:]
    w_k, w_qv, w_prj, w_gu, w_dwn = rest[:5]
    outs, scratch = rest[5:9], rest[9:]
    keys, qv_t, joined = scratch[0], scratch[1], scratch[-1]
    half_tok = TOK // 2
    spans = [slice(i * half_tok, (i + 1) * half_tok) for i in range(count)]

    def tokens():
        return jnp.concatenate([ref[s] for s in spans for ref in ins], axis=0).astype(jnp.float32)

    project_windows(tokens(), w_k, w_qv, keys, qv_t, 0)
    attend(count, *scratch)
    y = finished(tokens(), [joined[i] for i in range(count)], w_prj, w_gu, w_dwn)
    y = y.astype(jnp.bfloat16)
    for i in range(count):
        for j in range(4):
            low = i * LANES + j * half_tok
            outs[j][spans[i]] = y[low : low + half_tok]


def from_tokens_kernel(h_ref, *rest):
    ins, (out_ref, tiles, wide) = rest[:-3], rest[-3:]
    h = h_ref[0]
    for k, (low, high) in enumerate(SHIFTED):
        for j in range(4):
            half = h if j < 2 else 1 - h
            part = ins[4 * k + j][...].astype(jnp.float32)
            tiles[half, j % 2, low:high] = part.reshape(high - low, 4, WIN, LANES)
    for r in range(WIN):
        lo = 0 if r >= 4 else 1
        row = [tiles[half, lo, :, r % 4].reshape(LANES, LANES).T for half in range(2)]
        row = pltpu.roll(jnp.concatenate(row, axis=1), WIN // 2, 1)
        for half in range(2):
            part = row[:C, half * LANES : (half + 1) * LANES]
            wide.at[half][pl.ds(r, C, stride=WIN), :] = part
    for half in range(2):
        part = wide[half].reshape(C, WIN, LANES).astype(jnp.bfloat16)
        out_ref[:, :, half * LANES : (half + 1) * LANES] = part


VMEM = pl.BlockSpec(memory_space=pltpu.VMEM)
SMEM = pl.BlockSpec(memory_space=pltpu.SMEM)
COST = pl.CostEstimate(flops=8 * 10**9, bytes_accessed=2**20, transcendentals=2**20)
PARAMS = pltpu.CompilerParams(vmem_limit_bytes=VMEM_LIMIT)


def attention_scratch(count):
    return [
        pltpu.VMEM((count, LANES, 2 * LANES), jnp.bfloat16),
        pltpu.VMEM((count, 2 * LANES + 2 * HEADS * VHEAD, LANES), jnp.bfloat16),
        pltpu.VMEM((2, HEADS // 2, TOK, 2 * LANES), jnp.float32),
        pltpu.VMEM((2, HEADS // 2, 2 * TOK, 2 * LANES), jnp.float32),
        pltpu.VMEM((count, 2 * HEADS * VHEAD, LANES), jnp.bfloat16),
    ]


def tokens_shape(rows):
    return jax.ShapeDtypeStruct((rows, LANES), jnp.bfloat16)


def to_tokens(h, x):
    shapes = [tokens_shape((high - low) * TOK) for low, high in WINDOWS]
    return pl.pallas_call(
        to_tokens_kernel,
        out_shape=shapes * 2,
        in_specs=[SMEM, VMEM],
        out_specs=[VMEM] * (2 * len(shapes)),
        scratch_shapes=[
            pltpu.VMEM((2, C * WIN, LANES), jnp.float32),
            pltpu.VMEM((2, HALF + 1, WIN, WIN, LANES), jnp.float32),
        ],
        compiler_params=PARAMS,
        name="to_tokens",
    )(h, x)


def layer_one(chunk, own, oth, before, weights):
    first, last = chunk == 0, chunk == len(WINDOWS) - 1
    count = WINDOWS[chunk][1] - WINDOWS[chunk][0]
    width = SHIFTED[chunk][1] - SHIFTED[chunk][0]
    edge = [] if last else [jax.ShapeDtypeStruct((2, WIN, WIN, LANES), jnp.float32)]
    shapes = [tokens_shape(width * TOK // 2)] * 4 + edge
    args = (own, oth, *before, *weights)
    return pl.pallas_call(
        functools.partial(layer_one_kernel, count, first, last),
        out_shape=shapes,
        in_specs=[VMEM] * len(args),
        out_specs=[VMEM] * len(shapes),
        scratch_shapes=[
            pltpu.VMEM((2, WIN, (width + 1) * WIN, LANES), jnp.float32),
            pltpu.VMEM((2, 2, width, 4, WIN, LANES), jnp.float32),
            *attention_scratch(count),
        ],
        compiler_params=PARAMS,
        cost_estimate=COST,
        name="layer_one",
    )(*args)


def layer_two(chunk, pieces, weights):
    count = SHIFTED[chunk][1] - SHIFTED[chunk][0]
    return pl.pallas_call(
        functools.partial(layer_two_kernel, count),
        out_shape=[tokens_shape(count * TOK // 2)] * 4,
        in_specs=[VMEM] * 9,
        out_specs=[VMEM] * 4,
        scratch_shapes=attention_scratch(count),
        compiler_params=PARAMS,
        cost_estimate=COST,
        name="layer_two",
    )(*pieces, *weights)


def from_tokens(h, pieces):
    return pl.pallas_call(
        from_tokens_kernel,
        out_shape=jax.ShapeDtypeStruct((C, WIN, 2 * LANES), jnp.bfloat16),
        in_specs=[SMEM] + [VMEM] * len(pieces),
        out_specs=VMEM,
        scratch_shapes=[
            pltpu.VMEM((2, 2, HALF, 4, WIN, LANES), jnp.float32),
            pltpu.VMEM((2, C * WIN, LANES), jnp.float32),
        ],
        compiler_params=PARAMS,
        name="from_tokens",
    )(h, *pieces)


def prepare_kernel(w_mut, w_slf, w_prj, w_gte, w_upp, w_dwn, *outs):
    def selector(rows, cols, picks):
        row = lax.broadcasted_iota(jnp.int32, (rows, cols), 0)
        col = lax.broadcasted_iota(jnp.int32, (rows, cols), 1)
        hit = None
        for first_row, first_col, size in picks:
            inside = (row >= first_row) & (row < first_row + size)
            run = inside & (col - first_col == row - first_row)
            hit = run if hit is None else hit | run
        return jnp.where(hit, 1.0, 0.0).astype(jnp.bfloat16)

    by_head = [(h * VHEAD, h * HEAD, HEAD) for h in range(HEADS)]
    pick_q = selector(LANES, 3 * C, [(0, 0, C)])
    pick_v = selector(HEADS * VHEAD, 3 * C, [(r, 2 * C + c, n) for r, c, n in by_head])
    pick_k = selector(LANES, 3 * C, [(0, C, C)])
    spread = selector(HEADS * VHEAD, C, by_head)
    for layer in range(2):
        w_k, w_qv, w_p, w_gu, w_d = outs[5 * layer : 5 * layer + 5]
        for ref in (w_k, w_qv, w_p, w_gu, w_d):
            ref[...] = jnp.zeros(ref.shape, jnp.bfloat16)
        v_rows = HEADS * VHEAD
        for i, w in enumerate((w_mut, w_slf)):
            w = w[layer]
            w_k[:C, i * LANES : (i + 1) * LANES] = matmul_nt(w, pick_k).astype(jnp.bfloat16)
            w_qv[i * LANES : (i + 1) * LANES, :C] = matmul_nt(pick_q, w).astype(jnp.bfloat16)
            low = 2 * LANES + i * v_rows
            w_qv[low : low + v_rows, :C] = matmul_nt(pick_v, w).astype(jnp.bfloat16)
            part = matmul(spread, w_prj[layer, i * C : (i + 1) * C])
            w_p[i * v_rows : (i + 1) * v_rows, :C] = part.astype(jnp.bfloat16)
        w_gu[:C, :FFN] = w_gte[layer]
        w_gu[:C, 2 * LANES : 2 * LANES + FFN] = w_upp[layer]
        w_d[:FFN, :C] = w_dwn[layer]


def prepared(*weights):
    v_rows = HEADS * VHEAD
    shapes = [
        (LANES, 2 * LANES),
        (2 * LANES + 2 * v_rows, LANES),
        (2 * v_rows, LANES),
        (LANES, 4 * LANES),
        (2 * LANES, LANES),
    ] * 2
    return pl.pallas_call(
        prepare_kernel,
        out_shape=[jax.ShapeDtypeStruct(shape, jnp.bfloat16) for shape in shapes],
        in_specs=[VMEM] * len(weights),
        out_specs=[VMEM] * len(shapes),
        compiler_params=PARAMS,
        name="prepare",
    )(*weights)


def on_device(features, *weights):
    frames, strips = lax.axis_size("frame"), lax.axis_size("strip")

    def route(frame_step, strip_step):
        pairs = []
        for f in range(frames):
            for s in range(strips):
                to = (f + frame_step * (1 - 2 * (f % 2))) % frames
                pairs.append((f * strips + s, to * strips + (s + strip_step) % strips))
        return pairs

    def send(value, frame_step, strip_step):
        return lax.ppermute(value, ("frame", "strip"), route(frame_step, strip_step))

    h = (lax.axis_index("frame") % 2).astype(jnp.int32).reshape(1)
    ready = prepared(*weights)
    w_one, w_two = ready[:5], ready[5:]
    parts = to_tokens(h, features[0])
    chunks = range(len(WINDOWS))
    others = [send(parts[k], 1, 0) for k in chunks]
    edge = ()
    pieces = []
    for k in chunks:
        own_up, own_lo, oth_up, oth_lo, *edge = layer_one(
            k, parts[len(WINDOWS) + k], others[k], edge, w_one
        )
        oth_lo = send(oth_lo, 2, 0)
        oth_up = send(oth_up, 2, -1)
        own_up = send(own_up, 0, -1)
        pieces.append((own_lo, own_up, oth_lo, oth_up))
    home = []
    for k in chunks:
        own_lo, own_up, oth_lo, oth_up = layer_two(k, pieces[k], w_two)
        oth_lo = send(oth_lo, -1, 0)
        oth_up = send(oth_up, -1, 1)
        own_up = send(own_up, 0, 1)
        home += [own_lo, own_up, oth_lo, oth_up]
    return from_tokens(h, home)[None]


def solution(mesh):
    in_specs = (P("frame", None, "strip", None), P(), P(), P(), P(), P(), P())
    out_specs = P("frame", None, "strip", None)
    return jax.shard_map(
        on_device, mesh=mesh, in_specs=in_specs, out_specs=out_specs, check_vma=False
    )
```

```python
import functools

import jax
import jax.numpy as jnp
import numpy as np
from jax import lax
from jax.experimental import pallas as pl
from jax.experimental.pallas import tpu as pltpu
from jax.sharding import PartitionSpec as P

C = 120
HEADS = 6
HEAD = 20
FFN = 240
WIN = 8
LANES = 128
VHEAD = 24
HALF = 16
GROUP = 8
TOK = WIN * WIN
EPS = 1e-05
SHIFTED = ((0, 16),)
WINDOWS = ((0, 17),)
EXP2_SCALE = float(np.log2(np.e) * HEAD**-0.5)
VMEM_LIMIT = 56 * 1024 * 1024


def matmul(a, b):
    return lax.dot_general(a, b, (((1,), (0,)), ((), ())), preferred_element_type=jnp.float32)


def matmul_nt(a, b):
    return lax.dot_general(a, b, (((1,), (1,)), ((), ())), preferred_element_type=jnp.float32)


def matmul_tn(a, b):
    return lax.dot_general(a, b, (((0,), (0,)), ((), ())), preferred_element_type=jnp.float32)


def normed(x):
    lane = lax.broadcasted_iota(jnp.int32, x.shape, 1)
    mean = jnp.sum(x, axis=1, keepdims=True) * (1.0 / C)
    centred = jnp.where(lane < C, x - mean, 0.0)
    spread = jnp.sum(centred * centred, axis=1, keepdims=True) * (1.0 / C)
    return (centred * lax.rsqrt(spread + EPS)).astype(jnp.bfloat16)


def head_only(q_t, head):
    low = head * HEAD // 16 * 16
    high = -(-(head * HEAD + HEAD) // 16) * 16
    part = q_t[low:high].astype(jnp.float32)
    row = lax.broadcasted_iota(jnp.int32, part.shape, 0) + low
    keep = (row >= head * HEAD) & (row < head * HEAD + HEAD)
    part = jnp.where(keep, part, 0.0).astype(jnp.bfloat16)
    pieces = [part]
    if low:
        pieces.insert(0, jnp.zeros((low, q_t.shape[1]), jnp.bfloat16))
    if high < LANES:
        pieces.append(jnp.zeros((LANES - high, q_t.shape[1]), jnp.bfloat16))
    return jnp.concatenate(pieces, axis=0)


def softmax_rows(scores):
    top = jnp.max(scores, axis=0, keepdims=True)
    weights = jnp.exp2((scores - top) * EXP2_SCALE)
    total = jnp.sum(weights, axis=0, keepdims=True)
    return weights * (1.0 / total)


def project_windows(x, w_k, w_qv, keys, qv_t, first):
    normal = normed(x)
    new_keys = matmul(normal, w_k[...]).astype(jnp.bfloat16)
    new_qv = matmul_nt(w_qv[...], normal).astype(jnp.bfloat16)
    for i in range(x.shape[0] // LANES):
        span = slice(i * LANES, (i + 1) * LANES)
        keys[first + i] = new_keys[span]
        qv_t[first + i] = new_qv[:, span]


def score_block(kind, pair, keys, qv_t, window, of_first):
    kind_q = qv_t[window, kind * LANES : (kind + 1) * LANES]
    queries = jnp.concatenate(
        [head_only(kind_q, 2 * pair), head_only(kind_q, 2 * pair + 1)], axis=1
    )
    scores = matmul(keys[window, :, kind * LANES : (kind + 1) * LANES], queries)
    if kind == 0:
        scores = jnp.where(of_first, scores[TOK:], scores[:TOK])
    return scores


def mix_block(kind, pair, scores, qv_t, window, of_first):
    probs = [softmax_rows(scores[:, i * LANES : (i + 1) * LANES]) for i in range(2)]
    probs = jnp.concatenate(probs, axis=1)
    if kind == 0:
        probs = jnp.concatenate(
            [jnp.where(of_first, 0.0, probs), jnp.where(of_first, probs, 0.0)], axis=0
        )
    base = 2 * LANES + (kind * HEADS + 2 * pair) * VHEAD
    mixed = matmul(qv_t[window, base : base + 2 * VHEAD], probs.astype(jnp.bfloat16))
    return [mixed[:VHEAD, :LANES], mixed[VHEAD:, LANES:]]


def attend(count, keys, qv_t, mutual_scores, self_scores, joined):
    scores = (mutual_scores, self_scores)
    lane = lax.broadcasted_iota(jnp.int32, (TOK, 2 * LANES), 1)
    of_first = (lane % LANES) < TOK
    blocks = [(kind, pair) for kind in range(2) for pair in range(HEADS // 2)]
    for kind, pair in blocks:
        scores[kind][0, pair] = score_block(kind, pair, keys, qv_t, 0, of_first)
    for i in range(count):
        outs = []
        for kind, pair in blocks:
            ref = scores[kind]
            if i + 1 < count:
                ref[(i + 1) % 2, pair] = score_block(kind, pair, keys, qv_t, i + 1, of_first)
            outs += mix_block(kind, pair, ref[i % 2, pair], qv_t, i, of_first)
        joined[i] = jnp.concatenate(outs, axis=0).astype(jnp.bfloat16)


def finished(x, joined, w_prj, w_gu, w_dwn):
    mixed = [matmul_tn(block, w_prj[...]) for block in joined]
    middle = x + jnp.concatenate(mixed, axis=0)
    both = matmul(normed(middle), w_gu[...])
    gate, up = both[:, : 2 * LANES], both[:, 2 * LANES :]
    gelu = 0.5 * gate * (1.0 + lax.erf(gate * float(np.sqrt(0.5))))
    hidden = (gelu * up).astype(jnp.bfloat16)
    return middle + matmul(hidden, w_dwn[...])


def to_tokens_kernel(h_ref, x_ref, *rest):
    outs, (wide, tiles) = rest[:-2], rest[-2:]
    h = h_ref[0]
    for half in range(2):
        part = x_ref[:, :, half * LANES : (half + 1) * LANES].astype(jnp.float32)
        wide[half] = part.reshape(C * WIN, LANES)
    pad = jnp.zeros((LANES - C, LANES), jnp.float32)
    for k in range(2):
        half = 1 - h if k == 0 else h
        for r in range(WIN):
            block = wide.at[half][pl.ds(r, C, stride=WIN), :]
            block = jnp.concatenate([block, pad], axis=0).T
            tiles[k, :HALF, r] = block.reshape(HALF, WIN, LANES)
    for k in range(2):
        tiles[k, HALF] = tiles[1 - k, 0]
    for k in range(2):
        for j, (low, high) in enumerate(WINDOWS):
            part = tiles[k, low:high].reshape((high - low) * TOK, LANES)
            outs[k * len(WINDOWS) + j][...] = part.astype(jnp.bfloat16)


def grouped(count):
    parts = max(1, count // GROUP)
    cuts = [count * i // parts for i in range(parts + 1)]
    return [range(low, high) for low, high in zip(cuts[:-1], cuts[1:])]


def layer_one_kernel(count, first, last, own_ref, oth_ref, *rest):
    if not first:
        before, rest = rest[0], rest[1:]
    w_k, w_qv, w_prj, w_gu, w_dwn = rest[:5]
    outs, rest = rest[5:9], rest[9:]
    if not last:
        after, rest = rest[0], rest[1:]
    flat, tiles, *scratch = rest
    keys, qv_t, joined = scratch[0], scratch[1], scratch[-1]
    shift = 0 if first else WIN

    def tokens(group):
        parts = []
        for i in group:
            span = slice(i * TOK, (i + 1) * TOK)
            parts += [own_ref[span], oth_ref[span]]
        return jnp.concatenate(parts, axis=0).astype(jnp.float32)

    for group in grouped(count):
        project_windows(tokens(group), w_k, w_qv, keys, qv_t, group[0])
    attend(count, *scratch)
    if not first:
        flat[:, :, :WIN, :] = before[...]
    for group in grouped(count):
        y = finished(tokens(group), [joined[i] for i in group], w_prj, w_gu, w_dwn)
        y = y.reshape(len(group), 2, WIN, WIN, LANES)
        for j, i in enumerate(group):
            for f in range(2):
                flat[f, :, shift + i * WIN : shift + (i + 1) * WIN, :] = y[j, f]
    width = shift + (count - 1) * WIN
    if not last:
        after[...] = flat[:, :, width : width + WIN, :]
    for f in range(2):
        for r in range(WIN):
            block = flat[f, r, WIN // 2 : WIN // 2 + width, :]
            tiles[f, r // 4, :, r % 4] = block.reshape(width // WIN, WIN, LANES)
        for k in range(2):
            piece = tiles[f, k].reshape(width * 4, LANES)
            outs[2 * f + k][...] = piece.astype(jnp.bfloat16)


def layer_two_kernel(count, *rest):
    ins, rest = rest[:4], rest[4:]
    w_k, w_qv, w_prj, w_gu, w_dwn = rest[:5]
    outs, scratch = rest[5:9], rest[9:]
    keys, qv_t, joined = scratch[0], scratch[1], scratch[-1]
    half_tok = TOK // 2
    spans = [slice(i * half_tok, (i + 1) * half_tok) for i in range(count)]

    def tokens(group):
        parts = [ref[spans[i]] for i in group for ref in ins]
        return jnp.concatenate(parts, axis=0).astype(jnp.float32)

    for group in grouped(count):
        project_windows(tokens(group), w_k, w_qv, keys, qv_t, group[0])
    attend(count, *scratch)
    for group in grouped(count):
        y = finished(tokens(group), [joined[i] for i in group], w_prj, w_gu, w_dwn)
        y = y.astype(jnp.bfloat16)
        for k, i in enumerate(group):
            for j in range(4):
                low = k * LANES + j * half_tok
                outs[j][spans[i]] = y[low : low + half_tok]


def from_tokens_kernel(h_ref, *rest):
    ins, (out_ref, tiles, wide) = rest[:-3], rest[-3:]
    h = h_ref[0]
    for k, (low, high) in enumerate(SHIFTED):
        for j in range(4):
            half = h if j < 2 else 1 - h
            part = ins[4 * k + j][...].astype(jnp.float32)
            tiles[half, j % 2, low:high] = part.reshape(high - low, 4, WIN, LANES)
    for r in range(WIN):
        lo = 0 if r >= 4 else 1
        row = [tiles[half, lo, :, r % 4].reshape(LANES, LANES).T for half in range(2)]
        row = pltpu.roll(jnp.concatenate(row, axis=1), WIN // 2, 1)
        for half in range(2):
            part = row[:C, half * LANES : (half + 1) * LANES]
            wide.at[half][pl.ds(r, C, stride=WIN), :] = part
    for half in range(2):
        part = wide[half].reshape(C, WIN, LANES).astype(jnp.bfloat16)
        out_ref[:, :, half * LANES : (half + 1) * LANES] = part


VMEM = pl.BlockSpec(memory_space=pltpu.VMEM)
SMEM = pl.BlockSpec(memory_space=pltpu.SMEM)
COST = pl.CostEstimate(flops=8 * 10**9, bytes_accessed=2**20, transcendentals=2**20)
PARAMS = pltpu.CompilerParams(vmem_limit_bytes=VMEM_LIMIT)


def attention_scratch(count):
    return [
        pltpu.VMEM((count, LANES, 2 * LANES), jnp.bfloat16),
        pltpu.VMEM((count, 2 * LANES + 2 * HEADS * VHEAD, LANES), jnp.bfloat16),
        pltpu.VMEM((2, HEADS // 2, TOK, 2 * LANES), jnp.float32),
        pltpu.VMEM((2, HEADS // 2, 2 * TOK, 2 * LANES), jnp.float32),
        pltpu.VMEM((count, 2 * HEADS * VHEAD, LANES), jnp.bfloat16),
    ]


def tokens_shape(rows):
    return jax.ShapeDtypeStruct((rows, LANES), jnp.bfloat16)


def to_tokens(h, x):
    shapes = [tokens_shape((high - low) * TOK) for low, high in WINDOWS]
    return pl.pallas_call(
        to_tokens_kernel,
        out_shape=shapes * 2,
        in_specs=[SMEM, VMEM],
        out_specs=[VMEM] * (2 * len(shapes)),
        scratch_shapes=[
            pltpu.VMEM((2, C * WIN, LANES), jnp.float32),
            pltpu.VMEM((2, HALF + 1, WIN, WIN, LANES), jnp.float32),
        ],
        compiler_params=PARAMS,
        name="to_tokens",
    )(h, x)


def layer_one(chunk, own, oth, before, weights):
    first, last = chunk == 0, chunk == len(WINDOWS) - 1
    count = WINDOWS[chunk][1] - WINDOWS[chunk][0]
    width = SHIFTED[chunk][1] - SHIFTED[chunk][0]
    edge = [] if last else [jax.ShapeDtypeStruct((2, WIN, WIN, LANES), jnp.float32)]
    shapes = [tokens_shape(width * TOK // 2)] * 4 + edge
    args = (own, oth, *before, *weights)
    return pl.pallas_call(
        functools.partial(layer_one_kernel, count, first, last),
        out_shape=shapes,
        in_specs=[VMEM] * len(args),
        out_specs=[VMEM] * len(shapes),
        scratch_shapes=[
            pltpu.VMEM((2, WIN, (width + 1) * WIN, LANES), jnp.float32),
            pltpu.VMEM((2, 2, width, 4, WIN, LANES), jnp.float32),
            *attention_scratch(count),
        ],
        compiler_params=PARAMS,
        cost_estimate=COST,
        name="layer_one",
    )(*args)


def layer_two(chunk, pieces, weights):
    count = SHIFTED[chunk][1] - SHIFTED[chunk][0]
    return pl.pallas_call(
        functools.partial(layer_two_kernel, count),
        out_shape=[tokens_shape(count * TOK // 2)] * 4,
        in_specs=[VMEM] * 9,
        out_specs=[VMEM] * 4,
        scratch_shapes=attention_scratch(count),
        compiler_params=PARAMS,
        cost_estimate=COST,
        name="layer_two",
    )(*pieces, *weights)


def from_tokens(h, pieces):
    return pl.pallas_call(
        from_tokens_kernel,
        out_shape=jax.ShapeDtypeStruct((C, WIN, 2 * LANES), jnp.bfloat16),
        in_specs=[SMEM] + [VMEM] * len(pieces),
        out_specs=VMEM,
        scratch_shapes=[
            pltpu.VMEM((2, 2, HALF, 4, WIN, LANES), jnp.float32),
            pltpu.VMEM((2, C * WIN, LANES), jnp.float32),
        ],
        compiler_params=PARAMS,
        name="from_tokens",
    )(h, *pieces)


def prepare_kernel(w_mut, w_slf, w_prj, w_gte, w_upp, w_dwn, *outs):
    def selector(rows, cols, picks):
        row = lax.broadcasted_iota(jnp.int32, (rows, cols), 0)
        col = lax.broadcasted_iota(jnp.int32, (rows, cols), 1)
        hit = None
        for first_row, first_col, size in picks:
            inside = (row >= first_row) & (row < first_row + size)
            run = inside & (col - first_col == row - first_row)
            hit = run if hit is None else hit | run
        return jnp.where(hit, 1.0, 0.0).astype(jnp.bfloat16)

    by_head = [(h * VHEAD, h * HEAD, HEAD) for h in range(HEADS)]
    pick_q = selector(LANES, 3 * C, [(0, 0, C)])
    pick_v = selector(HEADS * VHEAD, 3 * C, [(r, 2 * C + c, n) for r, c, n in by_head])
    pick_k = selector(LANES, 3 * C, [(0, C, C)])
    spread = selector(HEADS * VHEAD, C, by_head)
    for layer in range(2):
        w_k, w_qv, w_p, w_gu, w_d = outs[5 * layer : 5 * layer + 5]
        for ref in (w_k, w_qv, w_p, w_gu, w_d):
            ref[...] = jnp.zeros(ref.shape, jnp.bfloat16)
        v_rows = HEADS * VHEAD
        for i, w in enumerate((w_mut, w_slf)):
            w = w[layer]
            w_k[:C, i * LANES : (i + 1) * LANES] = matmul_nt(w, pick_k).astype(jnp.bfloat16)
            w_qv[i * LANES : (i + 1) * LANES, :C] = matmul_nt(pick_q, w).astype(jnp.bfloat16)
            low = 2 * LANES + i * v_rows
            w_qv[low : low + v_rows, :C] = matmul_nt(pick_v, w).astype(jnp.bfloat16)
            part = matmul(spread, w_prj[layer, i * C : (i + 1) * C])
            w_p[i * v_rows : (i + 1) * v_rows, :C] = part.astype(jnp.bfloat16)
        w_gu[:C, :FFN] = w_gte[layer]
        w_gu[:C, 2 * LANES : 2 * LANES + FFN] = w_upp[layer]
        w_d[:FFN, :C] = w_dwn[layer]


def prepared(*weights):
    v_rows = HEADS * VHEAD
    shapes = [
        (LANES, 2 * LANES),
        (2 * LANES + 2 * v_rows, LANES),
        (2 * v_rows, LANES),
        (LANES, 4 * LANES),
        (2 * LANES, LANES),
    ] * 2
    return pl.pallas_call(
        prepare_kernel,
        out_shape=[jax.ShapeDtypeStruct(shape, jnp.bfloat16) for shape in shapes],
        in_specs=[VMEM] * len(weights),
        out_specs=[VMEM] * len(shapes),
        compiler_params=PARAMS,
        name="prepare",
    )(*weights)


def on_device(features, *weights):
    frames, strips = lax.axis_size("frame"), lax.axis_size("strip")

    def route(frame_step, strip_step):
        pairs = []
        for f in range(frames):
            for s in range(strips):
                to = (f + frame_step * (1 - 2 * (f % 2))) % frames
                pairs.append((f * strips + s, to * strips + (s + strip_step) % strips))
        return pairs

    def send(value, frame_step, strip_step):
        return lax.ppermute(value, ("frame", "strip"), route(frame_step, strip_step))

    h = (lax.axis_index("frame") % 2).astype(jnp.int32).reshape(1)
    ready = prepared(*weights)
    w_one, w_two = ready[:5], ready[5:]
    parts = to_tokens(h, features[0])
    chunks = range(len(WINDOWS))
    others = [send(parts[k], 1, 0) for k in chunks]
    edge = ()
    pieces = []
    for k in chunks:
        own_up, own_lo, oth_up, oth_lo, *edge = layer_one(
            k, parts[len(WINDOWS) + k], others[k], edge, w_one
        )
        oth_lo = send(oth_lo, 2, 0)
        oth_up = send(oth_up, 2, -1)
        own_up = send(own_up, 0, -1)
        pieces.append((own_lo, own_up, oth_lo, oth_up))
    home = []
    for k in chunks:
        own_lo, own_up, oth_lo, oth_up = layer_two(k, pieces[k], w_two)
        oth_lo = send(oth_lo, -1, 0)
        oth_up = send(oth_up, -1, 1)
        own_up = send(own_up, 0, 1)
        home += [own_lo, own_up, oth_lo, oth_up]
    return from_tokens(h, home)[None]


def solution(mesh):
    in_specs = (P("frame", None, "strip", None), P(), P(), P(), P(), P(), P())
    out_specs = P("frame", None, "strip", None)
    return jax.shard_map(
        on_device, mesh=mesh, in_specs=in_specs, out_specs=out_specs, check_vma=False
    )
```

```python
import functools

import jax
import jax.numpy as jnp
import numpy as np
from jax import lax
from jax.experimental import pallas as pl
from jax.experimental.pallas import tpu as pltpu
from jax.sharding import PartitionSpec as P

C = 120
HEADS = 6
HEAD = 20
FFN = 240
WIN = 8
LANES = 128
VHEAD = 24
HALF = 16
GROUP = 8
TOK = WIN * WIN
EPS = 1e-05
SHIFTED = ((0, 16),)
WINDOWS = ((0, 17),)
EXP2_SCALE = float(np.log2(np.e) * HEAD**-0.5)
VMEM_LIMIT = 56 * 1024 * 1024


def matmul(a, b):
    return lax.dot_general(a, b, (((1,), (0,)), ((), ())), preferred_element_type=jnp.float32)


def matmul_nt(a, b):
    return lax.dot_general(a, b, (((1,), (1,)), ((), ())), preferred_element_type=jnp.float32)


def matmul_tn(a, b):
    return lax.dot_general(a, b, (((0,), (0,)), ((), ())), preferred_element_type=jnp.float32)


def normed(x):
    lane = lax.broadcasted_iota(jnp.int32, x.shape, 1)
    mean = jnp.sum(x, axis=1, keepdims=True) * (1.0 / C)
    centred = jnp.where(lane < C, x - mean, 0.0)
    spread = jnp.sum(centred * centred, axis=1, keepdims=True) * (1.0 / C)
    return (centred * lax.rsqrt(spread + EPS)).astype(jnp.bfloat16)


def head_only(q_t, head):
    low = head * HEAD // 16 * 16
    high = -(-(head * HEAD + HEAD) // 16) * 16
    part = q_t[low:high].astype(jnp.float32)
    row = lax.broadcasted_iota(jnp.int32, part.shape, 0) + low
    keep = (row >= head * HEAD) & (row < head * HEAD + HEAD)
    part = jnp.where(keep, part, 0.0).astype(jnp.bfloat16)
    pieces = [part]
    if low:
        pieces.insert(0, jnp.zeros((low, q_t.shape[1]), jnp.bfloat16))
    if high < LANES:
        pieces.append(jnp.zeros((LANES - high, q_t.shape[1]), jnp.bfloat16))
    return jnp.concatenate(pieces, axis=0)


def softmax_rows(scores):
    top = jnp.max(scores, axis=0, keepdims=True)
    weights = jnp.exp2((scores - top) * EXP2_SCALE)
    total = jnp.sum(weights, axis=0, keepdims=True)
    return weights * (1.0 / total)


def project_windows(x, w_k, w_qv, keys, qv_t, first):
    normal = normed(x)
    new_keys = matmul(normal, w_k[...]).astype(jnp.bfloat16)
    new_qv = matmul_nt(w_qv[...], normal).astype(jnp.bfloat16)
    for i in range(x.shape[0] // LANES):
        span = slice(i * LANES, (i + 1) * LANES)
        keys[first + i] = new_keys[span]
        qv_t[first + i] = new_qv[:, span]


def score_block(kind, pair, keys, qv_t, window, of_first):
    kind_q = qv_t[window, kind * LANES : (kind + 1) * LANES]
    queries = jnp.concatenate(
        [head_only(kind_q, 2 * pair), head_only(kind_q, 2 * pair + 1)], axis=1
    )
    scores = matmul(keys[window, :, kind * LANES : (kind + 1) * LANES], queries)
    if kind == 0:
        scores = jnp.where(of_first, scores[TOK:], scores[:TOK])
    return scores


def mix_block(kind, pair, scores, qv_t, window, of_first):
    probs = [softmax_rows(scores[:, i * LANES : (i + 1) * LANES]) for i in range(2)]
    probs = jnp.concatenate(probs, axis=1)
    if kind == 0:
        probs = jnp.concatenate(
            [jnp.where(of_first, 0.0, probs), jnp.where(of_first, probs, 0.0)], axis=0
        )
    base = 2 * LANES + (kind * HEADS + 2 * pair) * VHEAD
    mixed = matmul(qv_t[window, base : base + 2 * VHEAD], probs.astype(jnp.bfloat16))
    return [mixed[:VHEAD, :LANES], mixed[VHEAD:, LANES:]]


def attend(count, keys, qv_t, mutual_scores, self_scores, joined):
    scores = (mutual_scores, self_scores)
    lane = lax.broadcasted_iota(jnp.int32, (TOK, 2 * LANES), 1)
    of_first = (lane % LANES) < TOK
    blocks = [(kind, pair) for kind in range(2) for pair in range(HEADS // 2)]
    for kind, pair in blocks:
        scores[kind][0, pair] = score_block(kind, pair, keys, qv_t, 0, of_first)
    for i in range(count):
        outs = []
        for kind, pair in blocks:
            ref = scores[kind]
            if i + 1 < count:
                ref[(i + 1) % 2, pair] = score_block(kind, pair, keys, qv_t, i + 1, of_first)
            outs += mix_block(kind, pair, ref[i % 2, pair], qv_t, i, of_first)
        joined[i] = jnp.concatenate(outs, axis=0).astype(jnp.bfloat16)


def finished(x, joined, w_prj, w_gu, w_dwn):
    mixed = [matmul_tn(block, w_prj[...]) for block in joined]
    middle = x + jnp.concatenate(mixed, axis=0)
    both = matmul(normed(middle), w_gu[...])
    gate, up = both[:, : 2 * LANES], both[:, 2 * LANES :]
    gelu = 0.5 * gate * (1.0 + lax.erf(gate * float(np.sqrt(0.5))))
    hidden = (gelu * up).astype(jnp.bfloat16)
    return middle + matmul(hidden, w_dwn[...])


def to_tokens_kernel(h_ref, x_ref, *rest):
    outs, (wide, tiles) = rest[:-2], rest[-2:]
    h = h_ref[0]
    for half in range(2):
        part = x_ref[:, :, half * LANES : (half + 1) * LANES].astype(jnp.float32)
        wide[half] = part.reshape(C * WIN, LANES)
    pad = jnp.zeros((LANES - C, LANES), jnp.float32)
    for k in range(2):
        half = 1 - h if k == 0 else h
        for r in range(WIN):
            block = wide.at[half][pl.ds(r, C, stride=WIN), :]
            block = jnp.concatenate([block, pad], axis=0).T
            tiles[k, :HALF, r] = block.reshape(HALF, WIN, LANES)
    for k in range(2):
        tiles[k, HALF] = tiles[1 - k, 0]
    for k in range(2):
        for j, (low, high) in enumerate(WINDOWS):
            part = tiles[k, low:high].reshape((high - low) * TOK, LANES)
            outs[k * len(WINDOWS) + j][...] = part.astype(jnp.bfloat16)


def grouped(count):
    parts = max(1, count // GROUP)
    cuts = [count * i // parts for i in range(parts + 1)]
    return [range(low, high) for low, high in zip(cuts[:-1], cuts[1:])]


def layer_one_kernel(count, first, last, own_ref, oth_ref, *rest):
    if not first:
        before, rest = rest[0], rest[1:]
    w_k, w_qv, w_prj, w_gu, w_dwn = rest[:5]
    outs, rest = rest[5:9], rest[9:]
    if not last:
        after, rest = rest[0], rest[1:]
    flat, tiles, *scratch = rest
    keys, qv_t, joined = scratch[0], scratch[1], scratch[-1]
    shift = 0 if first else WIN

    def tokens(group):
        parts = []
        for i in group:
            span = slice(i * TOK, (i + 1) * TOK)
            parts += [own_ref[span], oth_ref[span]]
        return jnp.concatenate(parts, axis=0).astype(jnp.float32)

    for group in grouped(count):
        project_windows(tokens(group), w_k, w_qv, keys, qv_t, group[0])
    attend(count, *scratch)
    if not first:
        flat[:, :, :WIN, :] = before[...]
    for group in grouped(count):
        y = finished(tokens(group), [joined[i] for i in group], w_prj, w_gu, w_dwn)
        y = y.reshape(len(group), 2, WIN, WIN, LANES)
        for j, i in enumerate(group):
            for f in range(2):
                flat[f, :, shift + i * WIN : shift + (i + 1) * WIN, :] = y[j, f]
    width = shift + (count - 1) * WIN
    if not last:
        after[...] = flat[:, :, width : width + WIN, :]
    for f in range(2):
        for r in range(WIN):
            block = flat[f, r, WIN // 2 : WIN // 2 + width, :]
            tiles[f, r // 4, :, r % 4] = block.reshape(width // WIN, WIN, LANES)
        for k in range(2):
            piece = tiles[f, k].reshape(width * 4, LANES)
            outs[2 * f + k][...] = piece.astype(jnp.bfloat16)


def layer_two_kernel(count, *rest):
    ins, rest = rest[:4], rest[4:]
    w_k, w_qv, w_prj, w_gu, w_dwn = rest[:5]
    outs, scratch = rest[5:9], rest[9:]
    keys, qv_t, joined = scratch[0], scratch[1], scratch[-1]
    half_tok = TOK // 2
    spans = [slice(i * half_tok, (i + 1) * half_tok) for i in range(count)]

    def tokens(group):
        parts = [ref[spans[i]] for i in group for ref in ins]
        return jnp.concatenate(parts, axis=0).astype(jnp.float32)

    for group in grouped(count):
        project_windows(tokens(group), w_k, w_qv, keys, qv_t, group[0])
    attend(count, *scratch)
    for group in grouped(count):
        y = finished(tokens(group), [joined[i] for i in group], w_prj, w_gu, w_dwn)
        y = y.astype(jnp.bfloat16)
        for k, i in enumerate(group):
            for j in range(4):
                low = k * LANES + j * half_tok
                outs[j][spans[i]] = y[low : low + half_tok]


def from_tokens_kernel(h_ref, *rest):
    ins, (out_ref, tiles, wide) = rest[:-3], rest[-3:]
    h = h_ref[0]
    for k, (low, high) in enumerate(SHIFTED):
        for j in range(4):
            half = 1 - h if j < 2 else h
            part = ins[4 * k + j][...].astype(jnp.float32)
            tiles[half, 1 - j % 2, low:high] = part.reshape(high - low, 4, WIN, LANES)
    for r in range(WIN):
        lo = 0 if r >= 4 else 1
        row = [tiles[half, lo, :, r % 4].reshape(LANES, LANES).T for half in range(2)]
        row = pltpu.roll(jnp.concatenate(row, axis=1), WIN // 2, 1)
        for half in range(2):
            part = row[:C, half * LANES : (half + 1) * LANES]
            wide.at[half][pl.ds(r, C, stride=WIN), :] = part
    for half in range(2):
        part = wide[half].reshape(C, WIN, LANES).astype(jnp.bfloat16)
        out_ref[:, :, half * LANES : (half + 1) * LANES] = part


VMEM = pl.BlockSpec(memory_space=pltpu.VMEM)
SMEM = pl.BlockSpec(memory_space=pltpu.SMEM)
COST = pl.CostEstimate(flops=8 * 10**9, bytes_accessed=2**20, transcendentals=2**20)
PARAMS = pltpu.CompilerParams(vmem_limit_bytes=VMEM_LIMIT)


def attention_scratch(count):
    return [
        pltpu.VMEM((count, LANES, 2 * LANES), jnp.bfloat16),
        pltpu.VMEM((count, 2 * LANES + 2 * HEADS * VHEAD, LANES), jnp.bfloat16),
        pltpu.VMEM((2, HEADS // 2, TOK, 2 * LANES), jnp.float32),
        pltpu.VMEM((2, HEADS // 2, 2 * TOK, 2 * LANES), jnp.float32),
        pltpu.VMEM((count, 2 * HEADS * VHEAD, LANES), jnp.bfloat16),
    ]


def tokens_shape(rows):
    return jax.ShapeDtypeStruct((rows, LANES), jnp.bfloat16)


def to_tokens(h, x):
    shapes = [tokens_shape((high - low) * TOK) for low, high in WINDOWS]
    return pl.pallas_call(
        to_tokens_kernel,
        out_shape=shapes * 2,
        in_specs=[SMEM, VMEM],
        out_specs=[VMEM] * (2 * len(shapes)),
        scratch_shapes=[
            pltpu.VMEM((2, C * WIN, LANES), jnp.float32),
            pltpu.VMEM((2, HALF + 1, WIN, WIN, LANES), jnp.float32),
        ],
        compiler_params=PARAMS,
        name="to_tokens",
    )(h, x)


def layer_one(chunk, own, oth, before, weights):
    first, last = chunk == 0, chunk == len(WINDOWS) - 1
    count = WINDOWS[chunk][1] - WINDOWS[chunk][0]
    width = SHIFTED[chunk][1] - SHIFTED[chunk][0]
    edge = [] if last else [jax.ShapeDtypeStruct((2, WIN, WIN, LANES), jnp.float32)]
    shapes = [tokens_shape(width * TOK // 2)] * 4 + edge
    args = (own, oth, *before, *weights)
    return pl.pallas_call(
        functools.partial(layer_one_kernel, count, first, last),
        out_shape=shapes,
        in_specs=[VMEM] * len(args),
        out_specs=[VMEM] * len(shapes),
        scratch_shapes=[
            pltpu.VMEM((2, WIN, (width + 1) * WIN, LANES), jnp.float32),
            pltpu.VMEM((2, 2, width, 4, WIN, LANES), jnp.float32),
            *attention_scratch(count),
        ],
        compiler_params=PARAMS,
        cost_estimate=COST,
        name="layer_one",
    )(*args)


def layer_two(chunk, pieces, weights):
    count = SHIFTED[chunk][1] - SHIFTED[chunk][0]
    return pl.pallas_call(
        functools.partial(layer_two_kernel, count),
        out_shape=[tokens_shape(count * TOK // 2)] * 4,
        in_specs=[VMEM] * 9,
        out_specs=[VMEM] * 4,
        scratch_shapes=attention_scratch(count),
        compiler_params=PARAMS,
        cost_estimate=COST,
        name="layer_two",
    )(*pieces, *weights)


def from_tokens(h, pieces):
    return pl.pallas_call(
        from_tokens_kernel,
        out_shape=jax.ShapeDtypeStruct((C, WIN, 2 * LANES), jnp.bfloat16),
        in_specs=[SMEM] + [VMEM] * len(pieces),
        out_specs=VMEM,
        scratch_shapes=[
            pltpu.VMEM((2, 2, HALF, 4, WIN, LANES), jnp.float32),
            pltpu.VMEM((2, C * WIN, LANES), jnp.float32),
        ],
        compiler_params=PARAMS,
        name="from_tokens",
    )(h, *pieces)


def prepare_kernel(w_mut, w_slf, w_prj, w_gte, w_upp, w_dwn, *outs):
    def selector(rows, cols, picks):
        row = lax.broadcasted_iota(jnp.int32, (rows, cols), 0)
        col = lax.broadcasted_iota(jnp.int32, (rows, cols), 1)
        hit = None
        for first_row, first_col, size in picks:
            inside = (row >= first_row) & (row < first_row + size)
            run = inside & (col - first_col == row - first_row)
            hit = run if hit is None else hit | run
        return jnp.where(hit, 1.0, 0.0).astype(jnp.bfloat16)

    by_head = [(h * VHEAD, h * HEAD, HEAD) for h in range(HEADS)]
    pick_q = selector(LANES, 3 * C, [(0, 0, C)])
    pick_v = selector(HEADS * VHEAD, 3 * C, [(r, 2 * C + c, n) for r, c, n in by_head])
    pick_k = selector(LANES, 3 * C, [(0, C, C)])
    spread = selector(HEADS * VHEAD, C, by_head)
    for layer in range(2):
        w_k, w_qv, w_p, w_gu, w_d = outs[5 * layer : 5 * layer + 5]
        for ref in (w_k, w_qv, w_p, w_gu, w_d):
            ref[...] = jnp.zeros(ref.shape, jnp.bfloat16)
        v_rows = HEADS * VHEAD
        for i, w in enumerate((w_mut, w_slf)):
            w = w[layer]
            w_k[:C, i * LANES : (i + 1) * LANES] = matmul_nt(w, pick_k).astype(jnp.bfloat16)
            w_qv[i * LANES : (i + 1) * LANES, :C] = matmul_nt(pick_q, w).astype(jnp.bfloat16)
            low = 2 * LANES + i * v_rows
            w_qv[low : low + v_rows, :C] = matmul_nt(pick_v, w).astype(jnp.bfloat16)
            part = matmul(spread, w_prj[layer, i * C : (i + 1) * C])
            w_p[i * v_rows : (i + 1) * v_rows, :C] = part.astype(jnp.bfloat16)
        w_gu[:C, :FFN] = w_gte[layer]
        w_gu[:C, 2 * LANES : 2 * LANES + FFN] = w_upp[layer]
        w_d[:FFN, :C] = w_dwn[layer]


def prepared(*weights):
    v_rows = HEADS * VHEAD
    shapes = [
        (LANES, 2 * LANES),
        (2 * LANES + 2 * v_rows, LANES),
        (2 * v_rows, LANES),
        (LANES, 4 * LANES),
        (2 * LANES, LANES),
    ] * 2
    return pl.pallas_call(
        prepare_kernel,
        out_shape=[jax.ShapeDtypeStruct(shape, jnp.bfloat16) for shape in shapes],
        in_specs=[VMEM] * len(weights),
        out_specs=[VMEM] * len(shapes),
        compiler_params=PARAMS,
        name="prepare",
    )(*weights)


def on_device(features, *weights):
    frames, strips = lax.axis_size("frame"), lax.axis_size("strip")

    def route(frame_step, strip_step):
        pairs = []
        for f in range(frames):
            for s in range(strips):
                to = (f + frame_step * (1 - 2 * (f % 2))) % frames
                pairs.append((f * strips + s, to * strips + (s + strip_step) % strips))
        return pairs

    def send(value, frame_step, strip_step):
        return lax.ppermute(value, ("frame", "strip"), route(frame_step, strip_step))

    h = (lax.axis_index("frame") % 2).astype(jnp.int32).reshape(1)
    ready = prepared(*weights)
    w_one, w_two = ready[:5], ready[5:]
    parts = to_tokens(h, features[0])
    chunks = range(len(WINDOWS))
    others = [send(parts[k], 1, 0) for k in chunks]
    edge = ()
    pieces = []
    for k in chunks:
        own_up, own_lo, oth_up, oth_lo, *edge = layer_one(
            k, parts[len(WINDOWS) + k], others[k], edge, w_one
        )
        oth_up = send(oth_up, 2, -1)
        oth_lo = send(oth_lo, 2, 0)
        own_up = send(own_up, 0, -1)
        pieces.append((oth_up, oth_lo, own_up, own_lo))
    home = []
    for k in chunks:
        oth_up, oth_lo, own_up, own_lo = layer_two(k, pieces[k], w_two)
        oth_up = send(oth_up, -1, 1)
        oth_lo = send(oth_lo, -1, 0)
        own_up = send(own_up, 0, 1)
        home += [oth_up, oth_lo, own_up, own_lo]
    return from_tokens(h, home)[None]


def solution(mesh):
    in_specs = (P("frame", None, "strip", None), P(), P(), P(), P(), P(), P())
    out_specs = P("frame", None, "strip", None)
    return jax.shard_map(
        on_device, mesh=mesh, in_specs=in_specs, out_specs=out_specs, check_vma=False
    )
```

```python
import functools

import jax
import jax.numpy as jnp
import numpy as np
from jax import lax
from jax.experimental import pallas as pl
from jax.experimental.pallas import tpu as pltpu
from jax.sharding import PartitionSpec as P

C = 120
HEADS = 6
HEAD = 20
FFN = 240
WIN = 8
LANES = 128
VHEAD = 24
HALF = 16
GROUP = 8
TOK = WIN * WIN
EPS = 1e-05
SHIFTED = ((0, 16),)
WINDOWS = ((0, 17),)
EXP2_SCALE = float(np.log2(np.e) * HEAD**-0.5)
VMEM_LIMIT = 56 * 1024 * 1024


def matmul(a, b):
    return lax.dot_general(a, b, (((1,), (0,)), ((), ())), preferred_element_type=jnp.float32)


def matmul_nt(a, b):
    return lax.dot_general(a, b, (((1,), (1,)), ((), ())), preferred_element_type=jnp.float32)


def matmul_tn(a, b):
    return lax.dot_general(a, b, (((0,), (0,)), ((), ())), preferred_element_type=jnp.float32)


def normed(x):
    lane = lax.broadcasted_iota(jnp.int32, x.shape, 1)
    mean = jnp.sum(x, axis=1, keepdims=True) * (1.0 / C)
    centred = jnp.where(lane < C, x - mean, 0.0)
    spread = jnp.sum(centred * centred, axis=1, keepdims=True) * (1.0 / C)
    return (centred * lax.rsqrt(spread + EPS)).astype(jnp.bfloat16)


def head_only(q_t, head):
    low = head * HEAD // 16 * 16
    high = -(-(head * HEAD + HEAD) // 16) * 16
    part = q_t[low:high].astype(jnp.float32)
    row = lax.broadcasted_iota(jnp.int32, part.shape, 0) + low
    keep = (row >= head * HEAD) & (row < head * HEAD + HEAD)
    part = jnp.where(keep, part, 0.0).astype(jnp.bfloat16)
    pieces = [part]
    if low:
        pieces.insert(0, jnp.zeros((low, q_t.shape[1]), jnp.bfloat16))
    if high < LANES:
        pieces.append(jnp.zeros((LANES - high, q_t.shape[1]), jnp.bfloat16))
    return jnp.concatenate(pieces, axis=0)


def softmax_rows(scores):
    top = jnp.max(scores, axis=0, keepdims=True)
    weights = jnp.exp2((scores - top) * EXP2_SCALE)
    total = jnp.sum(weights, axis=0, keepdims=True)
    return weights * (1.0 / total)


def project_windows(x, w_k, w_qv, keys, qv_t, first):
    normal = normed(x)
    new_keys = matmul(normal, w_k[...]).astype(jnp.bfloat16)
    new_qv = matmul_nt(w_qv[...], normal).astype(jnp.bfloat16)
    for i in range(x.shape[0] // LANES):
        span = slice(i * LANES, (i + 1) * LANES)
        keys[first + i] = new_keys[span]
        qv_t[first + i] = new_qv[:, span]


def score_block(kind, pair, keys, qv_t, window, of_first):
    kind_q = qv_t[window, kind * LANES : (kind + 1) * LANES]
    queries = jnp.concatenate(
        [head_only(kind_q, 2 * pair), head_only(kind_q, 2 * pair + 1)], axis=1
    )
    scores = matmul(keys[window, :, kind * LANES : (kind + 1) * LANES], queries)
    if kind == 0:
        scores = jnp.where(of_first, scores[TOK:], scores[:TOK])
    return scores


def mix_block(kind, pair, scores, qv_t, window, of_first):
    probs = [softmax_rows(scores[:, i * LANES : (i + 1) * LANES]) for i in range(2)]
    probs = jnp.concatenate(probs, axis=1)
    if kind == 0:
        probs = jnp.concatenate(
            [jnp.where(of_first, 0.0, probs), jnp.where(of_first, probs, 0.0)], axis=0
        )
    base = 2 * LANES + (kind * HEADS + 2 * pair) * VHEAD
    mixed = matmul(qv_t[window, base : base + 2 * VHEAD], probs.astype(jnp.bfloat16))
    return [mixed[:VHEAD, :LANES], mixed[VHEAD:, LANES:]]


def attend(count, keys, qv_t, mutual_scores, self_scores, joined):
    scores = (mutual_scores, self_scores)
    lane = lax.broadcasted_iota(jnp.int32, (TOK, 2 * LANES), 1)
    of_first = (lane % LANES) < TOK
    blocks = [(kind, pair) for kind in range(2) for pair in range(HEADS // 2)]
    for kind, pair in blocks:
        scores[kind][0, pair] = score_block(kind, pair, keys, qv_t, 0, of_first)
    for i in range(count):
        outs = []
        for kind, pair in blocks:
            ref = scores[kind]
            if i + 1 < count:
                ref[(i + 1) % 2, pair] = score_block(kind, pair, keys, qv_t, i + 1, of_first)
            outs += mix_block(kind, pair, ref[i % 2, pair], qv_t, i, of_first)
        joined[i] = jnp.concatenate(outs, axis=0).astype(jnp.bfloat16)


def finished(x, joined, w_prj, w_gu, w_dwn):
    mixed = [matmul_tn(block, w_prj[...]) for block in joined]
    middle = x + jnp.concatenate(mixed, axis=0)
    both = matmul(normed(middle), w_gu[...])
    gate, up = both[:, : 2 * LANES], both[:, 2 * LANES :]
    gelu = 0.5 * gate * (1.0 + lax.erf(gate * float(np.sqrt(0.5))))
    hidden = (gelu * up).astype(jnp.bfloat16)
    return middle + matmul(hidden, w_dwn[...])


def to_tokens_kernel(h_ref, x_ref, *rest):
    outs, (wide, tiles) = rest[:-2], rest[-2:]
    h = h_ref[0]
    for half in range(2):
        part = x_ref[:, :, half * LANES : (half + 1) * LANES].astype(jnp.float32)
        wide[half] = part.reshape(C * WIN, LANES)
    pad = jnp.zeros((LANES - C, LANES), jnp.float32)
    for k in range(2):
        half = 1 - h if k == 0 else h
        for r in range(WIN):
            block = wide.at[half][pl.ds(r, C, stride=WIN), :]
            block = jnp.concatenate([block, pad], axis=0).T
            tiles[k, :HALF, r] = block.reshape(HALF, WIN, LANES)
    for k in range(2):
        tiles[k, HALF] = tiles[1 - k, 0]
    for k in range(2):
        for j, (low, high) in enumerate(WINDOWS):
            part = tiles[k, low:high].reshape((high - low) * TOK, LANES)
            outs[k * len(WINDOWS) + j][...] = part.astype(jnp.bfloat16)


def grouped(count):
    parts = max(1, count // GROUP)
    cuts = [count * i // parts for i in range(parts + 1)]
    return [range(low, high) for low, high in zip(cuts[:-1], cuts[1:])]


def layer_one_kernel(count, first, last, own_ref, oth_ref, *rest):
    if not first:
        before, rest = rest[0], rest[1:]
    w_k, w_qv, w_prj, w_gu, w_dwn = rest[:5]
    outs, rest = rest[5:9], rest[9:]
    if not last:
        after, rest = rest[0], rest[1:]
    flat, tiles, *scratch = rest
    keys, qv_t, joined = scratch[0], scratch[1], scratch[-1]
    shift = 0 if first else WIN

    def tokens(group):
        parts = []
        for i in group:
            span = slice(i * TOK, (i + 1) * TOK)
            parts += [own_ref[span], oth_ref[span]]
        return jnp.concatenate(parts, axis=0).astype(jnp.float32)

    for group in grouped(count):
        project_windows(tokens(group), w_k, w_qv, keys, qv_t, group[0])
    attend(count, *scratch)
    if not first:
        flat[:, :, :WIN, :] = before[...]
    for group in grouped(count):
        y = finished(tokens(group), [joined[i] for i in group], w_prj, w_gu, w_dwn)
        y = y.reshape(len(group), 2, WIN, WIN, LANES)
        for j, i in enumerate(group):
            for f in range(2):
                flat[f, :, shift + i * WIN : shift + (i + 1) * WIN, :] = y[j, f]
    width = shift + (count - 1) * WIN
    if not last:
        after[...] = flat[:, :, width : width + WIN, :]
    for f in range(2):
        for r in range(WIN):
            block = flat[f, r, WIN // 2 : WIN // 2 + width, :]
            tiles[f, r // 4, :, r % 4] = block.reshape(width // WIN, WIN, LANES)
        for k in range(2):
            piece = tiles[f, k].reshape(width * 4, LANES)
            outs[2 * f + k][...] = piece.astype(jnp.bfloat16)


def layer_two_kernel(count, *rest):
    ins, rest = rest[:4], rest[4:]
    w_k, w_qv, w_prj, w_gu, w_dwn = rest[:5]
    outs, scratch = rest[5:11], rest[11:]
    keys, qv_t, joined = scratch[0], scratch[1], scratch[-1]
    half_tok = TOK // 2
    spans = [slice(i * half_tok, (i + 1) * half_tok) for i in range(count)]

    def tokens(group):
        parts = [ref[spans[i]] for i in group for ref in ins]
        return jnp.concatenate(parts, axis=0).astype(jnp.float32)

    for group in grouped(count):
        project_windows(tokens(group), w_k, w_qv, keys, qv_t, group[0])
    attend(count, *scratch)
    for group in grouped(count):
        y = finished(tokens(group), [joined[i] for i in group], w_prj, w_gu, w_dwn)
        y = y.astype(jnp.bfloat16)
        for k, i in enumerate(group):
            for j, ref in enumerate(outs):
                low = k * LANES + (j % 2 if j < 4 else j - 2) * half_tok
                ref[spans[i]] = y[low : low + half_tok]


def from_tokens_kernel(h_ref, *rest):
    ins, (out_ref, tiles, wide) = rest[:-3], rest[-3:]
    h = h_ref[0]
    for k, (low, high) in enumerate(SHIFTED):

        def place(j, half):
            part = ins[6 * k + j][...].astype(jnp.float32)
            tiles[half, 1 - j % 2, low:high] = part.reshape(high - low, 4, WIN, LANES)

        for side in range(2):

            @pl.when(h == side)
            def _():
                place(2 * side, 1 - side)
                place(2 * side + 1, 1 - side)

        place(4, h)
        place(5, h)
    for r in range(WIN):
        lo = 0 if r >= 4 else 1
        row = [tiles[half, lo, :, r % 4].reshape(LANES, LANES).T for half in range(2)]
        row = pltpu.roll(jnp.concatenate(row, axis=1), WIN // 2, 1)
        for half in range(2):
            part = row[:C, half * LANES : (half + 1) * LANES]
            wide.at[half][pl.ds(r, C, stride=WIN), :] = part
    for half in range(2):
        part = wide[half].reshape(C, WIN, LANES).astype(jnp.bfloat16)
        out_ref[:, :, half * LANES : (half + 1) * LANES] = part


VMEM = pl.BlockSpec(memory_space=pltpu.VMEM)
SMEM = pl.BlockSpec(memory_space=pltpu.SMEM)
COST = pl.CostEstimate(flops=8 * 10**9, bytes_accessed=2**20, transcendentals=2**20)
PARAMS = pltpu.CompilerParams(vmem_limit_bytes=VMEM_LIMIT)


def attention_scratch(count):
    return [
        pltpu.VMEM((count, LANES, 2 * LANES), jnp.bfloat16),
        pltpu.VMEM((count, 2 * LANES + 2 * HEADS * VHEAD, LANES), jnp.bfloat16),
        pltpu.VMEM((2, HEADS // 2, TOK, 2 * LANES), jnp.float32),
        pltpu.VMEM((2, HEADS // 2, 2 * TOK, 2 * LANES), jnp.float32),
        pltpu.VMEM((count, 2 * HEADS * VHEAD, LANES), jnp.bfloat16),
    ]


def tokens_shape(rows):
    return jax.ShapeDtypeStruct((rows, LANES), jnp.bfloat16)


def to_tokens(h, x):
    shapes = [tokens_shape((high - low) * TOK) for low, high in WINDOWS]
    return pl.pallas_call(
        to_tokens_kernel,
        out_shape=shapes * 2,
        in_specs=[SMEM, VMEM],
        out_specs=[VMEM] * (2 * len(shapes)),
        scratch_shapes=[
            pltpu.VMEM((2, C * WIN, LANES), jnp.float32),
            pltpu.VMEM((2, HALF + 1, WIN, WIN, LANES), jnp.float32),
        ],
        compiler_params=PARAMS,
        name="to_tokens",
    )(h, x)


def layer_one(chunk, own, oth, before, weights):
    first, last = chunk == 0, chunk == len(WINDOWS) - 1
    count = WINDOWS[chunk][1] - WINDOWS[chunk][0]
    width = SHIFTED[chunk][1] - SHIFTED[chunk][0]
    edge = [] if last else [jax.ShapeDtypeStruct((2, WIN, WIN, LANES), jnp.float32)]
    shapes = [tokens_shape(width * TOK // 2)] * 4 + edge
    args = (own, oth, *before, *weights)
    return pl.pallas_call(
        functools.partial(layer_one_kernel, count, first, last),
        out_shape=shapes,
        in_specs=[VMEM] * len(args),
        out_specs=[VMEM] * len(shapes),
        scratch_shapes=[
            pltpu.VMEM((2, WIN, (width + 1) * WIN, LANES), jnp.float32),
            pltpu.VMEM((2, 2, width, 4, WIN, LANES), jnp.float32),
            *attention_scratch(count),
        ],
        compiler_params=PARAMS,
        cost_estimate=COST,
        name="layer_one",
    )(*args)


def layer_two(chunk, pieces, weights):
    count = SHIFTED[chunk][1] - SHIFTED[chunk][0]
    return pl.pallas_call(
        functools.partial(layer_two_kernel, count),
        out_shape=[tokens_shape(count * TOK // 2)] * 6,
        in_specs=[VMEM] * 9,
        out_specs=[VMEM] * 6,
        scratch_shapes=attention_scratch(count),
        compiler_params=PARAMS,
        cost_estimate=COST,
        name="layer_two",
    )(*pieces, *weights)


def from_tokens(h, pieces):
    return pl.pallas_call(
        from_tokens_kernel,
        out_shape=jax.ShapeDtypeStruct((C, WIN, 2 * LANES), jnp.bfloat16),
        in_specs=[SMEM] + [VMEM] * len(pieces),
        out_specs=VMEM,
        scratch_shapes=[
            pltpu.VMEM((2, 2, HALF, 4, WIN, LANES), jnp.float32),
            pltpu.VMEM((2, C * WIN, LANES), jnp.float32),
        ],
        compiler_params=PARAMS,
        name="from_tokens",
    )(h, *pieces)


def prepare_kernel(w_mut, w_slf, w_prj, w_gte, w_upp, w_dwn, *outs):
    def selector(rows, cols, picks):
        row = lax.broadcasted_iota(jnp.int32, (rows, cols), 0)
        col = lax.broadcasted_iota(jnp.int32, (rows, cols), 1)
        hit = None
        for first_row, first_col, size in picks:
            inside = (row >= first_row) & (row < first_row + size)
            run = inside & (col - first_col == row - first_row)
            hit = run if hit is None else hit | run
        return jnp.where(hit, 1.0, 0.0).astype(jnp.bfloat16)

    by_head = [(h * VHEAD, h * HEAD, HEAD) for h in range(HEADS)]
    pick_q = selector(LANES, 3 * C, [(0, 0, C)])
    pick_v = selector(HEADS * VHEAD, 3 * C, [(r, 2 * C + c, n) for r, c, n in by_head])
    pick_k = selector(LANES, 3 * C, [(0, C, C)])
    spread = selector(HEADS * VHEAD, C, by_head)
    for layer in range(2):
        w_k, w_qv, w_p, w_gu, w_d = outs[5 * layer : 5 * layer + 5]
        for ref in (w_k, w_qv, w_p, w_gu, w_d):
            ref[...] = jnp.zeros(ref.shape, jnp.bfloat16)
        v_rows = HEADS * VHEAD
        for i, w in enumerate((w_mut, w_slf)):
            w = w[layer]
            w_k[:C, i * LANES : (i + 1) * LANES] = matmul_nt(w, pick_k).astype(jnp.bfloat16)
            w_qv[i * LANES : (i + 1) * LANES, :C] = matmul_nt(pick_q, w).astype(jnp.bfloat16)
            low = 2 * LANES + i * v_rows
            w_qv[low : low + v_rows, :C] = matmul_nt(pick_v, w).astype(jnp.bfloat16)
            part = matmul(spread, w_prj[layer, i * C : (i + 1) * C])
            w_p[i * v_rows : (i + 1) * v_rows, :C] = part.astype(jnp.bfloat16)
        w_gu[:C, :FFN] = w_gte[layer]
        w_gu[:C, 2 * LANES : 2 * LANES + FFN] = w_upp[layer]
        w_d[:FFN, :C] = w_dwn[layer]


def prepared(*weights):
    v_rows = HEADS * VHEAD
    shapes = [
        (LANES, 2 * LANES),
        (2 * LANES + 2 * v_rows, LANES),
        (2 * v_rows, LANES),
        (LANES, 4 * LANES),
        (2 * LANES, LANES),
    ] * 2
    return pl.pallas_call(
        prepare_kernel,
        out_shape=[jax.ShapeDtypeStruct(shape, jnp.bfloat16) for shape in shapes],
        in_specs=[VMEM] * len(weights),
        out_specs=[VMEM] * len(shapes),
        compiler_params=PARAMS,
        name="prepare",
    )(*weights)


def on_device(features, *weights):
    frames, strips = lax.axis_size("frame"), lax.axis_size("strip")

    def route(frame_step, strip_step, parity):
        pairs = []
        for f in range(frames):
            if parity not in (None, f % 2):
                continue
            for s in range(strips):
                to = (f + frame_step * (1 - 2 * (f % 2))) % frames
                pairs.append((f * strips + s, to * strips + (s + strip_step) % strips))
        return pairs

    def send(value, frame_step, strip_step, parity=None):
        return lax.ppermute(value, ("frame", "strip"), route(frame_step, strip_step, parity))

    h = (lax.axis_index("frame") % 2).astype(jnp.int32).reshape(1)
    ready = prepared(*weights)
    w_one, w_two = ready[:5], ready[5:]
    parts = to_tokens(h, features[0])
    chunks = range(len(WINDOWS))
    others = [send(parts[k], 1, 0) for k in chunks]
    edge = ()
    pieces = []
    for k in chunks:
        own_up, own_lo, oth_up, oth_lo, *edge = layer_one(
            k, parts[len(WINDOWS) + k], others[k], edge, w_one
        )
        oth_up = send(oth_up, 2, -1)
        oth_lo = send(oth_lo, 2, 0)
        own_up = send(own_up, 0, -1)
        pieces.append((oth_up, oth_lo, own_up, own_lo))
    home = []
    for k in chunks:
        *far, own_up, own_lo = layer_two(k, pieces[k], w_two)
        home += [send(far[j], -1, 1 - j % 2, 1 - j // 2) for j in range(4)]
        home += [send(own_up, 0, 1), own_lo]
    return from_tokens(h, home)[None]


def solution(mesh):
    in_specs = (P("frame", None, "strip", None), P(), P(), P(), P(), P(), P())
    out_specs = P("frame", None, "strip", None)
    return jax.shard_map(
        on_device, mesh=mesh, in_specs=in_specs, out_specs=out_specs, check_vma=False
    )
```

```python
import functools

import jax
import jax.numpy as jnp
import numpy as np
from jax import lax
from jax.experimental import pallas as pl
from jax.experimental.pallas import tpu as pltpu
from jax.sharding import PartitionSpec as P

C = 120
HEADS = 6
HEAD = 20
FFN = 240
WIN = 8
LANES = 128
HALF = 16
GROUP = 8
TOK = WIN * WIN
EPS = 1e-05
SHIFTED = ((0, 16),)
WINDOWS = ((0, 17),)
EXP2_SCALE = float(np.log2(np.e) * HEAD**-0.5)
VMEM_LIMIT = 56 * 1024 * 1024


def matmul(a, b):
    return lax.dot_general(a, b, (((1,), (0,)), ((), ())), preferred_element_type=jnp.float32)


def matmul_nt(a, b):
    return lax.dot_general(a, b, (((1,), (1,)), ((), ())), preferred_element_type=jnp.float32)


def matmul_tn(a, b):
    return lax.dot_general(a, b, (((0,), (0,)), ((), ())), preferred_element_type=jnp.float32)


def normed(x):
    lane = lax.broadcasted_iota(jnp.int32, x.shape, 1)
    mean = jnp.sum(x, axis=1, keepdims=True) * (1.0 / C)
    centred = jnp.where(lane < C, x - mean, 0.0)
    spread = jnp.sum(centred * centred, axis=1, keepdims=True) * (1.0 / C)
    return (centred * lax.rsqrt(spread + EPS)).astype(jnp.bfloat16)


def head_only(q_t, head):
    low = head * HEAD // 16 * 16
    high = -(-(head * HEAD + HEAD) // 16) * 16
    row = lax.broadcasted_iota(jnp.int32, (high - low, q_t.shape[1]), 0) + low
    keep = (row >= head * HEAD) & (row < head * HEAD + HEAD)
    pieces = [q_t[low:high] * jnp.where(keep, 1.0, 0.0).astype(jnp.bfloat16)]
    if low:
        pieces.insert(0, jnp.zeros((low, q_t.shape[1]), jnp.bfloat16))
    if high < LANES:
        pieces.append(jnp.zeros((LANES - high, q_t.shape[1]), jnp.bfloat16))
    return jnp.concatenate(pieces, axis=0)


def softmax_rows(scores):
    top = jnp.max(scores, axis=0, keepdims=True)
    weights = jnp.exp2((scores - top) * EXP2_SCALE)
    total = jnp.sum(weights, axis=0, keepdims=True)
    return weights * (1.0 / total)


def project_windows(x, w_k, w_qv, keys, qv_t, first):
    normal = normed(x)
    new_keys = matmul(normal, w_k[...]).astype(jnp.bfloat16)
    new_qv = matmul_nt(w_qv[...], normal).astype(jnp.bfloat16)
    for i in range(x.shape[0] // LANES):
        span = slice(i * LANES, (i + 1) * LANES)
        keys[first + i] = new_keys[span]
        qv_t[first + i] = new_qv[:, span]


def score_block(kind, pair, keys, qv_t, window, of_first):
    kind_q = qv_t[window, kind * LANES : (kind + 1) * LANES]
    queries = jnp.concatenate(
        [head_only(kind_q, 2 * pair), head_only(kind_q, 2 * pair + 1)], axis=1
    )
    scores = matmul(keys[window, :, kind * LANES : (kind + 1) * LANES], queries)
    if kind == 0:
        scores = jnp.where(of_first, scores[TOK:], scores[:TOK])
    return scores


def mix_block(kind, pair, scores, qv_t, window, of_first):
    probs = [softmax_rows(scores[:, i * LANES : (i + 1) * LANES]) for i in range(2)]
    probs = jnp.concatenate(probs, axis=1).astype(jnp.bfloat16)
    if kind == 0:
        first = jnp.where(of_first, 1.0, 0.0).astype(jnp.bfloat16)
        second = jnp.where(of_first, 0.0, 1.0).astype(jnp.bfloat16)
        probs = jnp.concatenate([probs * second, probs * first], axis=0)
    want = pair * 2 * HEAD
    low = want // 16 * 16
    base = (2 + kind) * LANES + low
    mixed = matmul(qv_t[window, base : base + 48], probs)[want - low : want - low + 2 * HEAD]
    one, two = mixed[:, :LANES], mixed[:, LANES:]
    row = lax.broadcasted_iota(jnp.int32, (8, LANES), 0)
    shared = jnp.where(row < HEAD - 16, one[16:24], two[16:24])
    return jnp.concatenate([one[:16], shared, two[24:]], axis=0)


def attend(count, keys, qv_t, mutual_scores, self_scores, joined):
    scores = (mutual_scores, self_scores)
    lane = lax.broadcasted_iota(jnp.int32, (TOK, 2 * LANES), 1)
    of_first = (lane % LANES) < TOK
    blocks = [(kind, pair) for kind in range(2) for pair in range(HEADS // 2)]
    for kind, pair in blocks:
        scores[kind][0, pair] = score_block(kind, pair, keys, qv_t, 0, of_first)
    for i in range(count):
        outs = []
        for kind, pair in blocks:
            ref = scores[kind]
            if i + 1 < count:
                ref[(i + 1) % 2, pair] = score_block(kind, pair, keys, qv_t, i + 1, of_first)
            outs.append(mix_block(kind, pair, ref[i % 2, pair], qv_t, i, of_first))
        joined[i] = jnp.concatenate(outs, axis=0).astype(jnp.bfloat16)


def finished(x, joined, w_prj, w_gu, w_dwn):
    mixed = [matmul_tn(block, w_prj[...]) for block in joined]
    middle = x + jnp.concatenate(mixed, axis=0)
    both = matmul(normed(middle), w_gu[...])
    gate, up = both[:, : 2 * LANES], both[:, 2 * LANES :]
    gelu = 0.5 * gate * (1.0 + lax.erf(gate * float(np.sqrt(0.5))))
    hidden = (gelu * up).astype(jnp.bfloat16)
    return middle + matmul(hidden, w_dwn[...])


def to_tokens_kernel(h_ref, x_ref, *rest):
    outs, (wide, tiles) = rest[:-2], rest[-2:]
    h = h_ref[0]
    for half in range(2):
        part = x_ref[:, :, half * LANES : (half + 1) * LANES].astype(jnp.float32)
        wide[half] = part.reshape(C * WIN, LANES)
    pad = jnp.zeros((LANES - C, LANES), jnp.float32)
    for k in range(2):
        half = 1 - h if k == 0 else h
        for r in range(WIN):
            block = wide.at[half][pl.ds(r, C, stride=WIN), :]
            block = jnp.concatenate([block, pad], axis=0).T
            tiles[k, :HALF, r] = block.reshape(HALF, WIN, LANES)
    for k in range(2):
        tiles[k, HALF] = tiles[1 - k, 0]
    for k in range(2):
        for j, (low, high) in enumerate(WINDOWS):
            part = tiles[k, low:high].reshape((high - low) * TOK, LANES)
            outs[k * len(WINDOWS) + j][...] = part.astype(jnp.bfloat16)


def grouped(count):
    parts = max(1, count // GROUP)
    cuts = [count * i // parts for i in range(parts + 1)]
    return [range(low, high) for low, high in zip(cuts[:-1], cuts[1:])]


def layer_one_kernel(count, first, last, h_ref, own_ref, oth_ref, *rest):
    h = h_ref[0]
    if not first:
        before, rest = rest[0], rest[1:]
    w_k, w_qv, w_prj, w_gu, w_dwn = rest[:5]
    outs, rest = rest[5:9], rest[9:]
    if not last:
        after, rest = rest[0], rest[1:]
    flat, tiles, *scratch = rest
    keys, qv_t, joined = scratch[0], scratch[1], scratch[-1]
    shift = 0 if first else WIN

    def tokens(group):
        parts = []
        for i in group:
            span = slice(i * TOK, (i + 1) * TOK)
            parts += [own_ref[span], oth_ref[span]]
        return jnp.concatenate(parts, axis=0).astype(jnp.float32)

    for group in grouped(count):
        project_windows(tokens(group), w_k, w_qv, keys, qv_t, group[0])
    attend(count, *scratch)
    if not first:
        flat[:, :, :WIN, :] = before[...]
    for group in grouped(count):
        y = finished(tokens(group), [joined[i] for i in group], w_prj, w_gu, w_dwn)
        y = y.reshape(len(group), 2, WIN, WIN, LANES)
        for j, i in enumerate(group):
            for f in range(2):
                flat[1 - h if f else h, :, shift + i * WIN : shift + (i + 1) * WIN, :] = y[j, f]
    width = shift + (count - 1) * WIN
    if not last:
        after[...] = flat[:, :, width : width + WIN, :]
    for f in range(2):
        for r in range(WIN):
            block = flat[f, r, WIN // 2 : WIN // 2 + width, :]
            tiles[f, r // 4, :, r % 4] = block.reshape(width // WIN, WIN, LANES)
        for k in range(2):
            piece = tiles[f, k].reshape(width * 4, LANES)
            outs[2 * f + k][...] = piece.astype(jnp.bfloat16)


def layer_two_kernel(count, h_ref, *rest):
    even = h_ref[0] == 0
    ins, rest = rest[:4], rest[4:]
    w_k, w_qv, w_prj, w_gu, w_dwn = rest[:5]
    outs, scratch = rest[5:9], rest[9:]
    keys, qv_t, joined = scratch[0], scratch[1], scratch[-1]
    half_tok = TOK // 2
    spans = [slice(i * half_tok, (i + 1) * half_tok) for i in range(count)]

    def tokens(group):
        parts = [ref[spans[i]] for i in group for ref in ins]
        return jnp.concatenate(parts, axis=0).astype(jnp.float32)

    for group in grouped(count):
        project_windows(tokens(group), w_k, w_qv, keys, qv_t, group[0])
    attend(count, *scratch)
    for group in grouped(count):
        y = finished(tokens(group), [joined[i] for i in group], w_prj, w_gu, w_dwn)
        for k, i in enumerate(group):
            moved, kept = (y[k * LANES + f * TOK : k * LANES + (f + 1) * TOK] for f in range(2))
            pair = (jnp.where(even, moved, kept), jnp.where(even, kept, moved))
            for f in range(2):
                part = pair[f].astype(jnp.bfloat16)
                for j in range(2):
                    outs[2 * f + j][spans[i]] = part[j * half_tok : (j + 1) * half_tok]


def from_tokens_kernel(h_ref, *rest):
    ins, (out_ref, tiles, wide) = rest[:-3], rest[-3:]
    h = h_ref[0]
    for k, (low, high) in enumerate(SHIFTED):
        for j in range(4):
            half = 1 - h if j < 2 else h
            part = ins[4 * k + j][...].astype(jnp.float32)
            tiles[half, 1 - j % 2, low:high] = part.reshape(high - low, 4, WIN, LANES)
    for r in range(WIN):
        lo = 0 if r >= 4 else 1
        row = [tiles[half, lo, :, r % 4].reshape(LANES, LANES).T for half in range(2)]
        row = pltpu.roll(jnp.concatenate(row, axis=1), WIN // 2, 1)
        for half in range(2):
            part = row[:C, half * LANES : (half + 1) * LANES]
            wide.at[half][pl.ds(r, C, stride=WIN), :] = part
    for half in range(2):
        part = wide[half].reshape(C, WIN, LANES).astype(jnp.bfloat16)
        out_ref[:, :, half * LANES : (half + 1) * LANES] = part


VMEM = pl.BlockSpec(memory_space=pltpu.VMEM)
SMEM = pl.BlockSpec(memory_space=pltpu.SMEM)
COST = pl.CostEstimate(flops=8 * 10**9, bytes_accessed=2**20, transcendentals=2**20)
PARAMS = pltpu.CompilerParams(vmem_limit_bytes=VMEM_LIMIT)


def attention_scratch(count):
    return [
        pltpu.VMEM((count, LANES, 2 * LANES), jnp.bfloat16),
        pltpu.VMEM((count, 4 * LANES, LANES), jnp.bfloat16),
        pltpu.VMEM((2, HEADS // 2, TOK, 2 * LANES), jnp.float32),
        pltpu.VMEM((2, HEADS // 2, 2 * TOK, 2 * LANES), jnp.float32),
        pltpu.VMEM((count, 2 * C, LANES), jnp.bfloat16),
    ]


def tokens_shape(rows):
    return jax.ShapeDtypeStruct((rows, LANES), jnp.bfloat16)


def to_tokens(h, x):
    shapes = [tokens_shape((high - low) * TOK) for low, high in WINDOWS]
    return pl.pallas_call(
        to_tokens_kernel,
        out_shape=shapes * 2,
        in_specs=[SMEM, VMEM],
        out_specs=[VMEM] * (2 * len(shapes)),
        scratch_shapes=[
            pltpu.VMEM((2, C * WIN, LANES), jnp.float32),
            pltpu.VMEM((2, HALF + 1, WIN, WIN, LANES), jnp.float32),
        ],
        compiler_params=PARAMS,
        name="to_tokens",
    )(h, x)


def layer_one(chunk, h, own, oth, before, weights):
    first, last = chunk == 0, chunk == len(WINDOWS) - 1
    count = WINDOWS[chunk][1] - WINDOWS[chunk][0]
    width = SHIFTED[chunk][1] - SHIFTED[chunk][0]
    edge = [] if last else [jax.ShapeDtypeStruct((2, WIN, WIN, LANES), jnp.float32)]
    shapes = [tokens_shape(width * TOK // 2)] * 4 + edge
    args = (h, own, oth, *before, *weights)
    return pl.pallas_call(
        functools.partial(layer_one_kernel, count, first, last),
        out_shape=shapes,
        in_specs=[SMEM] + [VMEM] * (len(args) - 1),
        out_specs=[VMEM] * len(shapes),
        scratch_shapes=[
            pltpu.VMEM((2, WIN, (width + 1) * WIN, LANES), jnp.float32),
            pltpu.VMEM((2, 2, width, 4, WIN, LANES), jnp.float32),
            *attention_scratch(count),
        ],
        compiler_params=PARAMS,
        cost_estimate=COST,
        name="layer_one",
    )(*args)


def layer_two(chunk, h, pieces, weights):
    count = SHIFTED[chunk][1] - SHIFTED[chunk][0]
    return pl.pallas_call(
        functools.partial(layer_two_kernel, count),
        out_shape=[tokens_shape(count * TOK // 2)] * 4,
        in_specs=[SMEM] + [VMEM] * 9,
        out_specs=[VMEM] * 4,
        scratch_shapes=attention_scratch(count),
        compiler_params=PARAMS,
        cost_estimate=COST,
        name="layer_two",
    )(h, *pieces, *weights)


def from_tokens(h, pieces):
    return pl.pallas_call(
        from_tokens_kernel,
        out_shape=jax.ShapeDtypeStruct((C, WIN, 2 * LANES), jnp.bfloat16),
        in_specs=[SMEM] + [VMEM] * len(pieces),
        out_specs=VMEM,
        scratch_shapes=[
            pltpu.VMEM((2, 2, HALF, 4, WIN, LANES), jnp.float32),
            pltpu.VMEM((2, C * WIN, LANES), jnp.float32),
        ],
        compiler_params=PARAMS,
        name="from_tokens",
    )(h, *pieces)


def prepare_kernel(w_mut, w_slf, w_prj, w_gte, w_upp, w_dwn, *outs):
    row = lax.broadcasted_iota(jnp.int32, (LANES, 3 * C), 0)
    col = lax.broadcasted_iota(jnp.int32, (LANES, 3 * C), 1)
    picks = []
    for part in range(3):
        hit = (col == row + part * C) & (row < C)
        picks.append(jnp.where(hit, 1.0, 0.0).astype(jnp.bfloat16))
    for layer in range(2):
        w_k, w_qv, w_p, w_gu, w_d = outs[5 * layer : 5 * layer + 5]
        for ref in (w_k, w_qv, w_p, w_gu, w_d):
            ref[...] = jnp.zeros(ref.shape, jnp.bfloat16)
        for i, w in enumerate((w_mut, w_slf)):
            w = w[layer]
            span = slice(i * LANES, (i + 1) * LANES)
            w_k[:C, span] = matmul_nt(w, picks[1]).astype(jnp.bfloat16)
            w_qv[span, :C] = matmul_nt(picks[0], w).astype(jnp.bfloat16)
            span = slice((2 + i) * LANES, (3 + i) * LANES)
            w_qv[span, :C] = matmul_nt(picks[2], w).astype(jnp.bfloat16)
        w_p[:, :C] = w_prj[layer]
        w_gu[:C, :FFN] = w_gte[layer]
        w_gu[:C, 2 * LANES : 2 * LANES + FFN] = w_upp[layer]
        w_d[:FFN, :C] = w_dwn[layer]


def prepared(*weights):
    shapes = [
        (LANES, 2 * LANES),
        (4 * LANES, LANES),
        (2 * C, LANES),
        (LANES, 4 * LANES),
        (2 * LANES, LANES),
    ] * 2
    return pl.pallas_call(
        prepare_kernel,
        out_shape=[jax.ShapeDtypeStruct(shape, jnp.bfloat16) for shape in shapes],
        in_specs=[VMEM] * len(weights),
        out_specs=[VMEM] * len(shapes),
        compiler_params=PARAMS,
        name="prepare",
    )(*weights)


def on_device(features, *weights):
    frames, strips = lax.axis_size("frame"), lax.axis_size("strip")

    def send(value, even_step, odd_step, strip_step):
        pairs = []
        for f in range(frames):
            for s in range(strips):
                to = (f + (odd_step if f % 2 else even_step)) % frames
                pairs.append((f * strips + s, to * strips + (s + strip_step) % strips))
        return lax.ppermute(value, ("frame", "strip"), pairs)

    h = (lax.axis_index("frame") % 2).astype(jnp.int32).reshape(1)
    ready = prepared(*weights)
    w_one, w_two = ready[:5], ready[5:]
    parts = to_tokens(h, features[0])
    chunks = range(len(WINDOWS))
    others = [send(parts[k], 1, -1, 0) for k in chunks]
    edge = ()
    pieces = []
    for k in chunks:
        kept_up, kept_lo, moved_up, moved_lo, *edge = layer_one(
            k, h, parts[len(WINDOWS) + k], others[k], edge, w_one
        )
        moved_up = send(moved_up, 2, 2, -1)
        moved_lo = send(moved_lo, 2, 2, 0)
        kept_up = send(kept_up, 0, 0, -1)
        pieces.append((moved_up, moved_lo, kept_up, kept_lo))
    home = []
    for k in chunks:
        far_up, far_lo, near_up, near_lo = layer_two(k, h, pieces[k], w_two)
        far_up = send(far_up, -1, -1, 1)
        far_lo = send(far_lo, -1, -1, 0)
        near_up = send(near_up, 0, -2, 1)
        near_lo = send(near_lo, 0, -2, 0)
        home += [far_up, far_lo, near_up, near_lo]
    return from_tokens(h, home)[None]


def solution(mesh):
    in_specs = (P("frame", None, "strip", None), P(), P(), P(), P(), P(), P())
    out_specs = P("frame", None, "strip", None)
    return jax.shard_map(
        on_device, mesh=mesh, in_specs=in_specs, out_specs=out_specs, check_vma=False
    )
```

```python
import functools

import jax
import jax.numpy as jnp
import numpy as np
from jax import lax
from jax.experimental import pallas as pl
from jax.experimental.pallas import tpu as pltpu
from jax.sharding import PartitionSpec as P

C = 120
HEADS = 6
HEAD = 20
FFN = 240
WIN = 8
LANES = 128
HALF = 16
GROUP = 8
TOK = WIN * WIN
EPS = 1e-05
SHIFTED = ((0, 16),)
WINDOWS = ((0, 17),)
EXP2_SCALE = float(np.log2(np.e) * HEAD**-0.5)
VMEM_LIMIT = 56 * 1024 * 1024


def matmul(a, b):
    return lax.dot_general(a, b, (((1,), (0,)), ((), ())), preferred_element_type=jnp.float32)


def matmul_nt(a, b):
    return lax.dot_general(a, b, (((1,), (1,)), ((), ())), preferred_element_type=jnp.float32)


def matmul_tn(a, b):
    return lax.dot_general(a, b, (((0,), (0,)), ((), ())), preferred_element_type=jnp.float32)


def normed(x):
    lane = lax.broadcasted_iota(jnp.int32, x.shape, 1)
    mean = jnp.sum(x, axis=1, keepdims=True) * (1.0 / C)
    centred = jnp.where(lane < C, x - mean, 0.0)
    spread = jnp.sum(centred * centred, axis=1, keepdims=True) * (1.0 / C)
    return (centred * lax.rsqrt(spread + EPS)).astype(jnp.bfloat16)


def head_only(q_t, head):
    low = head * HEAD // 16 * 16
    high = -(-(head * HEAD + HEAD) // 16) * 16
    row = lax.broadcasted_iota(jnp.int32, (high - low, q_t.shape[1]), 0) + low
    keep = (row >= head * HEAD) & (row < head * HEAD + HEAD)
    pieces = [q_t[low:high] * jnp.where(keep, 1.0, 0.0).astype(jnp.bfloat16)]
    if low:
        pieces.insert(0, jnp.zeros((low, q_t.shape[1]), jnp.bfloat16))
    if high < LANES:
        pieces.append(jnp.zeros((LANES - high, q_t.shape[1]), jnp.bfloat16))
    return jnp.concatenate(pieces, axis=0)


def softmax_rows(scores):
    top = jnp.max(scores, axis=0, keepdims=True)
    weights = jnp.exp2((scores - top) * EXP2_SCALE)
    total = jnp.sum(weights, axis=0, keepdims=True)
    return weights * (1.0 / total)


def project_windows(x, w_k, w_qv, keys, qv_t, first):
    normal = normed(x)
    new_keys = matmul(normal, w_k[...]).astype(jnp.bfloat16)
    new_qv = matmul_nt(w_qv[...], normal).astype(jnp.bfloat16)
    for i in range(x.shape[0] // LANES):
        span = slice(i * LANES, (i + 1) * LANES)
        keys[first + i] = new_keys[span]
        qv_t[first + i] = new_qv[:, span]


def score_block(kind, pair, keys, qv_t, window, of_first):
    kind_q = qv_t[window, kind * LANES : (kind + 1) * LANES]
    queries = jnp.concatenate(
        [head_only(kind_q, 2 * pair), head_only(kind_q, 2 * pair + 1)], axis=1
    )
    scores = matmul(keys[window, :, kind * LANES : (kind + 1) * LANES], queries)
    if kind == 0:
        scores = jnp.where(of_first, scores[TOK:], scores[:TOK])
    return scores


def mix_block(kind, pair, scores, qv_t, window, of_first):
    probs = [softmax_rows(scores[:, i * LANES : (i + 1) * LANES]) for i in range(2)]
    probs = jnp.concatenate(probs, axis=1).astype(jnp.bfloat16)
    if kind == 0:
        first = jnp.where(of_first, 1.0, 0.0).astype(jnp.bfloat16)
        second = jnp.where(of_first, 0.0, 1.0).astype(jnp.bfloat16)
        probs = jnp.concatenate([probs * second, probs * first], axis=0)
    want = pair * 2 * HEAD
    low = want // 16 * 16
    base = (2 + kind) * LANES + low
    mixed = matmul(qv_t[window, base : base + 48], probs)[want - low : want - low + 2 * HEAD]
    one, two = mixed[:, :LANES], mixed[:, LANES:]
    row = lax.broadcasted_iota(jnp.int32, (8, LANES), 0)
    shared = jnp.where(row < HEAD - 16, one[16:24], two[16:24])
    return jnp.concatenate([one[:16], shared, two[24:]], axis=0)


def attend(count, keys, qv_t, mutual_scores, self_scores, joined):
    scores = (mutual_scores, self_scores)
    lane = lax.broadcasted_iota(jnp.int32, (TOK, 2 * LANES), 1)
    of_first = (lane % LANES) < TOK
    blocks = [(kind, pair) for kind in range(2) for pair in range(HEADS // 2)]
    for kind, pair in blocks:
        scores[kind][0, pair] = score_block(kind, pair, keys, qv_t, 0, of_first)
    for i in range(count):
        outs = []
        for kind, pair in blocks:
            ref = scores[kind]
            if i + 1 < count:
                ref[(i + 1) % 2, pair] = score_block(kind, pair, keys, qv_t, i + 1, of_first)
            outs.append(mix_block(kind, pair, ref[i % 2, pair], qv_t, i, of_first))
        joined[i] = jnp.concatenate(outs, axis=0).astype(jnp.bfloat16)


def finished(x, joined, w_prj, w_gu, w_dwn):
    mixed = [matmul_tn(block, w_prj[...]) for block in joined]
    middle = x + jnp.concatenate(mixed, axis=0)
    both = matmul(normed(middle), w_gu[...])
    gate, up = both[:, : 2 * LANES], both[:, 2 * LANES :]
    gelu = 0.5 * gate * (1.0 + lax.erf(gate * float(np.sqrt(0.5))))
    hidden = (gelu * up).astype(jnp.bfloat16)
    return middle + matmul(hidden, w_dwn[...])


def to_tokens_kernel(h_ref, x_ref, send_ref, own_ref, raw, wide, tiles, sems):
    h = h_ref[0]
    copies = []
    for k in range(2):
        half = 1 - h if k == 0 else h
        source = x_ref.at[:, :, pl.ds(pl.multiple_of(half * LANES, LANES), LANES)]
        copies.append(pltpu.make_async_copy(source, raw.at[k], sems.at[k]))
        copies[-1].start()
    pad = jnp.zeros((LANES - C, LANES), jnp.float32)
    for k in range(2):
        copies[k].wait()
        wide[k] = raw[k].astype(jnp.float32).reshape(C * WIN, LANES)
        for r in range(WIN):
            block = wide.at[k][pl.ds(r, C, stride=WIN), :]
            block = jnp.concatenate([block, pad], axis=0).T
            tiles[k, :HALF, r] = block.reshape(HALF, WIN, LANES)
    for k, ref in enumerate((send_ref, own_ref)):
        main = tiles[k, :HALF].reshape(HALF * TOK, LANES)
        ref[: HALF * TOK] = main.astype(jnp.bfloat16)
        ref[HALF * TOK :] = tiles[1 - k, 0].reshape(TOK, LANES).astype(jnp.bfloat16)


def grouped(count):
    parts = max(1, count // GROUP)
    cuts = [count * i // parts for i in range(parts + 1)]
    return [range(low, high) for low, high in zip(cuts[:-1], cuts[1:])]


def layer_one_kernel(count, first, last, h_ref, own_ref, oth_ref, *rest):
    h = h_ref[0]
    if not first:
        before, rest = rest[0], rest[1:]
    w_k, w_qv, w_prj, w_gu, w_dwn = rest[:5]
    outs, rest = rest[5:9], rest[9:]
    if not last:
        after, rest = rest[0], rest[1:]
    flat, tiles, *scratch = rest
    keys, qv_t, joined = scratch[0], scratch[1], scratch[-1]
    shift = 0 if first else WIN

    def tokens(group):
        parts = []
        for i in group:
            span = slice(i * TOK, (i + 1) * TOK)
            parts += [own_ref[span], oth_ref[span]]
        return jnp.concatenate(parts, axis=0).astype(jnp.float32)

    for group in grouped(count):
        project_windows(tokens(group), w_k, w_qv, keys, qv_t, group[0])
    attend(count, *scratch)
    if not first:
        flat[:, :, :WIN, :] = before[...]
    for group in grouped(count):
        y = finished(tokens(group), [joined[i] for i in group], w_prj, w_gu, w_dwn)
        y = y.reshape(len(group), 2, WIN, WIN, LANES)
        for j, i in enumerate(group):
            for f in range(2):
                flat[1 - h if f else h, :, shift + i * WIN : shift + (i + 1) * WIN, :] = y[j, f]
    width = shift + (count - 1) * WIN
    if not last:
        after[...] = flat[:, :, width : width + WIN, :]
    for f in range(2):
        for r in range(WIN):
            block = flat[f, r, WIN // 2 : WIN // 2 + width, :]
            tiles[f, r // 4, :, r % 4] = block.reshape(width // WIN, WIN, LANES)
        for k in range(2):
            piece = tiles[f, k].reshape(width * 4, LANES)
            outs[2 * f + k][...] = piece.astype(jnp.bfloat16)


def layer_two_kernel(count, h_ref, *rest):
    even = h_ref[0] == 0
    ins, rest = rest[:4], rest[4:]
    w_k, w_qv, w_prj, w_gu, w_dwn = rest[:5]
    outs, scratch = rest[5:9], rest[9:]
    keys, qv_t, joined = scratch[0], scratch[1], scratch[-1]
    half_tok = TOK // 2
    spans = [slice(i * half_tok, (i + 1) * half_tok) for i in range(count)]

    def tokens(group):
        parts = [ref[spans[i]] for i in group for ref in ins]
        return jnp.concatenate(parts, axis=0).astype(jnp.float32)

    for group in grouped(count):
        project_windows(tokens(group), w_k, w_qv, keys, qv_t, group[0])
    attend(count, *scratch)
    for group in grouped(count):
        y = finished(tokens(group), [joined[i] for i in group], w_prj, w_gu, w_dwn)
        for k, i in enumerate(group):
            moved, kept = (y[k * LANES + f * TOK : k * LANES + (f + 1) * TOK] for f in range(2))
            pair = (jnp.where(even, moved, kept), jnp.where(even, kept, moved))
            for f in range(2):
                part = pair[f].astype(jnp.bfloat16)
                for j, out in enumerate((outs[f], outs[2 + f])):
                    out[spans[i]] = part[j * half_tok : (j + 1) * half_tok]


def from_tokens_kernel(h_ref, far_up, near_up, far_lo, near_lo, out_ref, rows, wide, ready, sems):
    edge = WIN // 2

    def place(h):
        for lo, pair in enumerate(((far_up, near_up), (far_lo, near_lo))):
            for half in range(2):
                part = pair[int(half == h)][...].astype(jnp.float32)
                part = part.reshape(HALF, 4, WIN, LANES)
                for r in range(4):
                    low = edge + half * LANES
                    rows[4 * lo + r, low : low + LANES] = part[:, r].reshape(LANES, LANES)

    for h in range(2):

        @pl.when(h_ref[0] == h)
        def _():
            place(h)

    copies = []
    for half in range(2):
        for r in range(WIN):
            if half == 0:
                rows[r, :edge] = rows[r, 2 * LANES : 2 * LANES + edge]
            block = rows[r, half * LANES : (half + 1) * LANES].T
            wide.at[half][pl.ds(r, C, stride=WIN), :] = block[:C]
        ready[half] = wide[half].reshape(C, WIN, LANES).astype(jnp.bfloat16)
        target = out_ref.at[:, :, half * LANES : (half + 1) * LANES]
        copies.append(pltpu.make_async_copy(ready.at[half], target, sems.at[half]))
        copies[-1].start()
    for copy in copies:
        copy.wait()


VMEM = pl.BlockSpec(memory_space=pltpu.VMEM)
SMEM = pl.BlockSpec(memory_space=pltpu.SMEM)
COST = pl.CostEstimate(flops=8 * 10**9, bytes_accessed=2**20, transcendentals=2**20)
PARAMS = pltpu.CompilerParams(vmem_limit_bytes=VMEM_LIMIT)


def attention_scratch(count):
    return [
        pltpu.VMEM((count, LANES, 2 * LANES), jnp.bfloat16),
        pltpu.VMEM((count, 4 * LANES, LANES), jnp.bfloat16),
        pltpu.VMEM((2, HEADS // 2, TOK, 2 * LANES), jnp.float32),
        pltpu.VMEM((2, HEADS // 2, 2 * TOK, 2 * LANES), jnp.float32),
        pltpu.VMEM((count, 2 * C, LANES), jnp.bfloat16),
    ]


def tokens_shape(rows):
    return jax.ShapeDtypeStruct((rows, LANES), jnp.bfloat16)


def to_tokens(h, x):
    return pl.pallas_call(
        to_tokens_kernel,
        out_shape=[tokens_shape((HALF + 1) * TOK)] * 2,
        in_specs=[SMEM, pl.BlockSpec(memory_space=pl.ANY)],
        out_specs=[VMEM] * 2,
        scratch_shapes=[
            pltpu.VMEM((2, C, WIN, LANES), jnp.bfloat16),
            pltpu.VMEM((2, C * WIN, LANES), jnp.float32),
            pltpu.VMEM((2, HALF, WIN, WIN, LANES), jnp.float32),
            pltpu.SemaphoreType.DMA((2,)),
        ],
        compiler_params=PARAMS,
        name="to_tokens",
    )(h, x)


def layer_one(chunk, h, own, oth, before, weights):
    first, last = chunk == 0, chunk == len(WINDOWS) - 1
    count = WINDOWS[chunk][1] - WINDOWS[chunk][0]
    width = SHIFTED[chunk][1] - SHIFTED[chunk][0]
    edge = [] if last else [jax.ShapeDtypeStruct((2, WIN, WIN, LANES), jnp.float32)]
    shapes = [tokens_shape(width * TOK // 2)] * 4 + edge
    args = (h, own, oth, *before, *weights)
    return pl.pallas_call(
        functools.partial(layer_one_kernel, count, first, last),
        out_shape=shapes,
        in_specs=[SMEM] + [VMEM] * (len(args) - 1),
        out_specs=[VMEM] * len(shapes),
        scratch_shapes=[
            pltpu.VMEM((2, WIN, (width + 1) * WIN, LANES), jnp.float32),
            pltpu.VMEM((2, 2, width, 4, WIN, LANES), jnp.float32),
            *attention_scratch(count),
        ],
        compiler_params=PARAMS,
        cost_estimate=COST,
        name="layer_one",
    )(*args)


def layer_two(chunk, h, pieces, weights):
    count = SHIFTED[chunk][1] - SHIFTED[chunk][0]
    return pl.pallas_call(
        functools.partial(layer_two_kernel, count),
        out_shape=[tokens_shape(count * TOK // 2)] * 4,
        in_specs=[SMEM] + [VMEM] * 9,
        out_specs=[VMEM] * 4,
        scratch_shapes=attention_scratch(count),
        compiler_params=PARAMS,
        cost_estimate=COST,
        name="layer_two",
    )(h, *pieces, *weights)


def from_tokens(h, pieces):
    return pl.pallas_call(
        from_tokens_kernel,
        out_shape=jax.ShapeDtypeStruct((C, WIN, 2 * LANES), jnp.bfloat16),
        in_specs=[SMEM] + [VMEM] * len(pieces),
        out_specs=pl.BlockSpec(memory_space=pl.ANY),
        scratch_shapes=[
            pltpu.VMEM((WIN, 2 * LANES + WIN, LANES), jnp.float32),
            pltpu.VMEM((2, C * WIN, LANES), jnp.float32),
            pltpu.VMEM((2, C, WIN, LANES), jnp.bfloat16),
            pltpu.SemaphoreType.DMA((2,)),
        ],
        compiler_params=PARAMS,
        name="from_tokens",
    )(h, *pieces)


def prepare_kernel(w_mut, w_slf, w_prj, w_gte, w_upp, w_dwn, *outs):
    row = lax.broadcasted_iota(jnp.int32, (LANES, 3 * C), 0)
    col = lax.broadcasted_iota(jnp.int32, (LANES, 3 * C), 1)
    picks = []
    for part in range(3):
        hit = (col == row + part * C) & (row < C)
        picks.append(jnp.where(hit, 1.0, 0.0).astype(jnp.bfloat16))
    for layer in range(2):
        w_k, w_qv, w_p, w_gu, w_d = outs[5 * layer : 5 * layer + 5]
        for ref in (w_k, w_qv, w_p, w_gu, w_d):
            ref[...] = jnp.zeros(ref.shape, jnp.bfloat16)
        for i, w in enumerate((w_mut, w_slf)):
            w = w[layer]
            span = slice(i * LANES, (i + 1) * LANES)
            w_k[:C, span] = matmul_nt(w, picks[1]).astype(jnp.bfloat16)
            w_qv[span, :C] = matmul_nt(picks[0], w).astype(jnp.bfloat16)
            span = slice((2 + i) * LANES, (3 + i) * LANES)
            w_qv[span, :C] = matmul_nt(picks[2], w).astype(jnp.bfloat16)
        w_p[:, :C] = w_prj[layer]
        w_gu[:C, :FFN] = w_gte[layer]
        w_gu[:C, 2 * LANES : 2 * LANES + FFN] = w_upp[layer]
        w_d[:FFN, :C] = w_dwn[layer]


def prepared(*weights):
    shapes = [
        (LANES, 2 * LANES),
        (4 * LANES, LANES),
        (2 * C, LANES),
        (LANES, 4 * LANES),
        (2 * LANES, LANES),
    ] * 2
    return pl.pallas_call(
        prepare_kernel,
        out_shape=[jax.ShapeDtypeStruct(shape, jnp.bfloat16) for shape in shapes],
        in_specs=[VMEM] * len(weights),
        out_specs=[VMEM] * len(shapes),
        compiler_params=PARAMS,
        name="prepare",
    )(*weights)


def on_device(features, *weights):
    frames, strips = lax.axis_size("frame"), lax.axis_size("strip")

    def send(value, even_step, odd_step, strip_step):
        pairs = []
        for f in range(frames):
            for s in range(strips):
                to = (f + (odd_step if f % 2 else even_step)) % frames
                pairs.append((f * strips + s, to * strips + (s + strip_step) % strips))
        return lax.ppermute(value, ("frame", "strip"), pairs)

    h = (lax.axis_index("frame") % 2).astype(jnp.int32).reshape(1)
    ready = prepared(*weights)
    w_one, w_two = ready[:5], ready[5:]
    parts = to_tokens(h, features[0])
    chunks = range(len(WINDOWS))
    others = [send(parts[k], 1, -1, 0) for k in chunks]
    edge = ()
    pieces = []
    for k in chunks:
        kept_up, kept_lo, moved_up, moved_lo, *edge = layer_one(
            k, h, parts[len(WINDOWS) + k], others[k], edge, w_one
        )
        moved_up = send(moved_up, 2, 2, -1)
        moved_lo = send(moved_lo, 2, 2, 0)
        kept_up = send(kept_up, 0, 0, -1)
        pieces.append((moved_up, moved_lo, kept_up, kept_lo))
    home = []
    for k in chunks:
        far_up, near_up, far_lo, near_lo = layer_two(k, h, pieces[k], w_two)
        far_up = send(far_up, -1, -1, 1)
        near_up = send(near_up, 0, -2, 1)
        far_lo = send(far_lo, -1, -1, 0)
        near_lo = send(near_lo, 0, -2, 0)
        home += [far_up, near_up, far_lo, near_lo]
    return from_tokens(h, home)[None]


def solution(mesh):
    in_specs = (P("frame", None, "strip", None), P(), P(), P(), P(), P(), P())
    out_specs = P("frame", None, "strip", None)
    return jax.shard_map(
        on_device, mesh=mesh, in_specs=in_specs, out_specs=out_specs, check_vma=False
    )
```

```python
import functools

import jax
import jax.numpy as jnp
import numpy as np
from jax import lax
from jax.experimental import pallas as pl
from jax.experimental.pallas import tpu as pltpu
from jax.sharding import PartitionSpec as P

C = 120
HEADS = 6
HEAD = 20
FFN = 240
WIN = 8
LANES = 128
HALF = 16
GROUP = 8
TOK = WIN * WIN
EPS = 1e-05
SHIFTED = ((0, 16),)
WINDOWS = ((0, 17),)
EXP2_SCALE = float(np.log2(np.e) * HEAD**-0.5)
VMEM_LIMIT = 56 * 1024 * 1024


def matmul(a, b):
    return lax.dot_general(a, b, (((1,), (0,)), ((), ())), preferred_element_type=jnp.float32)


def matmul_nt(a, b):
    return lax.dot_general(a, b, (((1,), (1,)), ((), ())), preferred_element_type=jnp.float32)


def matmul_tn(a, b):
    return lax.dot_general(a, b, (((0,), (0,)), ((), ())), preferred_element_type=jnp.float32)


def normed(x):
    lane = lax.broadcasted_iota(jnp.int32, x.shape, 1)
    mean = jnp.sum(x, axis=1, keepdims=True) * (1.0 / C)
    centred = jnp.where(lane < C, x - mean, 0.0)
    spread = jnp.sum(centred * centred, axis=1, keepdims=True) * (1.0 / C)
    return (centred * lax.rsqrt(spread + EPS)).astype(jnp.bfloat16)


def rows_of_head(head):
    low = head * HEAD // 16 * 16
    return low, low + 32


def head_only(q_t, head, lanes=None):
    low, high = rows_of_head(head)
    row = lax.broadcasted_iota(jnp.int32, (high - low, q_t.shape[1]), 0) + low
    keep = (row >= head * HEAD) & (row < head * HEAD + HEAD)
    if lanes is not None:
        lane = lax.broadcasted_iota(jnp.int32, keep.shape, 1)
        keep = keep & ((lane < TOK) if lanes == 0 else (lane >= TOK))
    pieces = [q_t[low:high] * jnp.where(keep, 1.0, 0.0).astype(jnp.bfloat16)]
    if low:
        pieces.insert(0, jnp.zeros((low, q_t.shape[1]), jnp.bfloat16))
    if high < LANES:
        pieces.append(jnp.zeros((LANES - high, q_t.shape[1]), jnp.bfloat16))
    return jnp.concatenate(pieces, axis=0)


def softmax_rows(scores):
    top = jnp.max(scores, axis=0, keepdims=True)
    weights = jnp.exp2((scores - top) * EXP2_SCALE)
    total = jnp.sum(weights, axis=0, keepdims=True)
    return weights * (1.0 / total)


def project_windows(x, w_k, w_qv, mutual_keys, self_keys, qv_t, first):
    normal = normed(x)
    new_keys = matmul(normal, w_k[...]).astype(jnp.bfloat16)
    new_qv = matmul_nt(w_qv[...], normal).astype(jnp.bfloat16)
    for i in range(x.shape[0] // LANES):
        low = i * LANES
        for f in range(2):
            span = slice(f * LANES, (f + 1) * LANES)
            mutual_keys[first + i, :, span] = new_keys[low + f * TOK : low + (f + 1) * TOK, :LANES]
        self_keys[first + i] = new_keys[low : low + LANES, LANES:]
        qv_t[first + i] = new_qv[:, low : low + LANES]


def score_mutual(pair, mutual_keys, qv_t, window):
    heads = (2 * pair, 2 * pair + 1)
    q_t = qv_t[window, :LANES]
    queries = [
        jnp.concatenate([head_only(q_t, head, lanes) for head in heads], axis=1) for lanes in (1, 0)
    ]
    return matmul(mutual_keys[window], jnp.concatenate(queries, axis=0))


def score_self(pair, self_keys, qv_t, window):
    heads = (2 * pair, 2 * pair + 1)
    q_t = qv_t[window, LANES : 2 * LANES]
    queries = jnp.concatenate([head_only(q_t, head) for head in heads], axis=1)
    return matmul(self_keys[window], queries)


def mix_head(head, mutual, own, qv_t, window):
    lane = lax.broadcasted_iota(jnp.int32, (TOK, LANES), 1)
    first = jnp.where(lane < TOK, 1.0, 0.0).astype(jnp.bfloat16)
    second = jnp.where(lane < TOK, 0.0, 1.0).astype(jnp.bfloat16)
    probs = softmax_rows(mutual).astype(jnp.bfloat16)
    probs = jnp.concatenate([probs * second, probs * first], axis=0)
    own = softmax_rows(own).astype(jnp.bfloat16)
    nothing = jnp.zeros((LANES, LANES), jnp.bfloat16)
    probs = jnp.concatenate(
        [jnp.concatenate([probs, nothing], axis=1), jnp.concatenate([nothing, own], axis=1)], axis=0
    )
    low, high = rows_of_head(head)
    values = [qv_t[window, (2 + kind) * LANES + low : (2 + kind) * LANES + high] for kind in range(2)]
    return matmul(jnp.concatenate(values, axis=1), probs)


def by_channel(mixed):
    row = lax.broadcasted_iota(jnp.int32, (8, LANES), 0)
    parts = []
    for head in range(0, HEADS, 2):
        base = head * HEAD
        one, two = mixed[head], mixed[head + 1]
        one_low, two_low = base - rows_of_head(head)[0], base - rows_of_head(head + 1)[0]
        shared = jnp.where(
            row < HEAD - 16, one[one_low + 16 : one_low + 24], two[two_low + 16 : two_low + 24]
        )
        parts += [one[one_low : one_low + 16], shared, two[two_low + 24 : two_low + 40]]
    return jnp.concatenate(parts, axis=0)


def attend(count, mutual_keys, self_keys, qv_t, mutual_scores, self_scores, joined):
    def score(i, pair):
        mutual_scores[i % 2, pair] = score_mutual(pair, mutual_keys, qv_t, i)
        self_scores[i % 2, pair] = score_self(pair, self_keys, qv_t, i)

    for pair in range(HEADS // 2):
        score(0, pair)
    for i in range(count):
        mixed = []
        for pair in range(HEADS // 2):
            if i + 1 < count:
                score(i + 1, pair)
            for j in range(2):
                span = slice(j * LANES, (j + 1) * LANES)
                mutual, own = mutual_scores[i % 2, pair, :, span], self_scores[i % 2, pair, :, span]
                mixed.append(mix_head(2 * pair + j, mutual, own, qv_t, i))
        for kind in range(2):
            span = slice(kind * LANES, (kind + 1) * LANES)
            part = by_channel([block[:, span] for block in mixed])
            joined[i, kind * C : (kind + 1) * C] = part.astype(jnp.bfloat16)


def finished(x, joined, w_prj, w_gu, w_dwn):
    mixed = [matmul_tn(block, w_prj[...]) for block in joined]
    middle = x + jnp.concatenate(mixed, axis=0)
    both = matmul(normed(middle), w_gu[...])
    gate, up = both[:, : 2 * LANES], both[:, 2 * LANES :]
    gelu = 0.5 * gate * (1.0 + lax.erf(gate * float(np.sqrt(0.5))))
    hidden = (gelu * up).astype(jnp.bfloat16)
    return middle + matmul(hidden, w_dwn[...])


def to_tokens_kernel(h_ref, x_ref, send_ref, own_ref, raw, wide, tiles, sems):
    h = h_ref[0]
    copies = []
    for k in range(2):
        half = 1 - h if k == 0 else h
        source = x_ref.at[:, :, pl.ds(pl.multiple_of(half * LANES, LANES), LANES)]
        copies.append(pltpu.make_async_copy(source, raw.at[k], sems.at[k]))
        copies[-1].start()
    pad = jnp.zeros((LANES - C, LANES), jnp.float32)
    for k in range(2):
        copies[k].wait()
        wide[k] = raw[k].astype(jnp.float32).reshape(C * WIN, LANES)
        for r in range(WIN):
            block = wide.at[k][pl.ds(r, C, stride=WIN), :]
            block = jnp.concatenate([block, pad], axis=0).T
            tiles[k, :HALF, r] = block.reshape(HALF, WIN, LANES)
    for k, ref in enumerate((send_ref, own_ref)):
        main = tiles[k, :HALF].reshape(HALF * TOK, LANES)
        ref[: HALF * TOK] = main.astype(jnp.bfloat16)
        ref[HALF * TOK :] = tiles[1 - k, 0].reshape(TOK, LANES).astype(jnp.bfloat16)


def grouped(count):
    parts = max(1, count // GROUP)
    cuts = [count * i // parts for i in range(parts + 1)]
    return [range(low, high) for low, high in zip(cuts[:-1], cuts[1:])]


def layer_one_kernel(count, first, last, h_ref, own_ref, oth_ref, *rest):
    h = h_ref[0]
    if not first:
        before, rest = rest[0], rest[1:]
    w_k, w_qv, w_prj, w_gu, w_dwn = rest[:5]
    outs, rest = rest[5:9], rest[9:]
    if not last:
        after, rest = rest[0], rest[1:]
    flat, tiles, *scratch = rest
    mutual_keys, self_keys, qv_t, joined = *scratch[:3], scratch[-1]
    shift = 0 if first else WIN

    def tokens(group):
        parts = []
        for i in group:
            span = slice(i * TOK, (i + 1) * TOK)
            parts += [own_ref[span], oth_ref[span]]
        return jnp.concatenate(parts, axis=0).astype(jnp.float32)

    for group in grouped(count):
        project_windows(tokens(group), w_k, w_qv, mutual_keys, self_keys, qv_t, group[0])
    attend(count, *scratch)
    if not first:
        flat[:, :, :WIN, :] = before[...]
    for group in grouped(count):
        y = finished(tokens(group), [joined[i] for i in group], w_prj, w_gu, w_dwn)
        y = y.reshape(len(group), 2, WIN, WIN, LANES)
        for j, i in enumerate(group):
            for f in range(2):
                flat[1 - h if f else h, :, shift + i * WIN : shift + (i + 1) * WIN, :] = y[j, f]
    width = shift + (count - 1) * WIN
    if not last:
        after[...] = flat[:, :, width : width + WIN, :]
    for f in range(2):
        for r in range(WIN):
            block = flat[f, r, WIN // 2 : WIN // 2 + width, :]
            tiles[f, r // 4, :, r % 4] = block.reshape(width // WIN, WIN, LANES)
        for k in range(2):
            piece = tiles[f, k].reshape(width * 4, LANES)
            outs[2 * f + k][...] = piece.astype(jnp.bfloat16)


def layer_two_kernel(count, h_ref, *rest):
    even = h_ref[0] == 0
    ins, rest = rest[:4], rest[4:]
    w_k, w_qv, w_prj, w_gu, w_dwn = rest[:5]
    outs, scratch = rest[5:9], rest[9:]
    mutual_keys, self_keys, qv_t, joined = *scratch[:3], scratch[-1]
    half_tok = TOK // 2
    spans = [slice(i * half_tok, (i + 1) * half_tok) for i in range(count)]

    def tokens(group):
        parts = [ref[spans[i]] for i in group for ref in ins]
        return jnp.concatenate(parts, axis=0).astype(jnp.float32)

    for group in grouped(count):
        project_windows(tokens(group), w_k, w_qv, mutual_keys, self_keys, qv_t, group[0])
    attend(count, *scratch)
    for group in grouped(count):
        y = finished(tokens(group), [joined[i] for i in group], w_prj, w_gu, w_dwn)
        for k, i in enumerate(group):
            moved, kept = (y[k * LANES + f * TOK : k * LANES + (f + 1) * TOK] for f in range(2))
            pair = (jnp.where(even, moved, kept), jnp.where(even, kept, moved))
            for f in range(2):
                part = pair[f].astype(jnp.bfloat16)
                for j, out in enumerate((outs[f], outs[2 + f])):
                    out[spans[i]] = part[j * half_tok : (j + 1) * half_tok]


def from_tokens_kernel(h_ref, far_up, near_up, far_lo, near_lo, out_ref, rows, wide, ready, sems):
    edge = WIN // 2

    def place(h):
        for lo, pair in enumerate(((far_up, near_up), (far_lo, near_lo))):
            for half in range(2):
                part = pair[int(half == h)][...].astype(jnp.float32)
                part = part.reshape(HALF, 4, WIN, LANES)
                for r in range(4):
                    low = edge + half * LANES
                    rows[4 * lo + r, low : low + LANES] = part[:, r].reshape(LANES, LANES)

    for h in range(2):

        @pl.when(h_ref[0] == h)
        def _():
            place(h)

    copies = []
    for half in range(2):
        for r in range(WIN):
            if half == 0:
                rows[r, :edge] = rows[r, 2 * LANES : 2 * LANES + edge]
            block = rows[r, half * LANES : (half + 1) * LANES].T
            wide.at[half][pl.ds(r, C, stride=WIN), :] = block[:C]
        ready[half] = wide[half].reshape(C, WIN, LANES).astype(jnp.bfloat16)
        target = out_ref.at[:, :, half * LANES : (half + 1) * LANES]
        copies.append(pltpu.make_async_copy(ready.at[half], target, sems.at[half]))
        copies[-1].start()
    for copy in copies:
        copy.wait()


VMEM = pl.BlockSpec(memory_space=pltpu.VMEM)
SMEM = pl.BlockSpec(memory_space=pltpu.SMEM)
COST = pl.CostEstimate(flops=8 * 10**9, bytes_accessed=2**20, transcendentals=2**20)
PARAMS = pltpu.CompilerParams(vmem_limit_bytes=VMEM_LIMIT)


def attention_scratch(count):
    return [
        pltpu.VMEM((count, TOK, 2 * LANES), jnp.bfloat16),
        pltpu.VMEM((count, LANES, LANES), jnp.bfloat16),
        pltpu.VMEM((count, 4 * LANES, LANES), jnp.bfloat16),
        pltpu.VMEM((2, HEADS // 2, TOK, 2 * LANES), jnp.float32),
        pltpu.VMEM((2, HEADS // 2, 2 * TOK, 2 * LANES), jnp.float32),
        pltpu.VMEM((count, 2 * C, LANES), jnp.bfloat16),
    ]


def tokens_shape(rows):
    return jax.ShapeDtypeStruct((rows, LANES), jnp.bfloat16)


def to_tokens(h, x):
    return pl.pallas_call(
        to_tokens_kernel,
        out_shape=[tokens_shape((HALF + 1) * TOK)] * 2,
        in_specs=[SMEM, pl.BlockSpec(memory_space=pl.ANY)],
        out_specs=[VMEM] * 2,
        scratch_shapes=[
            pltpu.VMEM((2, C, WIN, LANES), jnp.bfloat16),
            pltpu.VMEM((2, C * WIN, LANES), jnp.float32),
            pltpu.VMEM((2, HALF, WIN, WIN, LANES), jnp.float32),
            pltpu.SemaphoreType.DMA((2,)),
        ],
        compiler_params=PARAMS,
        name="to_tokens",
    )(h, x)


def layer_one(chunk, h, own, oth, before, weights):
    first, last = chunk == 0, chunk == len(WINDOWS) - 1
    count = WINDOWS[chunk][1] - WINDOWS[chunk][0]
    width = SHIFTED[chunk][1] - SHIFTED[chunk][0]
    edge = [] if last else [jax.ShapeDtypeStruct((2, WIN, WIN, LANES), jnp.float32)]
    shapes = [tokens_shape(width * TOK // 2)] * 4 + edge
    args = (h, own, oth, *before, *weights)
    return pl.pallas_call(
        functools.partial(layer_one_kernel, count, first, last),
        out_shape=shapes,
        in_specs=[SMEM] + [VMEM] * (len(args) - 1),
        out_specs=[VMEM] * len(shapes),
        scratch_shapes=[
            pltpu.VMEM((2, WIN, (width + 1) * WIN, LANES), jnp.float32),
            pltpu.VMEM((2, 2, width, 4, WIN, LANES), jnp.float32),
            *attention_scratch(count),
        ],
        compiler_params=PARAMS,
        cost_estimate=COST,
        name="layer_one",
    )(*args)


def layer_two(chunk, h, pieces, weights):
    count = SHIFTED[chunk][1] - SHIFTED[chunk][0]
    return pl.pallas_call(
        functools.partial(layer_two_kernel, count),
        out_shape=[tokens_shape(count * TOK // 2)] * 4,
        in_specs=[SMEM] + [VMEM] * 9,
        out_specs=[VMEM] * 4,
        scratch_shapes=attention_scratch(count),
        compiler_params=PARAMS,
        cost_estimate=COST,
        name="layer_two",
    )(h, *pieces, *weights)


def from_tokens(h, pieces):
    return pl.pallas_call(
        from_tokens_kernel,
        out_shape=jax.ShapeDtypeStruct((C, WIN, 2 * LANES), jnp.bfloat16),
        in_specs=[SMEM] + [VMEM] * len(pieces),
        out_specs=pl.BlockSpec(memory_space=pl.ANY),
        scratch_shapes=[
            pltpu.VMEM((WIN, 2 * LANES + WIN, LANES), jnp.float32),
            pltpu.VMEM((2, C * WIN, LANES), jnp.float32),
            pltpu.VMEM((2, C, WIN, LANES), jnp.bfloat16),
            pltpu.SemaphoreType.DMA((2,)),
        ],
        compiler_params=PARAMS,
        name="from_tokens",
    )(h, *pieces)


def prepare_kernel(w_mut, w_slf, w_prj, w_gte, w_upp, w_dwn, *outs):
    row = lax.broadcasted_iota(jnp.int32, (LANES, 3 * C), 0)
    col = lax.broadcasted_iota(jnp.int32, (LANES, 3 * C), 1)
    picks = []
    for part in range(3):
        hit = (col == row + part * C) & (row < C)
        picks.append(jnp.where(hit, 1.0, 0.0).astype(jnp.bfloat16))
    for layer in range(2):
        w_k, w_qv, w_p, w_gu, w_d = outs[5 * layer : 5 * layer + 5]
        for ref in (w_k, w_qv, w_p, w_gu, w_d):
            ref[...] = jnp.zeros(ref.shape, jnp.bfloat16)
        for i, w in enumerate((w_mut, w_slf)):
            w = w[layer]
            span = slice(i * LANES, (i + 1) * LANES)
            w_k[:C, span] = matmul_nt(w, picks[1]).astype(jnp.bfloat16)
            w_qv[span, :C] = matmul_nt(picks[0], w).astype(jnp.bfloat16)
            span = slice((2 + i) * LANES, (3 + i) * LANES)
            w_qv[span, :C] = matmul_nt(picks[2], w).astype(jnp.bfloat16)
        w_p[:, :C] = w_prj[layer]
        w_gu[:C, :FFN] = w_gte[layer]
        w_gu[:C, 2 * LANES : 2 * LANES + FFN] = w_upp[layer]
        w_d[:FFN, :C] = w_dwn[layer]


def prepared(*weights):
    shapes = [
        (LANES, 2 * LANES),
        (4 * LANES, LANES),
        (2 * C, LANES),
        (LANES, 4 * LANES),
        (2 * LANES, LANES),
    ] * 2
    return pl.pallas_call(
        prepare_kernel,
        out_shape=[jax.ShapeDtypeStruct(shape, jnp.bfloat16) for shape in shapes],
        in_specs=[VMEM] * len(weights),
        out_specs=[VMEM] * len(shapes),
        compiler_params=PARAMS,
        name="prepare",
    )(*weights)


def on_device(features, *weights):
    frames, strips = lax.axis_size("frame"), lax.axis_size("strip")

    def send(value, even_step, odd_step, strip_step):
        pairs = []
        for f in range(frames):
            for s in range(strips):
                to = (f + (odd_step if f % 2 else even_step)) % frames
                pairs.append((f * strips + s, to * strips + (s + strip_step) % strips))
        return lax.ppermute(value, ("frame", "strip"), pairs)

    h = (lax.axis_index("frame") % 2).astype(jnp.int32).reshape(1)
    ready = prepared(*weights)
    w_one, w_two = ready[:5], ready[5:]
    parts = to_tokens(h, features[0])
    chunks = range(len(WINDOWS))
    others = [send(parts[k], 1, -1, 0) for k in chunks]
    edge = ()
    pieces = []
    for k in chunks:
        kept_up, kept_lo, moved_up, moved_lo, *edge = layer_one(
            k, h, parts[len(WINDOWS) + k], others[k], edge, w_one
        )
        moved_up = send(moved_up, 2, 2, -1)
        moved_lo = send(moved_lo, 2, 2, 0)
        kept_up = send(kept_up, 0, 0, -1)
        pieces.append((moved_up, moved_lo, kept_up, kept_lo))
    home = []
    for k in chunks:
        far_up, near_up, far_lo, near_lo = layer_two(k, h, pieces[k], w_two)
        far_up = send(far_up, -1, -1, 1)
        near_up = send(near_up, 0, -2, 1)
        far_lo = send(far_lo, -1, -1, 0)
        near_lo = send(near_lo, 0, -2, 0)
        home += [far_up, near_up, far_lo, near_lo]
    return from_tokens(h, home)[None]


def solution(mesh):
    in_specs = (P("frame", None, "strip", None), P(), P(), P(), P(), P(), P())
    out_specs = P("frame", None, "strip", None)
    return jax.shard_map(
        on_device, mesh=mesh, in_specs=in_specs, out_specs=out_specs, check_vma=False
    )
```

```python
import functools

import jax
import jax.numpy as jnp
import numpy as np
from jax import lax
from jax.experimental import pallas as pl
from jax.experimental.pallas import tpu as pltpu
from jax.sharding import PartitionSpec as P

C = 120
HEADS = 6
HEAD = 20
FFN = 240
WIN = 8
LANES = 128
HALF = 16
GROUP = 8
TOK = WIN * WIN
EPS = 1e-05
SHIFTED = ((0, 16),)
WINDOWS = ((0, 17),)
EXP2_SCALE = float(np.log2(np.e) * HEAD**-0.5)
VMEM_LIMIT = 56 * 1024 * 1024


def matmul(a, b):
    return lax.dot_general(a, b, (((1,), (0,)), ((), ())), preferred_element_type=jnp.float32)


def matmul_nt(a, b):
    return lax.dot_general(a, b, (((1,), (1,)), ((), ())), preferred_element_type=jnp.float32)


def matmul_tn(a, b):
    return lax.dot_general(a, b, (((0,), (0,)), ((), ())), preferred_element_type=jnp.float32)


def normed(x):
    lane = lax.broadcasted_iota(jnp.int32, x.shape, 1)
    mean = jnp.sum(x, axis=1, keepdims=True) * (1.0 / C)
    centred = jnp.where(lane < C, x - mean, 0.0)
    spread = jnp.sum(centred * centred, axis=1, keepdims=True) * (1.0 / C)
    return (centred * lax.rsqrt(spread + EPS)).astype(jnp.bfloat16)


def rows_of_head(head):
    low = head * HEAD // 16 * 16
    return low, low + 32


def head_only(q_t, head, lanes=None):
    low, high = rows_of_head(head)
    row = lax.broadcasted_iota(jnp.int32, (high - low, q_t.shape[1]), 0) + low
    keep = (row >= head * HEAD) & (row < head * HEAD + HEAD)
    if lanes is not None:
        lane = lax.broadcasted_iota(jnp.int32, keep.shape, 1)
        keep = keep & ((lane < TOK) if lanes == 0 else (lane >= TOK))
    pieces = [q_t[low:high] * jnp.where(keep, 1.0, 0.0).astype(jnp.bfloat16)]
    if low:
        pieces.insert(0, jnp.zeros((low, q_t.shape[1]), jnp.bfloat16))
    if high < LANES:
        pieces.append(jnp.zeros((LANES - high, q_t.shape[1]), jnp.bfloat16))
    return jnp.concatenate(pieces, axis=0)


def softmax_rows(scores):
    top = jnp.max(scores, axis=0, keepdims=True)
    weights = jnp.exp2((scores - top) * EXP2_SCALE)
    total = jnp.sum(weights, axis=0, keepdims=True)
    return weights * (1.0 / total)


def project_windows(x, w_k, w_qv, mutual_keys, self_keys, qv_t, first):
    normal = normed(x)
    new_keys = matmul(normal, w_k[...]).astype(jnp.bfloat16)
    new_qv = matmul_nt(w_qv[...], normal).astype(jnp.bfloat16)
    for i in range(x.shape[0] // LANES):
        low = i * LANES
        for f in range(2):
            span = slice(f * LANES, (f + 1) * LANES)
            mutual_keys[first + i, :, span] = new_keys[low + f * TOK : low + (f + 1) * TOK, :LANES]
        self_keys[first + i] = new_keys[low : low + LANES, LANES:]
        qv_t[first + i] = new_qv[:, low : low + LANES]


def score_mutual(pair, mutual_keys, qv_t, window):
    heads = (2 * pair, 2 * pair + 1)
    q_t = qv_t[window, :LANES]
    queries = [
        jnp.concatenate([head_only(q_t, head, lanes) for head in heads], axis=1) for lanes in (1, 0)
    ]
    return matmul(mutual_keys[window], jnp.concatenate(queries, axis=0))


def score_self(pair, self_keys, qv_t, window):
    heads = (2 * pair, 2 * pair + 1)
    q_t = qv_t[window, LANES : 2 * LANES]
    queries = jnp.concatenate([head_only(q_t, head) for head in heads], axis=1)
    return matmul(self_keys[window], queries)


def mix_head(head, mutual, own, qv_t, window):
    lane = lax.broadcasted_iota(jnp.int32, (TOK, LANES), 1)
    first = jnp.where(lane < TOK, 1.0, 0.0).astype(jnp.bfloat16)
    second = jnp.where(lane < TOK, 0.0, 1.0).astype(jnp.bfloat16)
    probs = softmax_rows(mutual).astype(jnp.bfloat16)
    probs = jnp.concatenate([probs * second, probs * first], axis=0)
    own = softmax_rows(own).astype(jnp.bfloat16)
    nothing = jnp.zeros((LANES, LANES), jnp.bfloat16)
    probs = jnp.concatenate(
        [jnp.concatenate([probs, nothing], axis=1), jnp.concatenate([nothing, own], axis=1)], axis=0
    )
    low, high = rows_of_head(head)
    values = [qv_t[window, (2 + kind) * LANES + low : (2 + kind) * LANES + high] for kind in range(2)]
    return matmul(jnp.concatenate(values, axis=1), probs)


def by_channel(mixed):
    row = lax.broadcasted_iota(jnp.int32, (8, LANES), 0)
    parts = []
    for head in range(0, HEADS, 2):
        base = head * HEAD
        one, two = mixed[head], mixed[head + 1]
        one_low, two_low = base - rows_of_head(head)[0], base - rows_of_head(head + 1)[0]
        shared = jnp.where(
            row < HEAD - 16, one[one_low + 16 : one_low + 24], two[two_low + 16 : two_low + 24]
        )
        parts += [one[one_low : one_low + 16], shared, two[two_low + 24 : two_low + 40]]
    return jnp.concatenate(parts, axis=0)


def attend(count, mutual_keys, self_keys, qv_t, mutual_scores, self_scores, joined):
    def score(i, pair):
        mutual_scores[i % 2, pair] = score_mutual(pair, mutual_keys, qv_t, i)
        self_scores[i % 2, pair] = score_self(pair, self_keys, qv_t, i)

    for pair in range(HEADS // 2):
        score(0, pair)
    for i in range(count):
        mixed = []
        for pair in range(HEADS // 2):
            if i + 1 < count:
                score(i + 1, pair)
            for j in range(2):
                span = slice(j * LANES, (j + 1) * LANES)
                mutual, own = mutual_scores[i % 2, pair, :, span], self_scores[i % 2, pair, :, span]
                mixed.append(mix_head(2 * pair + j, mutual, own, qv_t, i))
        for kind in range(2):
            span = slice(kind * LANES, (kind + 1) * LANES)
            part = by_channel([block[:, span] for block in mixed])
            joined[i, kind * C : (kind + 1) * C] = part.astype(jnp.bfloat16)


def finished(x, joined, w_prj, w_gu, w_dwn):
    mixed = [matmul_tn(block, w_prj[...]) for block in joined]
    middle = x + jnp.concatenate(mixed, axis=0)
    both = matmul(normed(middle), w_gu[...])
    gate, up = both[:, : 2 * LANES], both[:, 2 * LANES :]
    gelu = 0.5 * gate * (1.0 + lax.erf(gate * float(np.sqrt(0.5))))
    hidden = (gelu * up).astype(jnp.bfloat16)
    return middle + matmul(hidden, w_dwn[...])


def to_tokens_kernel(h_ref, x_ref, send_ref, own_ref, raw, wide, tiles, sems):
    h = h_ref[0]
    copies = []
    for k in range(2):
        half = 1 - h if k == 0 else h
        source = x_ref.at[:, :, pl.ds(pl.multiple_of(half * LANES, LANES), LANES)]
        copies.append(pltpu.make_async_copy(source, raw.at[k], sems.at[k]))
        copies[-1].start()
    pad = jnp.zeros((LANES - C, LANES), jnp.float32)
    for k in range(2):
        copies[k].wait()
        wide[k] = raw[k].astype(jnp.float32).reshape(C * WIN, LANES)
        for r in range(WIN):
            block = wide.at[k][pl.ds(r, C, stride=WIN), :]
            block = jnp.concatenate([block, pad], axis=0).T
            tiles[k, :HALF, r] = block.reshape(HALF, WIN, LANES)
    for k, ref in enumerate((send_ref, own_ref)):
        main = tiles[k, :HALF].reshape(HALF * TOK, LANES)
        ref[: HALF * TOK] = main.astype(jnp.bfloat16)
        ref[HALF * TOK :] = tiles[1 - k, 0].reshape(TOK, LANES).astype(jnp.bfloat16)


def grouped(count):
    parts = max(1, count // GROUP)
    cuts = [count * i // parts for i in range(parts + 1)]
    return [range(low, high) for low, high in zip(cuts[:-1], cuts[1:])]


def layer_one_kernel(count, first, last, h_ref, own_ref, oth_ref, *rest):
    h = h_ref[0]
    if not first:
        before, rest = rest[0], rest[1:]
    w_k, w_qv, w_prj, w_gu, w_dwn = rest[:5]
    outs, rest = rest[5:9], rest[9:]
    if not last:
        after, rest = rest[0], rest[1:]
    flat, tiles, *scratch = rest
    mutual_keys, self_keys, qv_t, joined = *scratch[:3], scratch[-1]
    shift = 0 if first else WIN

    def tokens(group):
        parts = []
        for i in group:
            span = slice(i * TOK, (i + 1) * TOK)
            parts += [own_ref[span], oth_ref[span]]
        return jnp.concatenate(parts, axis=0).astype(jnp.float32)

    for group in grouped(count):
        project_windows(tokens(group), w_k, w_qv, mutual_keys, self_keys, qv_t, group[0])
    attend(count, *scratch)
    if not first:
        flat[:, :, :WIN, :] = before[...]
    for group in grouped(count):
        y = finished(tokens(group), [joined[i] for i in group], w_prj, w_gu, w_dwn)
        y = y.reshape(len(group), 2, WIN, WIN, LANES)
        for j, i in enumerate(group):
            for f in range(2):
                flat[1 - h if f else h, :, shift + i * WIN : shift + (i + 1) * WIN, :] = y[j, f]
    width = shift + (count - 1) * WIN
    if not last:
        after[...] = flat[:, :, width : width + WIN, :]
    for f in range(2):
        for r in range(WIN):
            block = flat[f, r, WIN // 2 : WIN // 2 + width, :]
            tiles[f, r // 4, :, r % 4] = block.reshape(width // WIN, WIN, LANES)
        for k in range(2):
            piece = tiles[f, k].reshape(width * 4, LANES)
            outs[2 * f + k][...] = piece.astype(jnp.bfloat16)


def layer_two_kernel(count, h_ref, *rest):
    even = h_ref[0] == 0
    ins, rest = rest[:4], rest[4:]
    w_k, w_qv, w_prj, w_gu, w_dwn = rest[:5]
    outs, scratch = rest[5:9], rest[9:]
    mutual_keys, self_keys, qv_t, joined = *scratch[:3], scratch[-1]
    half_tok = TOK // 2
    spans = [slice(i * half_tok, (i + 1) * half_tok) for i in range(count)]

    def tokens(group):
        parts = [ref[spans[i]] for i in group for ref in ins]
        return jnp.concatenate(parts, axis=0).astype(jnp.float32)

    for group in grouped(count):
        project_windows(tokens(group), w_k, w_qv, mutual_keys, self_keys, qv_t, group[0])
    attend(count, *scratch)
    for group in grouped(count):
        y = finished(tokens(group), [joined[i] for i in group], w_prj, w_gu, w_dwn)
        for k, i in enumerate(group):
            moved, kept = (y[k * LANES + f * TOK : k * LANES + (f + 1) * TOK] for f in range(2))
            pair = (jnp.where(even, moved, kept), jnp.where(even, kept, moved))
            for f in range(2):
                part = pair[f].astype(jnp.bfloat16)
                for j, out in enumerate((outs[f], outs[2 + f])):
                    out[spans[i]] = part[j * half_tok : (j + 1) * half_tok]


def from_tokens_kernel(h_ref, far_up, near_up, far_lo, near_lo, out_ref, rows, wide, ready, sems):
    edge = WIN // 2

    def place(h):
        for lo, pair in enumerate(((far_up, near_up), (far_lo, near_lo))):
            for half in range(2):
                part = pair[int(half == h)][...].astype(jnp.float32)
                part = part.reshape(HALF, 4, WIN, LANES)
                for r in range(4):
                    low = edge + half * LANES
                    rows[4 * lo + r, low : low + LANES] = part[:, r].reshape(LANES, LANES)

    for h in range(2):

        @pl.when(h_ref[0] == h)
        def _():
            place(h)

    copies = []
    for half in range(2):
        for r in range(WIN):
            if half == 0:
                rows[r, :edge] = rows[r, 2 * LANES : 2 * LANES + edge]
            block = rows[r, half * LANES : (half + 1) * LANES].T
            wide.at[half][pl.ds(r, C, stride=WIN), :] = block[:C]
        ready[half] = wide[half].reshape(C, WIN, LANES).astype(jnp.bfloat16)
        target = out_ref.at[:, :, half * LANES : (half + 1) * LANES]
        copies.append(pltpu.make_async_copy(ready.at[half], target, sems.at[half]))
        copies[-1].start()
    for copy in copies:
        copy.wait()


VMEM = pl.BlockSpec(memory_space=pltpu.VMEM)
SMEM = pl.BlockSpec(memory_space=pltpu.SMEM)
COST = pl.CostEstimate(flops=8 * 10**9, bytes_accessed=2**20, transcendentals=2**20)
PARAMS = pltpu.CompilerParams(vmem_limit_bytes=VMEM_LIMIT)


def attention_scratch(count):
    return [
        pltpu.VMEM((count, TOK, 2 * LANES), jnp.bfloat16),
        pltpu.VMEM((count, LANES, LANES), jnp.bfloat16),
        pltpu.VMEM((count, 4 * LANES, LANES), jnp.bfloat16),
        pltpu.VMEM((2, HEADS // 2, TOK, 2 * LANES), jnp.float32),
        pltpu.VMEM((2, HEADS // 2, 2 * TOK, 2 * LANES), jnp.float32),
        pltpu.VMEM((count, 2 * C, LANES), jnp.bfloat16),
    ]


def tokens_shape(rows):
    return pltpu.VMEM((rows, LANES), jnp.bfloat16)


def in_vmem(*arrays):
    return [pltpu.with_memory_space_constraint(array, pltpu.VMEM) for array in arrays]


def to_tokens(h, x):
    return pl.pallas_call(
        to_tokens_kernel,
        out_shape=[tokens_shape((HALF + 1) * TOK)] * 2,
        in_specs=[SMEM, pl.BlockSpec(memory_space=pl.ANY)],
        out_specs=[VMEM] * 2,
        scratch_shapes=[
            pltpu.VMEM((2, C, WIN, LANES), jnp.bfloat16),
            pltpu.VMEM((2, C * WIN, LANES), jnp.float32),
            pltpu.VMEM((2, HALF, WIN, WIN, LANES), jnp.float32),
            pltpu.SemaphoreType.DMA((2,)),
        ],
        compiler_params=PARAMS,
        name="to_tokens",
    )(h, x)


def layer_one(chunk, h, own, oth, before, weights):
    first, last = chunk == 0, chunk == len(WINDOWS) - 1
    count = WINDOWS[chunk][1] - WINDOWS[chunk][0]
    width = SHIFTED[chunk][1] - SHIFTED[chunk][0]
    edge = [] if last else [jax.ShapeDtypeStruct((2, WIN, WIN, LANES), jnp.float32)]
    shapes = [tokens_shape(width * TOK // 2)] * 4 + edge
    args = (h, *in_vmem(own, oth, *before, *weights))
    return pl.pallas_call(
        functools.partial(layer_one_kernel, count, first, last),
        out_shape=shapes,
        in_specs=[SMEM] + [VMEM] * (len(args) - 1),
        out_specs=[VMEM] * len(shapes),
        scratch_shapes=[
            pltpu.VMEM((2, WIN, (width + 1) * WIN, LANES), jnp.float32),
            pltpu.VMEM((2, 2, width, 4, WIN, LANES), jnp.float32),
            *attention_scratch(count),
        ],
        compiler_params=PARAMS,
        cost_estimate=COST,
        name="layer_one",
    )(*args)


def layer_two(chunk, h, pieces, weights):
    count = SHIFTED[chunk][1] - SHIFTED[chunk][0]
    return pl.pallas_call(
        functools.partial(layer_two_kernel, count),
        out_shape=[tokens_shape(count * TOK // 2)] * 4,
        in_specs=[SMEM] + [VMEM] * 9,
        out_specs=[VMEM] * 4,
        scratch_shapes=attention_scratch(count),
        compiler_params=PARAMS,
        cost_estimate=COST,
        name="layer_two",
    )(h, *in_vmem(*pieces, *weights))


def from_tokens(h, pieces):
    return pl.pallas_call(
        from_tokens_kernel,
        out_shape=jax.ShapeDtypeStruct((C, WIN, 2 * LANES), jnp.bfloat16),
        in_specs=[SMEM] + [VMEM] * len(pieces),
        out_specs=pl.BlockSpec(memory_space=pl.ANY),
        scratch_shapes=[
            pltpu.VMEM((WIN, 2 * LANES + WIN, LANES), jnp.float32),
            pltpu.VMEM((2, C * WIN, LANES), jnp.float32),
            pltpu.VMEM((2, C, WIN, LANES), jnp.bfloat16),
            pltpu.SemaphoreType.DMA((2,)),
        ],
        compiler_params=PARAMS,
        name="from_tokens",
    )(h, *in_vmem(*pieces))


def prepare_kernel(w_mut, w_slf, w_prj, w_gte, w_upp, w_dwn, *outs):
    row = lax.broadcasted_iota(jnp.int32, (LANES, 3 * C), 0)
    col = lax.broadcasted_iota(jnp.int32, (LANES, 3 * C), 1)
    picks = []
    for part in range(3):
        hit = (col == row + part * C) & (row < C)
        picks.append(jnp.where(hit, 1.0, 0.0).astype(jnp.bfloat16))
    for layer in range(2):
        w_k, w_qv, w_p, w_gu, w_d = outs[5 * layer : 5 * layer + 5]
        for ref in (w_k, w_qv, w_p, w_gu, w_d):
            ref[...] = jnp.zeros(ref.shape, jnp.bfloat16)
        for i, w in enumerate((w_mut, w_slf)):
            w = w[layer]
            span = slice(i * LANES, (i + 1) * LANES)
            w_k[:C, span] = matmul_nt(w, picks[1]).astype(jnp.bfloat16)
            w_qv[span, :C] = matmul_nt(picks[0], w).astype(jnp.bfloat16)
            span = slice((2 + i) * LANES, (3 + i) * LANES)
            w_qv[span, :C] = matmul_nt(picks[2], w).astype(jnp.bfloat16)
        w_p[:, :C] = w_prj[layer]
        w_gu[:C, :FFN] = w_gte[layer]
        w_gu[:C, 2 * LANES : 2 * LANES + FFN] = w_upp[layer]
        w_d[:FFN, :C] = w_dwn[layer]


def prepared(*weights):
    shapes = [
        (LANES, 2 * LANES),
        (4 * LANES, LANES),
        (2 * C, LANES),
        (LANES, 4 * LANES),
        (2 * LANES, LANES),
    ] * 2
    return pl.pallas_call(
        prepare_kernel,
        out_shape=[pltpu.VMEM(shape, jnp.bfloat16) for shape in shapes],
        in_specs=[VMEM] * len(weights),
        out_specs=[VMEM] * len(shapes),
        compiler_params=PARAMS,
        name="prepare",
    )(*weights)


def on_device(features, *weights):
    frames, strips = lax.axis_size("frame"), lax.axis_size("strip")

    def send(value, even_step, odd_step, strip_step):
        pairs = []
        for f in range(frames):
            for s in range(strips):
                to = (f + (odd_step if f % 2 else even_step)) % frames
                pairs.append((f * strips + s, to * strips + (s + strip_step) % strips))
        return lax.ppermute(value, ("frame", "strip"), pairs)

    h = (lax.axis_index("frame") % 2).astype(jnp.int32).reshape(1)
    ready = prepared(*weights)
    w_one, w_two = ready[:5], ready[5:]
    parts = to_tokens(h, features[0])
    chunks = range(len(WINDOWS))
    others = [send(parts[k], 1, -1, 0) for k in chunks]
    edge = ()
    pieces = []
    for k in chunks:
        kept_up, kept_lo, moved_up, moved_lo, *edge = layer_one(
            k, h, parts[len(WINDOWS) + k], others[k], edge, w_one
        )
        moved_up = send(moved_up, 2, 2, -1)
        moved_lo = send(moved_lo, 2, 2, 0)
        kept_up = send(kept_up, 0, 0, -1)
        pieces.append((moved_up, moved_lo, kept_up, kept_lo))
    home = []
    for k in chunks:
        far_up, near_up, far_lo, near_lo = layer_two(k, h, pieces[k], w_two)
        far_up = send(far_up, -1, -1, 1)
        near_up = send(near_up, 0, -2, 1)
        far_lo = send(far_lo, -1, -1, 0)
        near_lo = send(near_lo, 0, -2, 0)
        home += [far_up, near_up, far_lo, near_lo]
    return from_tokens(h, home)[None]


def solution(mesh):
    in_specs = (P("frame", None, "strip", None), P(), P(), P(), P(), P(), P())
    out_specs = P("frame", None, "strip", None)
    return jax.shard_map(
        on_device, mesh=mesh, in_specs=in_specs, out_specs=out_specs, check_vma=False
    )
```

```python
import functools

import jax
import jax.numpy as jnp
import numpy as np
from jax import lax
from jax.experimental import pallas as pl
from jax.experimental.pallas import tpu as pltpu
from jax.sharding import PartitionSpec as P

C = 120
HEADS = 6
HEAD = 20
FFN = 240
WIN = 8
LANES = 128
HALF = 16
GROUP = 8
TOK = WIN * WIN
EPS = 1e-05
SHIFTED = ((0, 16),)
WINDOWS = ((0, 17),)
EXP2_SCALE = float(np.log2(np.e) * HEAD**-0.5)
VMEM_LIMIT = 56 * 1024 * 1024


def matmul(a, b):
    return lax.dot_general(a, b, (((1,), (0,)), ((), ())), preferred_element_type=jnp.float32)


def matmul_nt(a, b):
    return lax.dot_general(a, b, (((1,), (1,)), ((), ())), preferred_element_type=jnp.float32)


def matmul_tn(a, b):
    return lax.dot_general(a, b, (((0,), (0,)), ((), ())), preferred_element_type=jnp.float32)


def normed(x):
    lane = lax.broadcasted_iota(jnp.int32, x.shape, 1)
    mean = jnp.sum(x, axis=1, keepdims=True) * (1.0 / C)
    centred = jnp.where(lane < C, x - mean, 0.0)
    spread = jnp.sum(centred * centred, axis=1, keepdims=True) * (1.0 / C)
    return (centred * lax.rsqrt(spread + EPS)).astype(jnp.bfloat16)


def rows_of_head(head):
    low = head * HEAD // 16 * 16
    return low, low + 32


def head_only(q_t, head, lanes=None):
    low, high = rows_of_head(head)
    row = lax.broadcasted_iota(jnp.int32, (high - low, q_t.shape[1]), 0) + low
    keep = (row >= head * HEAD) & (row < head * HEAD + HEAD)
    if lanes is not None:
        lane = lax.broadcasted_iota(jnp.int32, keep.shape, 1)
        keep = keep & ((lane < TOK) if lanes == 0 else (lane >= TOK))
    pieces = [q_t[low:high] * jnp.where(keep, 1.0, 0.0).astype(jnp.bfloat16)]
    if low:
        pieces.insert(0, jnp.zeros((low, q_t.shape[1]), jnp.bfloat16))
    if high < LANES:
        pieces.append(jnp.zeros((LANES - high, q_t.shape[1]), jnp.bfloat16))
    return jnp.concatenate(pieces, axis=0)


def softmax_rows(scores):
    top = jnp.max(scores, axis=0, keepdims=True)
    weights = jnp.exp2((scores - top) * EXP2_SCALE)
    total = jnp.sum(weights, axis=0, keepdims=True)
    return weights * (1.0 / total)


def project_windows(x, w_k, w_qv, mutual_keys, self_keys, qv_t, first):
    normal = normed(x)
    new_keys = matmul(normal, w_k[...]).astype(jnp.bfloat16)
    new_qv = matmul_nt(w_qv[...], normal).astype(jnp.bfloat16)
    for i in range(x.shape[0] // LANES):
        low = i * LANES
        for f in range(2):
            span = slice(f * LANES, (f + 1) * LANES)
            mutual_keys[first + i, :, span] = new_keys[low + f * TOK : low + (f + 1) * TOK, :LANES]
        self_keys[first + i] = new_keys[low : low + LANES, LANES:]
        qv_t[first + i] = new_qv[:, low : low + LANES]


def score_mutual(pair, mutual_keys, qv_t, window):
    heads = (2 * pair, 2 * pair + 1)
    q_t = qv_t[window, :LANES]
    queries = [
        jnp.concatenate([head_only(q_t, head, lanes) for head in heads], axis=1) for lanes in (1, 0)
    ]
    return matmul(mutual_keys[window], jnp.concatenate(queries, axis=0))


def score_self(pair, self_keys, qv_t, window):
    heads = (2 * pair, 2 * pair + 1)
    q_t = qv_t[window, LANES : 2 * LANES]
    queries = jnp.concatenate([head_only(q_t, head) for head in heads], axis=1)
    return matmul(self_keys[window], queries)


def mix_head(head, mutual, own, qv_t, window):
    lane = lax.broadcasted_iota(jnp.int32, (TOK, LANES), 1)
    first = jnp.where(lane < TOK, 1.0, 0.0).astype(jnp.bfloat16)
    second = jnp.where(lane < TOK, 0.0, 1.0).astype(jnp.bfloat16)
    probs = softmax_rows(mutual).astype(jnp.bfloat16)
    probs = jnp.concatenate([probs * second, probs * first], axis=0)
    own = softmax_rows(own).astype(jnp.bfloat16)
    nothing = jnp.zeros((LANES, LANES), jnp.bfloat16)
    probs = jnp.concatenate(
        [jnp.concatenate([probs, nothing], axis=1), jnp.concatenate([nothing, own], axis=1)], axis=0
    )
    low, high = rows_of_head(head)
    values = [qv_t[window, (2 + kind) * LANES + low : (2 + kind) * LANES + high] for kind in range(2)]
    return matmul(jnp.concatenate(values, axis=1), probs)


def by_channel(mixed):
    row = lax.broadcasted_iota(jnp.int32, (8, LANES), 0)
    parts = []
    for head in range(0, HEADS, 2):
        base = head * HEAD
        one, two = mixed[head], mixed[head + 1]
        one_low, two_low = base - rows_of_head(head)[0], base - rows_of_head(head + 1)[0]
        shared = jnp.where(
            row < HEAD - 16, one[one_low + 16 : one_low + 24], two[two_low + 16 : two_low + 24]
        )
        parts += [one[one_low : one_low + 16], shared, two[two_low + 24 : two_low + 40]]
    return jnp.concatenate(parts, axis=0)


def attend(count, mutual_keys, self_keys, qv_t, mutual_scores, self_scores, joined):
    def score(i, pair):
        mutual_scores[i % 2, pair] = score_mutual(pair, mutual_keys, qv_t, i)
        self_scores[i % 2, pair] = score_self(pair, self_keys, qv_t, i)

    for pair in range(HEADS // 2):
        score(0, pair)
    for i in range(count):
        mixed = []
        for pair in range(HEADS // 2):
            if i + 1 < count:
                score(i + 1, pair)
            for j in range(2):
                span = slice(j * LANES, (j + 1) * LANES)
                mutual, own = mutual_scores[i % 2, pair, :, span], self_scores[i % 2, pair, :, span]
                mixed.append(mix_head(2 * pair + j, mutual, own, qv_t, i))
        for kind in range(2):
            span = slice(kind * LANES, (kind + 1) * LANES)
            part = by_channel([block[:, span] for block in mixed])
            joined[i, kind * C : (kind + 1) * C] = part.astype(jnp.bfloat16)


def finished(x, joined, w_prj, w_gu, w_dwn):
    mixed = [matmul_tn(block, w_prj[...]) for block in joined]
    middle = x + jnp.concatenate(mixed, axis=0)
    both = matmul(normed(middle), w_gu[...])
    gate, up = both[:, : 2 * LANES], both[:, 2 * LANES :]
    gelu = 0.5 * gate * (1.0 + lax.erf(gate * float(np.sqrt(0.5))))
    hidden = (gelu * up).astype(jnp.bfloat16)
    return middle + matmul(hidden, w_dwn[...])


def to_tokens_kernel(h_ref, x_ref, send_ref, own_ref, raw, wide, tiles, sems):
    h = h_ref[0]
    copies = []
    for k in range(2):
        half = 1 - h if k == 0 else h
        source = x_ref.at[:, :, pl.ds(pl.multiple_of(half * LANES, LANES), LANES)]
        copies.append(pltpu.make_async_copy(source, raw.at[k], sems.at[k]))
        copies[-1].start()
    pad = jnp.zeros((LANES - C, LANES), jnp.float32)
    for k in range(2):
        copies[k].wait()
        wide[k] = raw[k].astype(jnp.float32).reshape(C * WIN, LANES)
        for r in range(WIN):
            block = wide.at[k][pl.ds(r, C, stride=WIN), :]
            block = jnp.concatenate([block, pad], axis=0).T
            tiles[k, :HALF, r] = block.reshape(HALF, WIN, LANES)
    for k, ref in enumerate((send_ref, own_ref)):
        main = tiles[k, :HALF].reshape(HALF * TOK, LANES)
        ref[: HALF * TOK] = main.astype(jnp.bfloat16)
        ref[HALF * TOK :] = tiles[1 - k, 0].reshape(TOK, LANES).astype(jnp.bfloat16)


def grouped(count):
    parts = max(1, count // GROUP)
    cuts = [count * i // parts for i in range(parts + 1)]
    return [range(low, high) for low, high in zip(cuts[:-1], cuts[1:])]


def layer_one_kernel(count, first, last, h_ref, own_ref, oth_ref, *rest):
    h = h_ref[0]
    if not first:
        before, rest = rest[0], rest[1:]
    w_k, w_qv, w_prj, w_gu, w_dwn = rest[:5]
    outs, rest = rest[5:9], rest[9:]
    if not last:
        after, rest = rest[0], rest[1:]
    flat, tiles, *scratch = rest
    mutual_keys, self_keys, qv_t, joined = *scratch[:3], scratch[-1]
    shift = 0 if first else WIN

    def tokens(group):
        parts = []
        for i in group:
            span = slice(i * TOK, (i + 1) * TOK)
            parts += [own_ref[span], oth_ref[span]]
        return jnp.concatenate(parts, axis=0).astype(jnp.float32)

    for group in grouped(count):
        project_windows(tokens(group), w_k, w_qv, mutual_keys, self_keys, qv_t, group[0])
    attend(count, *scratch)
    if not first:
        flat[:, :, :WIN, :] = before[...]
    for group in grouped(count):
        y = finished(tokens(group), [joined[i] for i in group], w_prj, w_gu, w_dwn)
        y = y.reshape(len(group), 2, WIN, WIN, LANES)
        for j, i in enumerate(group):
            for f in range(2):
                flat[1 - h if f else h, :, shift + i * WIN : shift + (i + 1) * WIN, :] = y[j, f]
    width = shift + (count - 1) * WIN
    if not last:
        after[...] = flat[:, :, width : width + WIN, :]
    for f in range(2):
        for r in range(WIN):
            block = flat[f, r, WIN // 2 : WIN // 2 + width, :]
            tiles[f, r // 4, :, r % 4] = block.reshape(width // WIN, WIN, LANES)
        for k in range(2):
            piece = tiles[f, k].reshape(width * 4, LANES)
            outs[2 * f + k][...] = piece.astype(jnp.bfloat16)


def layer_two_kernel(count, h_ref, *rest):
    even = h_ref[0] == 0
    ins, rest = rest[:4], rest[4:]
    w_k, w_qv, w_prj, w_gu, w_dwn = rest[:5]
    outs, scratch = rest[5:9], rest[9:]
    mutual_keys, self_keys, qv_t, joined = *scratch[:3], scratch[-1]
    half_tok = TOK // 2
    spans = [slice(i * half_tok, (i + 1) * half_tok) for i in range(count)]

    def tokens(group):
        parts = [ref[spans[i]] for i in group for ref in ins]
        return jnp.concatenate(parts, axis=0).astype(jnp.float32)

    for group in grouped(count):
        project_windows(tokens(group), w_k, w_qv, mutual_keys, self_keys, qv_t, group[0])
    attend(count, *scratch)
    for group in grouped(count):
        y = finished(tokens(group), [joined[i] for i in group], w_prj, w_gu, w_dwn)
        for k, i in enumerate(group):
            moved, kept = (y[k * LANES + f * TOK : k * LANES + (f + 1) * TOK] for f in range(2))
            pair = (jnp.where(even, moved, kept), jnp.where(even, kept, moved))
            for f in range(2):
                part = pair[f].astype(jnp.bfloat16)
                for j, out in enumerate((outs[2 * f], outs[2 * f + 1])):
                    out[spans[i]] = part[j * half_tok : (j + 1) * half_tok]


def from_tokens_kernel(h_ref, far_up, far_lo, near_up, near_lo, out_ref, rows, wide, ready, sems):
    edge = WIN // 2

    def place(h):
        for lo, pair in enumerate(((far_up, near_up), (far_lo, near_lo))):
            for half in range(2):
                part = pair[int(half == h)][...].astype(jnp.float32)
                part = part.reshape(HALF, 4, WIN, LANES)
                for r in range(4):
                    low = edge + half * LANES
                    rows[4 * lo + r, low : low + LANES] = part[:, r].reshape(LANES, LANES)

    for h in range(2):

        @pl.when(h_ref[0] == h)
        def _():
            place(h)

    copies = []
    for half in range(2):
        for r in range(WIN):
            if half == 0:
                rows[r, :edge] = rows[r, 2 * LANES : 2 * LANES + edge]
            block = rows[r, half * LANES : (half + 1) * LANES].T
            wide.at[half][pl.ds(r, C, stride=WIN), :] = block[:C]
        ready[half] = wide[half].reshape(C, WIN, LANES).astype(jnp.bfloat16)
        target = out_ref.at[:, :, half * LANES : (half + 1) * LANES]
        copies.append(pltpu.make_async_copy(ready.at[half], target, sems.at[half]))
        copies[-1].start()
    for copy in copies:
        copy.wait()


VMEM = pl.BlockSpec(memory_space=pltpu.VMEM)
SMEM = pl.BlockSpec(memory_space=pltpu.SMEM)
COST = pl.CostEstimate(flops=8 * 10**9, bytes_accessed=2**20, transcendentals=2**20)
PARAMS = pltpu.CompilerParams(vmem_limit_bytes=VMEM_LIMIT)


def attention_scratch(count):
    return [
        pltpu.VMEM((count, TOK, 2 * LANES), jnp.bfloat16),
        pltpu.VMEM((count, LANES, LANES), jnp.bfloat16),
        pltpu.VMEM((count, 4 * LANES, LANES), jnp.bfloat16),
        pltpu.VMEM((2, HEADS // 2, TOK, 2 * LANES), jnp.float32),
        pltpu.VMEM((2, HEADS // 2, 2 * TOK, 2 * LANES), jnp.float32),
        pltpu.VMEM((count, 2 * C, LANES), jnp.bfloat16),
    ]


def tokens_shape(rows):
    return pltpu.VMEM((rows, LANES), jnp.bfloat16)


def in_vmem(*arrays):
    return [pltpu.with_memory_space_constraint(array, pltpu.VMEM) for array in arrays]


def to_tokens(h, x):
    return pl.pallas_call(
        to_tokens_kernel,
        out_shape=[tokens_shape((HALF + 1) * TOK)] * 2,
        in_specs=[SMEM, pl.BlockSpec(memory_space=pl.ANY)],
        out_specs=[VMEM] * 2,
        scratch_shapes=[
            pltpu.VMEM((2, C, WIN, LANES), jnp.bfloat16),
            pltpu.VMEM((2, C * WIN, LANES), jnp.float32),
            pltpu.VMEM((2, HALF, WIN, WIN, LANES), jnp.float32),
            pltpu.SemaphoreType.DMA((2,)),
        ],
        compiler_params=PARAMS,
        name="to_tokens",
    )(h, x)


def layer_one(chunk, h, own, oth, before, weights):
    first, last = chunk == 0, chunk == len(WINDOWS) - 1
    count = WINDOWS[chunk][1] - WINDOWS[chunk][0]
    width = SHIFTED[chunk][1] - SHIFTED[chunk][0]
    edge = [] if last else [jax.ShapeDtypeStruct((2, WIN, WIN, LANES), jnp.float32)]
    shapes = [tokens_shape(width * TOK // 2)] * 4 + edge
    args = (h, *in_vmem(own, oth, *before, *weights))
    return pl.pallas_call(
        functools.partial(layer_one_kernel, count, first, last),
        out_shape=shapes,
        in_specs=[SMEM] + [VMEM] * (len(args) - 1),
        out_specs=[VMEM] * len(shapes),
        scratch_shapes=[
            pltpu.VMEM((2, WIN, (width + 1) * WIN, LANES), jnp.float32),
            pltpu.VMEM((2, 2, width, 4, WIN, LANES), jnp.float32),
            *attention_scratch(count),
        ],
        compiler_params=PARAMS,
        cost_estimate=COST,
        name="layer_one",
    )(*args)


def layer_two(chunk, h, pieces, weights):
    count = SHIFTED[chunk][1] - SHIFTED[chunk][0]
    return pl.pallas_call(
        functools.partial(layer_two_kernel, count),
        out_shape=[tokens_shape(count * TOK // 2)] * 4,
        in_specs=[SMEM] + [VMEM] * 9,
        out_specs=[VMEM] * 4,
        scratch_shapes=attention_scratch(count),
        compiler_params=PARAMS,
        cost_estimate=COST,
        name="layer_two",
    )(h, *in_vmem(*pieces, *weights))


def from_tokens(h, pieces):
    return pl.pallas_call(
        from_tokens_kernel,
        out_shape=jax.ShapeDtypeStruct((C, WIN, 2 * LANES), jnp.bfloat16),
        in_specs=[SMEM] + [VMEM] * len(pieces),
        out_specs=pl.BlockSpec(memory_space=pl.ANY),
        scratch_shapes=[
            pltpu.VMEM((WIN, 2 * LANES + WIN, LANES), jnp.float32),
            pltpu.VMEM((2, C * WIN, LANES), jnp.float32),
            pltpu.VMEM((2, C, WIN, LANES), jnp.bfloat16),
            pltpu.SemaphoreType.DMA((2,)),
        ],
        compiler_params=PARAMS,
        name="from_tokens",
    )(h, *in_vmem(*pieces))


def prepare_kernel(w_mut, w_slf, w_prj, w_gte, w_upp, w_dwn, *outs):
    row = lax.broadcasted_iota(jnp.int32, (LANES, 3 * C), 0)
    col = lax.broadcasted_iota(jnp.int32, (LANES, 3 * C), 1)
    picks = []
    for part in range(3):
        hit = (col == row + part * C) & (row < C)
        picks.append(jnp.where(hit, 1.0, 0.0).astype(jnp.bfloat16))
    for layer in range(2):
        w_k, w_qv, w_p, w_gu, w_d = outs[5 * layer : 5 * layer + 5]
        for ref in (w_k, w_qv, w_p, w_gu, w_d):
            ref[...] = jnp.zeros(ref.shape, jnp.bfloat16)
        for i, w in enumerate((w_mut, w_slf)):
            w = w[layer]
            span = slice(i * LANES, (i + 1) * LANES)
            w_k[:C, span] = matmul_nt(w, picks[1]).astype(jnp.bfloat16)
            w_qv[span, :C] = matmul_nt(picks[0], w).astype(jnp.bfloat16)
            span = slice((2 + i) * LANES, (3 + i) * LANES)
            w_qv[span, :C] = matmul_nt(picks[2], w).astype(jnp.bfloat16)
        w_p[:, :C] = w_prj[layer]
        w_gu[:C, :FFN] = w_gte[layer]
        w_gu[:C, 2 * LANES : 2 * LANES + FFN] = w_upp[layer]
        w_d[:FFN, :C] = w_dwn[layer]


def prepared(*weights):
    shapes = [
        (LANES, 2 * LANES),
        (4 * LANES, LANES),
        (2 * C, LANES),
        (LANES, 4 * LANES),
        (2 * LANES, LANES),
    ] * 2
    return pl.pallas_call(
        prepare_kernel,
        out_shape=[pltpu.VMEM(shape, jnp.bfloat16) for shape in shapes],
        in_specs=[VMEM] * len(weights),
        out_specs=[VMEM] * len(shapes),
        compiler_params=PARAMS,
        name="prepare",
    )(*weights)


def on_device(features, *weights):
    frames, strips = lax.axis_size("frame"), lax.axis_size("strip")

    def send(value, even_step, odd_step, strip_step):
        pairs = []
        for f in range(frames):
            for s in range(strips):
                to = (f + (odd_step if f % 2 else even_step)) % frames
                pairs.append((f * strips + s, to * strips + (s + strip_step) % strips))
        return lax.ppermute(value, ("frame", "strip"), pairs)

    h = (lax.axis_index("frame") % 2).astype(jnp.int32).reshape(1)
    ready = prepared(*weights)
    w_one, w_two = ready[:5], ready[5:]
    parts = to_tokens(h, features[0])
    chunks = range(len(WINDOWS))
    others = [send(parts[k], 1, -1, 0) for k in chunks]
    edge = ()
    pieces = []
    for k in chunks:
        kept_up, kept_lo, moved_up, moved_lo, *edge = layer_one(
            k, h, parts[len(WINDOWS) + k], others[k], edge, w_one
        )
        moved_up = send(moved_up, 2, 2, -1)
        moved_lo = send(moved_lo, 2, 2, 0)
        kept_up = send(kept_up, 0, 0, -1)
        pieces.append((moved_up, moved_lo, kept_up, kept_lo))
    home = []
    for k in chunks:
        far_up, far_lo, near_up, near_lo = layer_two(k, h, pieces[k], w_two)
        far_up = send(far_up, -1, -1, 1)
        far_lo = send(far_lo, -1, -1, 0)
        near_up = send(near_up, 0, -2, 1)
        near_lo = send(near_lo, 0, -2, 0)
        home += [far_up, far_lo, near_up, near_lo]
    return from_tokens(h, home)[None]


def solution(mesh):
    in_specs = (P("frame", None, "strip", None), P(), P(), P(), P(), P(), P())
    out_specs = P("frame", None, "strip", None)
    return jax.shard_map(
        on_device, mesh=mesh, in_specs=in_specs, out_specs=out_specs, check_vma=False
    )
```

```python
import functools

import jax
import jax.numpy as jnp
import numpy as np
from jax import lax
from jax.experimental import pallas as pl
from jax.experimental.pallas import tpu as pltpu
from jax.sharding import PartitionSpec as P

C = 120
HEADS = 6
HEAD = 20
FFN = 240
WIN = 8
LANES = 128
HALF = 16
GROUP = 8
TOK = WIN * WIN
EPS = 1e-05
SHIFTED = ((0, 16),)
WINDOWS = ((0, 17),)
EXP2_SCALE = float(np.log2(np.e) * HEAD**-0.5)
VMEM_LIMIT = 56 * 1024 * 1024


def matmul(a, b):
    return lax.dot_general(a, b, (((1,), (0,)), ((), ())), preferred_element_type=jnp.float32)


def matmul_nt(a, b):
    return lax.dot_general(a, b, (((1,), (1,)), ((), ())), preferred_element_type=jnp.float32)


def matmul_tn(a, b):
    return lax.dot_general(a, b, (((0,), (0,)), ((), ())), preferred_element_type=jnp.float32)


def normed(x):
    lane = lax.broadcasted_iota(jnp.int32, x.shape, 1)
    mean = jnp.sum(x, axis=1, keepdims=True) * (1.0 / C)
    centred = jnp.where(lane < C, x - mean, 0.0)
    spread = jnp.sum(centred * centred, axis=1, keepdims=True) * (1.0 / C)
    return (centred * lax.rsqrt(spread + EPS)).astype(jnp.bfloat16)


def rows_of_head(head):
    low = head * HEAD // 16 * 16
    return low, low + 32


def head_only(q_t, head, lanes=None):
    low, high = rows_of_head(head)
    row = lax.broadcasted_iota(jnp.int32, (high - low, q_t.shape[1]), 0) + low
    keep = (row >= head * HEAD) & (row < head * HEAD + HEAD)
    if lanes is not None:
        lane = lax.broadcasted_iota(jnp.int32, keep.shape, 1)
        keep = keep & ((lane < TOK) if lanes == 0 else (lane >= TOK))
    pieces = [q_t[low:high] * jnp.where(keep, 1.0, 0.0).astype(jnp.bfloat16)]
    if low:
        pieces.insert(0, jnp.zeros((low, q_t.shape[1]), jnp.bfloat16))
    if high < LANES:
        pieces.append(jnp.zeros((LANES - high, q_t.shape[1]), jnp.bfloat16))
    return jnp.concatenate(pieces, axis=0)


def softmax_rows(scores):
    top = jnp.max(scores, axis=0, keepdims=True)
    weights = jnp.exp2((scores - top) * EXP2_SCALE)
    total = jnp.sum(weights, axis=0, keepdims=True)
    return weights * (1.0 / total)


def project_windows(x, w_k, w_qv, mutual_keys, self_keys, qv_t, first):
    normal = normed(x)
    new_keys = matmul(normal, w_k[...]).astype(jnp.bfloat16)
    new_qv = matmul_nt(w_qv[...], normal).astype(jnp.bfloat16)
    for i in range(x.shape[0] // LANES):
        low = i * LANES
        for f in range(2):
            span = slice(f * LANES, (f + 1) * LANES)
            mutual_keys[first + i, :, span] = new_keys[low + f * TOK : low + (f + 1) * TOK, :LANES]
        self_keys[first + i] = new_keys[low : low + LANES, LANES:]
        qv_t[first + i] = new_qv[:, low : low + LANES]


def score_mutual(pair, mutual_keys, qv_t, window):
    heads = (2 * pair, 2 * pair + 1)
    q_t = qv_t[window, :LANES]
    queries = [
        jnp.concatenate([head_only(q_t, head, lanes) for head in heads], axis=1) for lanes in (1, 0)
    ]
    return matmul(mutual_keys[window], jnp.concatenate(queries, axis=0))


def score_self(pair, self_keys, qv_t, window):
    heads = (2 * pair, 2 * pair + 1)
    q_t = qv_t[window, LANES : 2 * LANES]
    queries = jnp.concatenate([head_only(q_t, head) for head in heads], axis=1)
    return matmul(self_keys[window], queries)


def mix_head(head, mutual, own, qv_t, window):
    lane = lax.broadcasted_iota(jnp.int32, (TOK, LANES), 1)
    first = jnp.where(lane < TOK, 1.0, 0.0).astype(jnp.bfloat16)
    second = jnp.where(lane < TOK, 0.0, 1.0).astype(jnp.bfloat16)
    probs = softmax_rows(mutual).astype(jnp.bfloat16)
    probs = jnp.concatenate([probs * second, probs * first], axis=0)
    own = softmax_rows(own).astype(jnp.bfloat16)
    nothing = jnp.zeros((LANES, LANES), jnp.bfloat16)
    probs = jnp.concatenate(
        [jnp.concatenate([probs, nothing], axis=1), jnp.concatenate([nothing, own], axis=1)], axis=0
    )
    low, high = rows_of_head(head)
    values = [qv_t[window, (2 + kind) * LANES + low : (2 + kind) * LANES + high] for kind in range(2)]
    return matmul(jnp.concatenate(values, axis=1), probs)


def by_channel(mixed):
    row = lax.broadcasted_iota(jnp.int32, (8, LANES), 0)
    parts = []
    for head in range(0, HEADS, 2):
        base = head * HEAD
        one, two = mixed[head], mixed[head + 1]
        one_low, two_low = base - rows_of_head(head)[0], base - rows_of_head(head + 1)[0]
        shared = jnp.where(
            row < HEAD - 16, one[one_low + 16 : one_low + 24], two[two_low + 16 : two_low + 24]
        )
        parts += [one[one_low : one_low + 16], shared, two[two_low + 24 : two_low + 40]]
    return jnp.concatenate(parts, axis=0)


def attend(count, mutual_keys, self_keys, qv_t, mutual_scores, self_scores, joined):
    def score(i, pair):
        mutual_scores[i % 2, pair] = score_mutual(pair, mutual_keys, qv_t, i)
        self_scores[i % 2, pair] = score_self(pair, self_keys, qv_t, i)

    for pair in range(HEADS // 2):
        score(0, pair)
    for i in range(count):
        mixed = []
        for pair in range(HEADS // 2):
            if i + 1 < count:
                score(i + 1, pair)
            for j in range(2):
                span = slice(j * LANES, (j + 1) * LANES)
                mutual, own = mutual_scores[i % 2, pair, :, span], self_scores[i % 2, pair, :, span]
                mixed.append(mix_head(2 * pair + j, mutual, own, qv_t, i))
        parts = [
            by_channel([block[:, kind * LANES : (kind + 1) * LANES] for block in mixed])
            for kind in range(2)
        ]
        joined[i] = jnp.concatenate(parts, axis=0).astype(jnp.bfloat16)


def finished(x, joined, w_prj, w_gu, w_dwn):
    mixed = [matmul_tn(block, w_prj[...]) for block in joined]
    middle = x + jnp.concatenate(mixed, axis=0)
    both = matmul(normed(middle), w_gu[...])
    gate, up = both[:, : 2 * LANES], both[:, 2 * LANES :]
    gelu = 0.5 * gate * (1.0 + lax.erf(gate * float(np.sqrt(0.5))))
    hidden = (gelu * up).astype(jnp.bfloat16)
    return middle + matmul(hidden, w_dwn[...])


def to_tokens_kernel(h_ref, x_ref, send_ref, own_ref, raw, wide, tiles, sems):
    h = h_ref[0]
    copies = []
    for k in range(2):
        half = 1 - h if k == 0 else h
        source = x_ref.at[:, :, pl.ds(pl.multiple_of(half * LANES, LANES), LANES)]
        copies.append(pltpu.make_async_copy(source, raw.at[k], sems.at[k]))
        copies[-1].start()
    pad = jnp.zeros((LANES - C, LANES), jnp.float32)
    for k in range(2):
        copies[k].wait()
        wide[k] = raw[k].astype(jnp.float32).reshape(C * WIN, LANES)
        for r in range(WIN):
            block = wide.at[k][pl.ds(r, C, stride=WIN), :]
            block = jnp.concatenate([block, pad], axis=0).T
            tiles[k, :HALF, r] = block.reshape(HALF, WIN, LANES)
    for k, ref in enumerate((send_ref, own_ref)):
        main = tiles[k, :HALF].reshape(HALF * TOK, LANES)
        ref[: HALF * TOK] = main.astype(jnp.bfloat16)
        ref[HALF * TOK :] = tiles[1 - k, 0].reshape(TOK, LANES).astype(jnp.bfloat16)


def grouped(count):
    parts = max(1, count // GROUP)
    cuts = [count * i // parts for i in range(parts + 1)]
    return [range(low, high) for low, high in zip(cuts[:-1], cuts[1:])]


def layer_one_kernel(count, first, last, h_ref, own_ref, oth_ref, *rest):
    h = h_ref[0]
    if not first:
        before, rest = rest[0], rest[1:]
    w_k, w_qv, w_prj, w_gu, w_dwn = rest[:5]
    outs, rest = rest[5:9], rest[9:]
    if not last:
        after, rest = rest[0], rest[1:]
    flat, tiles, *scratch = rest
    mutual_keys, self_keys, qv_t, joined = *scratch[:3], scratch[-1]
    shift = 0 if first else WIN

    def tokens(group):
        parts = []
        for i in group:
            span = slice(i * TOK, (i + 1) * TOK)
            parts += [own_ref[span], oth_ref[span]]
        return jnp.concatenate(parts, axis=0).astype(jnp.float32)

    for group in grouped(count):
        project_windows(tokens(group), w_k, w_qv, mutual_keys, self_keys, qv_t, group[0])
    attend(count, *scratch)
    if not first:
        flat[:, :, :WIN, :] = before[...]
    for group in grouped(count):
        y = finished(tokens(group), [joined[i] for i in group], w_prj, w_gu, w_dwn)
        y = y.reshape(len(group), 2, WIN, WIN, LANES)
        for j, i in enumerate(group):
            for f in range(2):
                flat[1 - h if f else h, :, shift + i * WIN : shift + (i + 1) * WIN, :] = y[j, f]
    width = shift + (count - 1) * WIN
    if not last:
        after[...] = flat[:, :, width : width + WIN, :]
    for f in range(2):
        for r in range(WIN):
            block = flat[f, r, WIN // 2 : WIN // 2 + width, :]
            tiles[f, r // 4, :, r % 4] = block.reshape(width // WIN, WIN, LANES)
        for k in range(2):
            piece = tiles[f, k].reshape(width * 4, LANES)
            outs[2 * f + k][...] = piece.astype(jnp.bfloat16)


def layer_two_kernel(count, h_ref, *rest):
    even = h_ref[0] == 0
    ins, rest = rest[:4], rest[4:]
    w_k, w_qv, w_prj, w_gu, w_dwn = rest[:5]
    outs, scratch = rest[5:9], rest[9:]
    mutual_keys, self_keys, qv_t, joined = *scratch[:3], scratch[-1]
    half_tok = TOK // 2
    spans = [slice(i * half_tok, (i + 1) * half_tok) for i in range(count)]

    def tokens(group):
        parts = [ref[spans[i]] for i in group for ref in ins]
        return jnp.concatenate(parts, axis=0).astype(jnp.float32)

    for group in grouped(count):
        project_windows(tokens(group), w_k, w_qv, mutual_keys, self_keys, qv_t, group[0])
    attend(count, *scratch)
    for group in grouped(count):
        y = finished(tokens(group), [joined[i] for i in group], w_prj, w_gu, w_dwn)
        for k, i in enumerate(group):
            moved, kept = (y[k * LANES + f * TOK : k * LANES + (f + 1) * TOK] for f in range(2))
            pair = (jnp.where(even, moved, kept), jnp.where(even, kept, moved))
            for f in range(2):
                part = pair[f].astype(jnp.bfloat16)
                for j, out in enumerate((outs[f], outs[2 + f])):
                    out[spans[i]] = part[j * half_tok : (j + 1) * half_tok]


def from_tokens_kernel(h_ref, far_up, near_up, far_lo, near_lo, out_ref, rows, wide, ready, sems):
    edge = WIN // 2

    def place(h):
        for lo, pair in enumerate(((far_up, near_up), (far_lo, near_lo))):
            for half in range(2):
                part = pair[int(half == h)][...].astype(jnp.float32)
                part = part.reshape(HALF, 4, WIN, LANES)
                for r in range(4):
                    low = edge + half * LANES
                    rows[4 * lo + r, low : low + LANES] = part[:, r].reshape(LANES, LANES)

    for h in range(2):

        @pl.when(h_ref[0] == h)
        def _():
            place(h)

    copies = []
    for half in range(2):
        for r in range(WIN):
            if half == 0:
                rows[r, :edge] = rows[r, 2 * LANES : 2 * LANES + edge]
            block = rows[r, half * LANES : (half + 1) * LANES].T
            wide.at[half][pl.ds(r, C, stride=WIN), :] = block[:C]
        ready[half] = wide[half].reshape(C, WIN, LANES).astype(jnp.bfloat16)
        target = out_ref.at[:, :, half * LANES : (half + 1) * LANES]
        copies.append(pltpu.make_async_copy(ready.at[half], target, sems.at[half]))
        copies[-1].start()
    for copy in copies:
        copy.wait()


VMEM = pl.BlockSpec(memory_space=pltpu.VMEM)
SMEM = pl.BlockSpec(memory_space=pltpu.SMEM)
COST = pl.CostEstimate(flops=8 * 10**9, bytes_accessed=2**20, transcendentals=2**20)
PARAMS = pltpu.CompilerParams(vmem_limit_bytes=VMEM_LIMIT)


def attention_scratch(count):
    return [
        pltpu.VMEM((count, TOK, 2 * LANES), jnp.bfloat16),
        pltpu.VMEM((count, LANES, LANES), jnp.bfloat16),
        pltpu.VMEM((count, 4 * LANES, LANES), jnp.bfloat16),
        pltpu.VMEM((2, HEADS // 2, TOK, 2 * LANES), jnp.float32),
        pltpu.VMEM((2, HEADS // 2, 2 * TOK, 2 * LANES), jnp.float32),
        pltpu.VMEM((count, 2 * C, LANES), jnp.bfloat16),
    ]


def tokens_shape(rows):
    return pltpu.VMEM((rows, LANES), jnp.bfloat16)


def in_vmem(*arrays):
    return [pltpu.with_memory_space_constraint(array, pltpu.VMEM) for array in arrays]


def to_tokens(h, x):
    return pl.pallas_call(
        to_tokens_kernel,
        out_shape=[tokens_shape((HALF + 1) * TOK)] * 2,
        in_specs=[SMEM, pl.BlockSpec(memory_space=pl.ANY)],
        out_specs=[VMEM] * 2,
        scratch_shapes=[
            pltpu.VMEM((2, C, WIN, LANES), jnp.bfloat16),
            pltpu.VMEM((2, C * WIN, LANES), jnp.float32),
            pltpu.VMEM((2, HALF, WIN, WIN, LANES), jnp.float32),
            pltpu.SemaphoreType.DMA((2,)),
        ],
        compiler_params=PARAMS,
        name="to_tokens",
    )(h, x)


def layer_one(chunk, h, own, oth, before, weights):
    first, last = chunk == 0, chunk == len(WINDOWS) - 1
    count = WINDOWS[chunk][1] - WINDOWS[chunk][0]
    width = SHIFTED[chunk][1] - SHIFTED[chunk][0]
    edge = [] if last else [jax.ShapeDtypeStruct((2, WIN, WIN, LANES), jnp.float32)]
    shapes = [tokens_shape(width * TOK // 2)] * 4 + edge
    args = (h, *in_vmem(own, oth, *before, *weights))
    return pl.pallas_call(
        functools.partial(layer_one_kernel, count, first, last),
        out_shape=shapes,
        in_specs=[SMEM] + [VMEM] * (len(args) - 1),
        out_specs=[VMEM] * len(shapes),
        scratch_shapes=[
            pltpu.VMEM((2, WIN, (width + 1) * WIN, LANES), jnp.float32),
            pltpu.VMEM((2, 2, width, 4, WIN, LANES), jnp.float32),
            *attention_scratch(count),
        ],
        compiler_params=PARAMS,
        cost_estimate=COST,
        name="layer_one",
    )(*args)


def layer_two(chunk, h, pieces, weights):
    count = SHIFTED[chunk][1] - SHIFTED[chunk][0]
    return pl.pallas_call(
        functools.partial(layer_two_kernel, count),
        out_shape=[tokens_shape(count * TOK // 2)] * 4,
        in_specs=[SMEM] + [VMEM] * 9,
        out_specs=[VMEM] * 4,
        scratch_shapes=attention_scratch(count),
        compiler_params=PARAMS,
        cost_estimate=COST,
        name="layer_two",
    )(h, *in_vmem(*pieces, *weights))


def from_tokens(h, pieces):
    return pl.pallas_call(
        from_tokens_kernel,
        out_shape=jax.ShapeDtypeStruct((C, WIN, 2 * LANES), jnp.bfloat16),
        in_specs=[SMEM] + [VMEM] * len(pieces),
        out_specs=pl.BlockSpec(memory_space=pl.ANY),
        scratch_shapes=[
            pltpu.VMEM((WIN, 2 * LANES + WIN, LANES), jnp.float32),
            pltpu.VMEM((2, C * WIN, LANES), jnp.float32),
            pltpu.VMEM((2, C, WIN, LANES), jnp.bfloat16),
            pltpu.SemaphoreType.DMA((2,)),
        ],
        compiler_params=PARAMS,
        name="from_tokens",
    )(h, *in_vmem(*pieces))


def all_rows(part):
    pad = jnp.zeros((LANES - C, part.shape[1]), jnp.float32)
    return jnp.concatenate([part, pad], axis=0).astype(jnp.bfloat16)


def prepare_kernel(w_mut, w_slf, w_prj, w_gte, w_upp, w_dwn, *outs):
    row = lax.broadcasted_iota(jnp.int32, (LANES, 3 * C), 0)
    col = lax.broadcasted_iota(jnp.int32, (LANES, 3 * C), 1)
    picks = []
    for part in range(3):
        hit = (col == row + part * C) & (row < C)
        picks.append(jnp.where(hit, 1.0, 0.0).astype(jnp.bfloat16))
    for layer in range(2):
        w_k, w_qv, w_p, w_gu, w_d = outs[5 * layer : 5 * layer + 5]
        for ref in (w_k, w_qv, w_p, w_gu, w_d):
            ref[...] = jnp.zeros(ref.shape, jnp.bfloat16)
        for i, w in enumerate((w_mut, w_slf)):
            w = w[layer]
            span = slice(i * LANES, (i + 1) * LANES)
            w_k[:, span] = all_rows(matmul_nt(w, picks[1]))
            w_qv[span, :C] = matmul_nt(picks[0], w).astype(jnp.bfloat16)
            span = slice((2 + i) * LANES, (3 + i) * LANES)
            w_qv[span, :C] = matmul_nt(picks[2], w).astype(jnp.bfloat16)
        w_p[:, :C] = w_prj[layer]
        w_gu[:, :FFN] = all_rows(w_gte[layer].astype(jnp.float32))
        w_gu[:, 2 * LANES : 2 * LANES + FFN] = all_rows(w_upp[layer].astype(jnp.float32))
        w_d[:FFN, :C] = w_dwn[layer]


def prepared(*weights):
    shapes = [
        (LANES, 2 * LANES),
        (4 * LANES, LANES),
        (2 * C, LANES),
        (LANES, 4 * LANES),
        (2 * LANES, LANES),
    ] * 2
    return pl.pallas_call(
        prepare_kernel,
        out_shape=[pltpu.VMEM(shape, jnp.bfloat16) for shape in shapes],
        in_specs=[VMEM] * len(weights),
        out_specs=[VMEM] * len(shapes),
        compiler_params=PARAMS,
        name="prepare",
    )(*weights)


def on_device(features, *weights):
    frames, strips = lax.axis_size("frame"), lax.axis_size("strip")

    def send(value, even_step, odd_step, strip_step):
        pairs = []
        for f in range(frames):
            for s in range(strips):
                to = (f + (odd_step if f % 2 else even_step)) % frames
                pairs.append((f * strips + s, to * strips + (s + strip_step) % strips))
        return lax.ppermute(value, ("frame", "strip"), pairs)

    h = (lax.axis_index("frame") % 2).astype(jnp.int32).reshape(1)
    ready = prepared(*weights)
    w_one, w_two = ready[:5], ready[5:]
    parts = to_tokens(h, features[0])
    chunks = range(len(WINDOWS))
    others = [send(parts[k], 1, -1, 0) for k in chunks]
    edge = ()
    pieces = []
    for k in chunks:
        kept_up, kept_lo, moved_up, moved_lo, *edge = layer_one(
            k, h, parts[len(WINDOWS) + k], others[k], edge, w_one
        )
        moved_up = send(moved_up, 2, 2, -1)
        moved_lo = send(moved_lo, 2, 2, 0)
        kept_up = send(kept_up, 0, 0, -1)
        pieces.append((moved_up, moved_lo, kept_up, kept_lo))
    home = []
    for k in chunks:
        far_up, near_up, far_lo, near_lo = layer_two(k, h, pieces[k], w_two)
        far_up = send(far_up, -1, -1, 1)
        near_up = send(near_up, 0, -2, 1)
        far_lo = send(far_lo, -1, -1, 0)
        near_lo = send(near_lo, 0, -2, 0)
        home += [far_up, near_up, far_lo, near_lo]
    return from_tokens(h, home)[None]


def solution(mesh):
    in_specs = (P("frame", None, "strip", None), P(), P(), P(), P(), P(), P())
    out_specs = P("frame", None, "strip", None)
    return jax.shard_map(
        on_device, mesh=mesh, in_specs=in_specs, out_specs=out_specs, check_vma=False
    )
```

```python
import functools

import jax
import jax.numpy as jnp
import numpy as np
from jax import lax
from jax.experimental import pallas as pl
from jax.experimental.pallas import tpu as pltpu
from jax.sharding import PartitionSpec as P

C = 120
HEADS = 6
HEAD = 20
FFN = 240
WIN = 8
LANES = 128
HALF = 16
GROUP = 8
TOK = WIN * WIN
EPS = 1e-05
SHIFTED = ((0, 16),)
WINDOWS = ((0, 17),)
EXP2_SCALE = float(np.log2(np.e) * HEAD**-0.5)
VMEM_LIMIT = 56 * 1024 * 1024


def matmul(a, b):
    return lax.dot_general(a, b, (((1,), (0,)), ((), ())), preferred_element_type=jnp.float32)


def matmul_nt(a, b):
    return lax.dot_general(a, b, (((1,), (1,)), ((), ())), preferred_element_type=jnp.float32)


def matmul_tn(a, b):
    return lax.dot_general(a, b, (((0,), (0,)), ((), ())), preferred_element_type=jnp.float32)


def normed(x):
    lane = lax.broadcasted_iota(jnp.int32, x.shape, 1)
    mean = jnp.sum(x, axis=1, keepdims=True) * (1.0 / C)
    centred = jnp.where(lane < C, x - mean, 0.0)
    spread = jnp.sum(centred * centred, axis=1, keepdims=True) * (1.0 / C)
    return (centred * lax.rsqrt(spread + EPS)).astype(jnp.bfloat16)


def rows_of_head(head):
    low = head * HEAD // 16 * 16
    return low, low + 32


def head_only(q_t, head, lanes=None):
    low, high = rows_of_head(head)
    row = lax.broadcasted_iota(jnp.int32, (high - low, q_t.shape[1]), 0) + low
    keep = (row >= head * HEAD) & (row < head * HEAD + HEAD)
    if lanes is not None:
        lane = lax.broadcasted_iota(jnp.int32, keep.shape, 1)
        keep = keep & ((lane < TOK) if lanes == 0 else (lane >= TOK))
    pieces = [q_t[low:high] * jnp.where(keep, 1.0, 0.0).astype(jnp.bfloat16)]
    if low:
        pieces.insert(0, jnp.zeros((low, q_t.shape[1]), jnp.bfloat16))
    if high < LANES:
        pieces.append(jnp.zeros((LANES - high, q_t.shape[1]), jnp.bfloat16))
    return jnp.concatenate(pieces, axis=0)


def softmax_rows(scores):
    top = jnp.max(scores, axis=0, keepdims=True)
    weights = jnp.exp2((scores - top) * EXP2_SCALE)
    total = jnp.sum(weights, axis=0, keepdims=True)
    return weights * (1.0 / total)


def project_windows(x, w_k, w_qv, mutual_keys, self_keys, qv_t, first):
    normal = normed(x)
    new_keys = matmul(normal, w_k[...]).astype(jnp.bfloat16)
    new_qv = matmul_nt(w_qv[...], normal).astype(jnp.bfloat16)
    for i in range(x.shape[0] // LANES):
        low = i * LANES
        for f in range(2):
            span = slice(f * LANES, (f + 1) * LANES)
            mutual_keys[first + i, :, span] = new_keys[low + f * TOK : low + (f + 1) * TOK, :LANES]
        self_keys[first + i] = new_keys[low : low + LANES, LANES:]
        qv_t[first + i] = new_qv[:, low : low + LANES]


def score_mutual(pair, mutual_keys, qv_t, window):
    heads = (2 * pair, 2 * pair + 1)
    q_t = qv_t[window, :LANES]
    queries = [
        jnp.concatenate([head_only(q_t, head, lanes) for head in heads], axis=1) for lanes in (1, 0)
    ]
    return matmul(mutual_keys[window], jnp.concatenate(queries, axis=0))


def score_self(pair, self_keys, qv_t, window):
    heads = (2 * pair, 2 * pair + 1)
    q_t = qv_t[window, LANES : 2 * LANES]
    queries = jnp.concatenate([head_only(q_t, head) for head in heads], axis=1)
    return matmul(self_keys[window], queries)


def mix_head(head, mutual, own, qv_t, window):
    lane = lax.broadcasted_iota(jnp.int32, (TOK, LANES), 1)
    first = jnp.where(lane < TOK, 1.0, 0.0).astype(jnp.bfloat16)
    second = jnp.where(lane < TOK, 0.0, 1.0).astype(jnp.bfloat16)
    probs = softmax_rows(mutual).astype(jnp.bfloat16)
    probs = jnp.concatenate([probs * second, probs * first], axis=0)
    own = softmax_rows(own).astype(jnp.bfloat16)
    nothing = jnp.zeros((LANES, LANES), jnp.bfloat16)
    probs = jnp.concatenate(
        [jnp.concatenate([probs, nothing], axis=1), jnp.concatenate([nothing, own], axis=1)], axis=0
    )
    low, high = rows_of_head(head)
    values = [qv_t[window, (2 + kind) * LANES + low : (2 + kind) * LANES + high] for kind in range(2)]
    return matmul(jnp.concatenate(values, axis=1), probs)


def by_channel(mixed):
    row = lax.broadcasted_iota(jnp.int32, (8, LANES), 0)
    parts = []
    for head in range(0, HEADS, 2):
        base = head * HEAD
        one, two = mixed[head], mixed[head + 1]
        one_low, two_low = base - rows_of_head(head)[0], base - rows_of_head(head + 1)[0]
        shared = jnp.where(
            row < HEAD - 16, one[one_low + 16 : one_low + 24], two[two_low + 16 : two_low + 24]
        )
        parts += [one[one_low : one_low + 16], shared, two[two_low + 24 : two_low + 40]]
    return jnp.concatenate(parts, axis=0)


def attend(count, mutual_keys, self_keys, qv_t, mutual_scores, self_scores, joined):
    def score(i, pair):
        mutual_scores[i % 2, pair] = score_mutual(pair, mutual_keys, qv_t, i)
        self_scores[i % 2, pair] = score_self(pair, self_keys, qv_t, i)

    for pair in range(HEADS // 2):
        score(0, pair)
    for i in range(count):
        mixed = []
        for pair in range(HEADS // 2):
            if i + 1 < count:
                score(i + 1, pair)
            for j in range(2):
                span = slice(j * LANES, (j + 1) * LANES)
                mutual, own = mutual_scores[i % 2, pair, :, span], self_scores[i % 2, pair, :, span]
                mixed.append(mix_head(2 * pair + j, mutual, own, qv_t, i))
        parts = [
            by_channel([block[:, kind * LANES : (kind + 1) * LANES] for block in mixed])
            for kind in range(2)
        ]
        joined[i] = jnp.concatenate(parts, axis=0).astype(jnp.bfloat16)


def finished(x, joined, w_prj, w_gu, w_dwn):
    mixed = [matmul_tn(block, w_prj[...]) for block in joined]
    middle = x + jnp.concatenate(mixed, axis=0)
    both = matmul(normed(middle), w_gu[...])
    gate, up = both[:, : 2 * LANES], both[:, 2 * LANES :]
    gelu = 0.5 * gate * (1.0 + lax.erf(gate * float(np.sqrt(0.5))))
    hidden = (gelu * up).astype(jnp.bfloat16)
    return middle + matmul(hidden, w_dwn[...])


def to_tokens_kernel(h_ref, x_ref, send_ref, own_ref, raw, wide, tiles, sems):
    h = h_ref[0]
    copies = []
    for k in range(2):
        half = 1 - h if k == 0 else h
        source = x_ref.at[:, :, pl.ds(pl.multiple_of(half * LANES, LANES), LANES)]
        copies.append(pltpu.make_async_copy(source, raw.at[k], sems.at[k]))
        copies[-1].start()
    pad = jnp.zeros((LANES - C, LANES), jnp.float32)
    for k in range(2):
        copies[k].wait()
        wide[k] = raw[k].astype(jnp.float32).reshape(C * WIN, LANES)
        for r in range(WIN):
            block = wide.at[k][pl.ds(r, C, stride=WIN), :]
            block = jnp.concatenate([block, pad], axis=0).T
            tiles[k, :HALF, r] = block.reshape(HALF, WIN, LANES)
    for k, ref in enumerate((send_ref, own_ref)):
        main = tiles[k, :HALF].reshape(HALF * TOK, LANES)
        ref[: HALF * TOK] = main.astype(jnp.bfloat16)
        ref[HALF * TOK :] = tiles[1 - k, 0].reshape(TOK, LANES).astype(jnp.bfloat16)


def grouped(count):
    parts = max(1, count // GROUP)
    cuts = [count * i // parts for i in range(parts + 1)]
    return [range(low, high) for low, high in zip(cuts[:-1], cuts[1:])]


def layer_one_kernel(count, first, last, h_ref, own_ref, oth_ref, *rest):
    h = h_ref[0]
    if not first:
        before, rest = rest[0], rest[1:]
    w_k, w_qv, w_prj, w_gu, w_dwn = rest[:5]
    outs, rest = rest[5:9], rest[9:]
    if not last:
        after, rest = rest[0], rest[1:]
    flat, tiles, *scratch = rest
    mutual_keys, self_keys, qv_t, joined = *scratch[:3], scratch[-1]
    shift = 0 if first else WIN

    def tokens(group):
        parts = []
        for i in group:
            span = slice(i * TOK, (i + 1) * TOK)
            parts += [own_ref[span], oth_ref[span]]
        return jnp.concatenate(parts, axis=0).astype(jnp.float32)

    for group in grouped(count):
        project_windows(tokens(group), w_k, w_qv, mutual_keys, self_keys, qv_t, group[0])
    attend(count, *scratch)
    if not first:
        flat[:, :, :WIN, :] = before[...]
    for group in grouped(count):
        y = finished(tokens(group), [joined[i] for i in group], w_prj, w_gu, w_dwn)
        y = y.reshape(len(group), 2, WIN, WIN, LANES)
        for j, i in enumerate(group):
            for f in range(2):
                flat[1 - h if f else h, :, shift + i * WIN : shift + (i + 1) * WIN, :] = y[j, f]
    width = shift + (count - 1) * WIN
    if not last:
        after[...] = flat[:, :, width : width + WIN, :]
    for f in range(2):
        for r in range(WIN):
            block = flat[f, r, WIN // 2 : WIN // 2 + width, :]
            tiles[f, r // 4, :, r % 4] = block.reshape(width // WIN, WIN, LANES)
        for k in range(2):
            piece = tiles[f, k].reshape(width * 4, LANES)
            outs[2 * f + k][...] = piece.astype(jnp.bfloat16)


def layer_two_kernel(count, h_ref, *rest):
    even = h_ref[0] == 0
    ins, rest = rest[:4], rest[4:]
    w_k, w_qv, w_prj, w_gu, w_dwn = rest[:5]
    outs, scratch = rest[5:9], rest[9:]
    mutual_keys, self_keys, qv_t, joined = *scratch[:3], scratch[-1]
    half_tok = TOK // 2
    spans = [slice(i * half_tok, (i + 1) * half_tok) for i in range(count)]

    def tokens(group):
        parts = [ref[spans[i]] for i in group for ref in ins]
        return jnp.concatenate(parts, axis=0).astype(jnp.float32)

    for group in grouped(count):
        project_windows(tokens(group), w_k, w_qv, mutual_keys, self_keys, qv_t, group[0])
    attend(count, *scratch)
    for group in grouped(count):
        y = finished(tokens(group), [joined[i] for i in group], w_prj, w_gu, w_dwn)
        for k, i in enumerate(group):
            moved, kept = (y[k * LANES + f * TOK : k * LANES + (f + 1) * TOK] for f in range(2))
            pair = (jnp.where(even, moved, kept), jnp.where(even, kept, moved))
            for f in range(2):
                part = pair[f].astype(jnp.bfloat16)
                for j, out in enumerate((outs[f], outs[3 - f])):
                    out[spans[i]] = part[j * half_tok : (j + 1) * half_tok]


def from_tokens_kernel(h_ref, far_up, near_up, near_lo, far_lo, out_ref, rows, wide, ready, sems):
    edge = WIN // 2

    def place(h):
        for lo, pair in enumerate(((far_up, near_up), (far_lo, near_lo))):
            for half in range(2):
                part = pair[int(half == h)][...].astype(jnp.float32)
                part = part.reshape(HALF, 4, WIN, LANES)
                for r in range(4):
                    low = edge + half * LANES
                    rows[4 * lo + r, low : low + LANES] = part[:, r].reshape(LANES, LANES)

    for h in range(2):

        @pl.when(h_ref[0] == h)
        def _():
            place(h)

    copies = []
    for half in range(2):
        for r in range(WIN):
            if half == 0:
                rows[r, :edge] = rows[r, 2 * LANES : 2 * LANES + edge]
            block = rows[r, half * LANES : (half + 1) * LANES].T
            wide.at[half][pl.ds(r, C, stride=WIN), :] = block[:C]
        ready[half] = wide[half].reshape(C, WIN, LANES).astype(jnp.bfloat16)
        target = out_ref.at[:, :, half * LANES : (half + 1) * LANES]
        copies.append(pltpu.make_async_copy(ready.at[half], target, sems.at[half]))
        copies[-1].start()
    for copy in copies:
        copy.wait()


VMEM = pl.BlockSpec(memory_space=pltpu.VMEM)
SMEM = pl.BlockSpec(memory_space=pltpu.SMEM)
COST = pl.CostEstimate(flops=8 * 10**9, bytes_accessed=2**20, transcendentals=2**20)
PARAMS = pltpu.CompilerParams(vmem_limit_bytes=VMEM_LIMIT)


def attention_scratch(count):
    return [
        pltpu.VMEM((count, TOK, 2 * LANES), jnp.bfloat16),
        pltpu.VMEM((count, LANES, LANES), jnp.bfloat16),
        pltpu.VMEM((count, 4 * LANES, LANES), jnp.bfloat16),
        pltpu.VMEM((2, HEADS // 2, TOK, 2 * LANES), jnp.float32),
        pltpu.VMEM((2, HEADS // 2, 2 * TOK, 2 * LANES), jnp.float32),
        pltpu.VMEM((count, 2 * C, LANES), jnp.bfloat16),
    ]


def tokens_shape(rows):
    return pltpu.VMEM((rows, LANES), jnp.bfloat16)


def in_vmem(*arrays):
    return [pltpu.with_memory_space_constraint(array, pltpu.VMEM) for array in arrays]


def to_tokens(h, x):
    return pl.pallas_call(
        to_tokens_kernel,
        out_shape=[tokens_shape((HALF + 1) * TOK)] * 2,
        in_specs=[SMEM, pl.BlockSpec(memory_space=pl.ANY)],
        out_specs=[VMEM] * 2,
        scratch_shapes=[
            pltpu.VMEM((2, C, WIN, LANES), jnp.bfloat16),
            pltpu.VMEM((2, C * WIN, LANES), jnp.float32),
            pltpu.VMEM((2, HALF, WIN, WIN, LANES), jnp.float32),
            pltpu.SemaphoreType.DMA((2,)),
        ],
        compiler_params=PARAMS,
        name="to_tokens",
    )(h, x)


def layer_one(chunk, h, own, oth, before, weights):
    first, last = chunk == 0, chunk == len(WINDOWS) - 1
    count = WINDOWS[chunk][1] - WINDOWS[chunk][0]
    width = SHIFTED[chunk][1] - SHIFTED[chunk][0]
    edge = [] if last else [jax.ShapeDtypeStruct((2, WIN, WIN, LANES), jnp.float32)]
    shapes = [tokens_shape(width * TOK // 2)] * 4 + edge
    args = (h, *in_vmem(own, oth, *before, *weights))
    return pl.pallas_call(
        functools.partial(layer_one_kernel, count, first, last),
        out_shape=shapes,
        in_specs=[SMEM] + [VMEM] * (len(args) - 1),
        out_specs=[VMEM] * len(shapes),
        scratch_shapes=[
            pltpu.VMEM((2, WIN, (width + 1) * WIN, LANES), jnp.float32),
            pltpu.VMEM((2, 2, width, 4, WIN, LANES), jnp.float32),
            *attention_scratch(count),
        ],
        compiler_params=PARAMS,
        cost_estimate=COST,
        name="layer_one",
    )(*args)


def layer_two(chunk, h, pieces, weights):
    count = SHIFTED[chunk][1] - SHIFTED[chunk][0]
    return pl.pallas_call(
        functools.partial(layer_two_kernel, count),
        out_shape=[tokens_shape(count * TOK // 2)] * 4,
        in_specs=[SMEM] + [VMEM] * 9,
        out_specs=[VMEM] * 4,
        scratch_shapes=attention_scratch(count),
        compiler_params=PARAMS,
        cost_estimate=COST,
        name="layer_two",
    )(h, *in_vmem(*pieces, *weights))


def from_tokens(h, pieces):
    return pl.pallas_call(
        from_tokens_kernel,
        out_shape=jax.ShapeDtypeStruct((C, WIN, 2 * LANES), jnp.bfloat16),
        in_specs=[SMEM] + [VMEM] * len(pieces),
        out_specs=pl.BlockSpec(memory_space=pl.ANY),
        scratch_shapes=[
            pltpu.VMEM((WIN, 2 * LANES + WIN, LANES), jnp.float32),
            pltpu.VMEM((2, C * WIN, LANES), jnp.float32),
            pltpu.VMEM((2, C, WIN, LANES), jnp.bfloat16),
            pltpu.SemaphoreType.DMA((2,)),
        ],
        compiler_params=PARAMS,
        name="from_tokens",
    )(h, *in_vmem(*pieces))


def all_rows(part):
    pad = jnp.zeros((LANES - C, part.shape[1]), jnp.float32)
    return jnp.concatenate([part, pad], axis=0).astype(jnp.bfloat16)


def prepare_kernel(w_mut, w_slf, w_prj, w_gte, w_upp, w_dwn, *outs):
    row = lax.broadcasted_iota(jnp.int32, (LANES, 3 * C), 0)
    col = lax.broadcasted_iota(jnp.int32, (LANES, 3 * C), 1)
    picks = []
    for part in range(3):
        hit = (col == row + part * C) & (row < C)
        picks.append(jnp.where(hit, 1.0, 0.0).astype(jnp.bfloat16))
    for layer in range(2):
        w_k, w_qv, w_p, w_gu, w_d = outs[5 * layer : 5 * layer + 5]
        for ref in (w_k, w_qv, w_p, w_gu, w_d):
            ref[...] = jnp.zeros(ref.shape, jnp.bfloat16)
        for i, w in enumerate((w_mut, w_slf)):
            w = w[layer]
            span = slice(i * LANES, (i + 1) * LANES)
            w_k[:, span] = all_rows(matmul_nt(w, picks[1]))
            w_qv[span, :C] = matmul_nt(picks[0], w).astype(jnp.bfloat16)
            span = slice((2 + i) * LANES, (3 + i) * LANES)
            w_qv[span, :C] = matmul_nt(picks[2], w).astype(jnp.bfloat16)
        w_p[:, :C] = w_prj[layer]
        w_gu[:, :FFN] = all_rows(w_gte[layer].astype(jnp.float32))
        w_gu[:, 2 * LANES : 2 * LANES + FFN] = all_rows(w_upp[layer].astype(jnp.float32))
        w_d[:FFN, :C] = w_dwn[layer]


def prepared(*weights):
    shapes = [
        (LANES, 2 * LANES),
        (4 * LANES, LANES),
        (2 * C, LANES),
        (LANES, 4 * LANES),
        (2 * LANES, LANES),
    ] * 2
    return pl.pallas_call(
        prepare_kernel,
        out_shape=[pltpu.VMEM(shape, jnp.bfloat16) for shape in shapes],
        in_specs=[VMEM] * len(weights),
        out_specs=[VMEM] * len(shapes),
        compiler_params=PARAMS,
        name="prepare",
    )(*weights)


def on_device(features, *weights):
    frames, strips = lax.axis_size("frame"), lax.axis_size("strip")

    def send(value, even_step, odd_step, strip_step):
        pairs = []
        for f in range(frames):
            for s in range(strips):
                to = (f + (odd_step if f % 2 else even_step)) % frames
                pairs.append((f * strips + s, to * strips + (s + strip_step) % strips))
        return lax.ppermute(value, ("frame", "strip"), pairs)

    h = (lax.axis_index("frame") % 2).astype(jnp.int32).reshape(1)
    ready = prepared(*weights)
    w_one, w_two = ready[:5], ready[5:]
    parts = to_tokens(h, features[0])
    chunks = range(len(WINDOWS))
    others = [send(parts[k], 1, -1, 0) for k in chunks]
    edge = ()
    pieces = []
    for k in chunks:
        kept_up, kept_lo, moved_up, moved_lo, *edge = layer_one(
            k, h, parts[len(WINDOWS) + k], others[k], edge, w_one
        )
        moved_up = send(moved_up, 2, 2, -1)
        moved_lo = send(moved_lo, 2, 2, 0)
        kept_up = send(kept_up, 0, 0, -1)
        pieces.append((moved_up, moved_lo, kept_up, kept_lo))
    home = []
    for k in chunks:
        far_up, near_up, near_lo, far_lo = layer_two(k, h, pieces[k], w_two)
        far_up = send(far_up, -1, -1, 1)
        near_up = send(near_up, 0, -2, 1)
        near_lo = send(near_lo, 0, -2, 0)
        far_lo = send(far_lo, -1, -1, 0)
        home += [far_up, near_up, near_lo, far_lo]
    return from_tokens(h, home)[None]


def solution(mesh):
    in_specs = (P("frame", None, "strip", None), P(), P(), P(), P(), P(), P())
    out_specs = P("frame", None, "strip", None)
    return jax.shard_map(
        on_device, mesh=mesh, in_specs=in_specs, out_specs=out_specs, check_vma=False
    )
```
